256 devices in a mesh: tm: 8 (over y, core), rows: 8 (over z), dp: 4 (over x).
Axes of the slice: x: 4, y: 4, z: 8, core: 2. Of those that a mesh axis runs over, the one named last changes fastest.
Arguments:
- video: bfloat16 [4, 128, 32, 32, 128], P('dp', 'tm', 'rows'), may hold values from -6 to 6
- cotangent: bfloat16 [4, 128, 32, 32, 128], P('dp', 'tm', 'rows'), may hold values from -6 to 6
- in_kernel: bfloat16 [3, 3, 128, 128], replicated, may hold values from -0.03125 to 0.03125
- out_kernel: bfloat16 [3, 3, 128, 128], replicated, may hold values from -0.1875 to 0.1875
- skip_gain: float32 [128], replicated, may hold values from 0.5 to 1.5
- log_decay: float32 [128, 128], P('tm'), may hold values from -3 to 0, as said below
Outputs:
- layer_out: bfloat16 [4, 128, 32, 32, 128], P('dp', 'tm', 'rows')
- video_grad: bfloat16 [4, 128, 32, 32, 128], P('dp', 'tm', 'rows')
- in_kernel_grad: float32 [3, 3, 128, 128], replicated
- out_kernel_grad: float32 [3, 3, 128, 128], replicated
- skip_gain_grad: float32 [128], replicated
- decay_grad: float32 [128, 128], P('tm')
The draws below stay inside these ranges and needn't reach their ends.
Inputs may be any that keep to these rules, and one draw needn't show every extreme that they name: log_decay is negative.
All inputs are finite; a program needn't handle non-finite values.
Results may differ from the reference program's by a relative error of at most 0.0085.
Values may be sent and summed in bfloat16 or wider, within the bound.
A program may use at most 64 MiB of HBM per device.

```python
import math
import jax
import jax.numpy as jnp
from jax import lax

U = 128
P_SIZE = 128
WIDTH = 32
FRAMES = 128
HEIGHT = 32
SEQS = 4


def draw_log_decay(key, part):
    keys = jax.random.split(jax.random.fold_in(key, 11), 6)
    share = 0.5
    slow = jax.random.uniform(keys[0], (P_SIZE,)) < share
    fast_rate = jnp.exp(jax.random.uniform(keys[1], (P_SIZE,), minval=math.log(0.045), maxval=math.log(0.08)))
    slow_rate = jnp.exp(jax.random.uniform(keys[2], (P_SIZE,), minval=math.log(0.1), maxval=math.log(1.0))) / FRAMES
    rate = jnp.where(slow, slow_rate, fast_rate)
    jitter = jnp.exp(jax.random.uniform(keys[3], (FRAMES, P_SIZE), minval=-0.5, maxval=0.5))
    base = -rate[None, :] * jitter
    spots = jax.random.randint(keys[4], (3,), 0, FRAMES)
    depth = jnp.log(jax.random.uniform(keys[5], (3, P_SIZE), minval=0.6, maxval=0.85))
    hits = (jnp.arange(FRAMES)[:, None] == spots[None, :]).astype(jnp.float32)
    return base + jnp.dot(hits, depth, precision=lax.Precision.HIGHEST)


def levels(key, extent, shards, low, largest):
    level, own = 1.0, jax.random.fold_in(key, 6)
    for dim, parts in shards:
        draws = jnp.exp(jax.random.uniform(jax.random.fold_in(own, dim), (parts,), jnp.float32, low / len(shards), largest / len(shards)))
        level = level * jnp.repeat(draws, extent[dim] // parts).reshape([-1 if axis == dim else 1 for axis in range(len(extent))])
    return level


def gaussian(own_key, extent, scale, most, cuts=(), held_as=jnp.bfloat16):
    drawn = scale * jax.random.normal(own_key, extent, jnp.float32)
    if cuts:
        drawn = drawn * levels(own_key, extent, cuts, -0.22, 0.18)
    return jnp.clip(drawn, -most, most).astype(held_as)


def setup_inputs(seed: int = 0) -> dict:
    key_of = jax.random.split(jax.random.key(seed), 7)
    return {
        "video": gaussian(key_of[0], (SEQS, FRAMES, HEIGHT, WIDTH, U), 1.0, 6.0, ((0, 4), (1, 8), (2, 8))),
        "cotangent": gaussian(key_of[1], (SEQS, FRAMES, HEIGHT, WIDTH, U), 1.0, 6.0, ((0, 4), (1, 8), (2, 8))),
        "in_kernel": gaussian(key_of[2], (3, 3, U, P_SIZE), (256 * U) ** -0.5, 0.03125),
        "out_kernel": gaussian(key_of[3], (3, 3, P_SIZE, U), (9 * P_SIZE) ** -0.5, 0.1875),
        "skip_gain": jnp.clip(jax.random.uniform(key_of[4], (U,), jnp.float32, 0.5, 1.5), 0.5, 1.5),
        "log_decay": draw_log_decay(jax.random.fold_in(key_of[6], 71), 0),
    }


def pad_both(field):
    return jnp.pad(field, ((0, 0), (0, 0), (1, 1), (1, 1), (0, 0)))

def forward_conv(padded, kernel):
    seqs, frames, rows_two, cols_two, chans = padded.shape
    rows, cols = (rows_two - 2, cols_two - 2)
    total = None
    for i in range(3):
        for j in range(3):
            piece = padded[:, :, i:i + rows, j:j + cols, :].reshape(-1, chans)
            term = jnp.dot(piece, kernel[i, j], preferred_element_type=jnp.float32)
            total = term if total is None else total + term
    return total.reshape(seqs, frames, rows, cols, kernel.shape[3])

def adjoint_conv(padded, kernel):
    seqs, frames, rows_two, cols_two, chans = padded.shape
    rows, cols = (rows_two - 2, cols_two - 2)
    total = None
    for i in range(3):
        for j in range(3):
            piece = padded[:, :, 2 - i:2 - i + rows, 2 - j:2 - j + cols, :].reshape(-1, chans)
            term = lax.dot_general(piece, kernel[i, j], (((1,), (1,)), ((), ())), preferred_element_type=jnp.float32)
            total = term if total is None else total + term
    return total.reshape(seqs, frames, rows, cols, kernel.shape[2])

def kernel_grad(padded, grad):
    seqs, frames, rows_two, cols_two, chans = padded.shape
    rows, cols = (rows_two - 2, cols_two - 2)
    flat_grad = grad.reshape(-1, grad.shape[-1])
    outer_list = []
    for i in range(3):
        inner_list = []
        for j in range(3):
            piece = padded[:, :, i:i + rows, j:j + cols, :].reshape(-1, chans)
            inner_list.append(lax.dot_general(piece, flat_grad, (((0,), (0,)), ((), ())), preferred_element_type=jnp.float32))
        outer_list.append(jnp.stack(inner_list))
    return jnp.stack(outer_list)

def reference(video, cotangent, in_kernel, out_kernel, skip_gain, log_decay):
    lam = jnp.exp(log_decay)

    def one_sequence(pair):
        frames_in, cot = pair
        padded_x = pad_both(frames_in)
        drive = forward_conv(padded_x, in_kernel)

        def forward_step(state, inputs):
            lam_t, drive_t = inputs
            state = lam_t * state + drive_t
            return (state, state)
        start = jnp.zeros(drive.shape[:1] + drive.shape[2:], jnp.float32)
        _, states = lax.scan(forward_step, start, (lam, jnp.moveaxis(drive, 1, 0)))
        states = jnp.moveaxis(states, 0, 1)
        states_bf = states.astype(jnp.bfloat16)
        padded_s = pad_both(states_bf)
        pre = forward_conv(padded_s, out_kernel) + skip_gain * frames_in.astype(jnp.float32)
        activated, pullback = jax.vjp(jax.nn.gelu, pre)
        grad_pre = pullback(cot.astype(jnp.float32))[0]
        grad_bf = grad_pre.astype(jnp.bfloat16)
        out_grad = kernel_grad(padded_s, grad_bf)
        gain_grad = lax.optimization_barrier(jnp.sum(grad_pre * frames_in.astype(jnp.float32), axis=(0, 1, 2, 3)))
        state_grad = adjoint_conv(pad_both(grad_bf), out_kernel)

        def back_step(carry, inputs):
            lam_t, grad_t = inputs
            adj = grad_t + carry
            return (lam_t * adj, adj)
        _, adjoint = lax.scan(back_step, start, (lam, jnp.moveaxis(state_grad, 1, 0)), reverse=True)
        adjoint = jnp.moveaxis(adjoint, 0, 1)
        previous = jnp.concatenate([jnp.zeros_like(states[:, :1]), states[:, :-1]], axis=1)
        decay_part = lax.optimization_barrier(jnp.sum(adjoint * lam[None, :, None, None, :] * previous, axis=(0, 2, 3)))
        adjoint_bf = adjoint.astype(jnp.bfloat16)
        in_grad = kernel_grad(padded_x, adjoint_bf)
        back = adjoint_conv(pad_both(adjoint_bf), in_kernel) + skip_gain * grad_pre
        return (activated.astype(jnp.bfloat16)[0], back.astype(jnp.bfloat16)[0], in_grad, out_grad, gain_grad, decay_part)
    outs = lax.map(one_sequence, (video[:, None], cotangent[:, None]))
    weight_scale = 1.0 / math.sqrt(SEQS * FRAMES * HEIGHT * WIDTH)
    decay_scale = 1.0 / math.sqrt(SEQS * HEIGHT * WIDTH)
    return (outs[0], outs[1], lax.optimization_barrier(jnp.sum(outs[2], axis=0)) * weight_scale, lax.optimization_barrier(jnp.sum(outs[3], axis=0)) * weight_scale, lax.optimization_barrier(jnp.sum(outs[4], axis=0)) * weight_scale, lax.optimization_barrier(jnp.sum(outs[5], axis=0)) * decay_scale)
```

```python
import functools
import math

import jax
import jax.numpy as jnp
from jax import lax
from jax.experimental import pallas as pl
from jax.experimental.pallas import tpu as pltpu
from jax.sharding import PartitionSpec as P

MESH = pl.DeviceIdType.MESH
F32, BF16 = jnp.float32, jnp.bfloat16
C = 128
TAPS = 3
LANES = TAPS * C
GELU_A = math.sqrt(2.0 / math.pi)
GELU_B = 0.044715


def at_next(field):
    cols = field.shape[1]
    col = lax.broadcasted_iota(jnp.int32, field.shape, 1)
    return jnp.where(col == cols - 1, 0.0, pltpu.roll(field, cols - 1, 1))


def at_previous(field):
    col = lax.broadcasted_iota(jnp.int32, field.shape, 1)
    return jnp.where(col == 0, 0.0, pltpu.roll(field, 1, 1))


def taps(w_ref, i):
    return jnp.concatenate([w_ref[i, j] for j in range(TAPS)], axis=-1)


def forward_rows(pad, w_ref, frames, r0, nr):
    n, cols = frames.size * nr, pad.shape[2]
    lhs = jnp.concatenate(
        [pad[frames, r0 + i : r0 + i + nr].reshape(n * cols, C) for i in range(TAPS)], axis=-1
    )
    rhs = jnp.concatenate([taps(w_ref, i) for i in range(TAPS)], axis=0)
    y = jnp.dot(lhs, rhs, preferred_element_type=F32).reshape(n, cols, LANES)
    return at_previous(y[..., :C]) + y[..., C : 2 * C] + at_next(y[..., 2 * C :])


def adjoint_rows(wide, w_ref, frames, r0, nr):
    n, cols = frames.size * nr, wide.shape[2]
    lhs = jnp.concatenate(
        [wide[frames, r0 + 2 - i : r0 + 2 - i + nr].reshape(n * cols, LANES) for i in range(TAPS)],
        axis=-1,
    )
    rhs = jnp.concatenate([taps(w_ref, i) for i in range(TAPS)], axis=-1)
    y = lax.dot_general(lhs, rhs, (((1,), (1,)), ((), ())), preferred_element_type=F32)
    return y.reshape(n, cols, C)


def widen(wide, frames, r0, nr, value):
    shape = (frames.size, nr) + value.shape[1:]
    for j, part in enumerate((at_next(value), value, at_previous(value))):
        wide[frames, r0 : r0 + nr, :, j * C : (j + 1) * C] = part.astype(BF16).reshape(shape)


def body(
    nt, nz, nx, total_cells, total_positions,
    x_hbm, ct_hbm, w_in, w_out, gain, ld,
    lo_hbm, vg_hbm, ig_out, og_out, gg_out, dg_out,
    xpad, spad, g3, a3, st, ag, gp, ct, lo, vg,
    es, eg, ea, hs, hg, ha, ces, cer,
    lam, ecum, erev, dsend, dall, csend, crecv, cin, bin_, gsum, dpart,
    acc, snd1, rcv1, snd2, rcv2, x3, f4, g5,
    loc, hal_s, hal_r, ce_s, ce_r, dec_s, dec_r, car_s, car_r,
    p1_s, p1_r, p2_s, p2_r, p3_s, p3_r, p4_s, p4_r, p5_s, p5_r,
):
    T, R, W, _ = x_hbm.shape
    CH = LANES // nt
    SR = TAPS * CH + 16
    BR = snd2.shape[1] // (-(-SR // rcv2.shape[2]))
    NB = snd2.shape[1] // BR
    half = T // 2
    all_frames = pl.ds(0, T)
    me, mez, mex = lax.axis_index("tm"), lax.axis_index("rows"), lax.axis_index("dp")

    def to_tm(src, dst, s, r, k):
        return pltpu.make_async_remote_copy(src, dst, s, r, device_id={"tm": k}, device_id_type=MESH)

    def to_rows(src, dst, s, r, k):
        return pltpu.make_async_remote_copy(src, dst, s, r, device_id={"rows": k}, device_id_type=MESH)

    def to_dp(src, dst, s, r, k):
        return pltpu.make_async_remote_copy(src, dst, s, r, device_id={"dp": k}, device_id_type=MESH)

    def others(mine, count, act):
        def step(o, _):
            act(lax.rem(mine + o, count))
            return 0

        lax.fori_loop(1, count, step, 0)

    def each(low, high, act):
        def step(k, _):
            act(k)
            return 0

        lax.fori_loop(low, high, step, 0)

    barrier = pltpu.get_barrier_semaphore()
    for axis, mine, count in (("tm", me, nt), ("rows", mez, nz), ("dp", mex, nx)):
        others(
            mine, count,
            lambda k, axis=axis: pl.semaphore_signal(
                barrier, inc=1, device_id={axis: k}, device_id_type=MESH
            ),
        )
    load_x = pltpu.make_async_copy(x_hbm, xpad.at[:, 1 : R + 1], loc.at[0])
    load_x.start()
    load_ct = pltpu.make_async_copy(ct_hbm, ct, loc.at[1])
    load_ct.start()

    run = jnp.zeros((1, C), F32)
    for t in range(T):
        run = run + ld[t : t + 1]
        ecum[t : t + 1] = run
    erev[...] = jnp.exp(run - ecum[...])
    ecum[...] = jnp.exp(ecum[...])
    lam[...] = jnp.exp(ld[...])
    dsend[...] = jnp.broadcast_to(jnp.exp(run), dsend.shape)
    gsum[...] = jnp.zeros_like(gsum)

    @pl.when(mez == 0)
    def _():
        for ref in (xpad, spad, g3, a3):
            ref[:, 0] = jnp.zeros((T, W, ref.shape[3]), BF16)

    @pl.when(mez == nz - 1)
    def _():
        for ref in (xpad, spad, g3, a3):
            ref[:, R + 1] = jnp.zeros((T, W, ref.shape[3]), BF16)

    pl.semaphore_wait(barrier, nt + nz + nx - 3)

    def edge(stage, way, src, dst, sems=None):
        s, r = sems or (hal_s, hal_r)
        return to_rows(
            src, dst, s.at[stage, way], r.at[stage, way],
            jnp.maximum(mez - 1, 0) if way == 0 else jnp.minimum(mez + 1, nz - 1),
        )

    def edges(stage, srcs, dsts, what, sems=None):
        for way in range(2):
            from_there = (mez < nz - 1) if way == 0 else (mez > 0)
            to_there = (mez > 0) if way == 0 else (mez < nz - 1)

            @pl.when(from_there if what == "recv" else to_there)
            def _(way=way):
                copy = edge(stage, way, srcs[way], dsts[way], sems)
                {"start": copy.start, "recv": copy.wait_recv, "send": copy.wait_send}[what]()

    def received(act):
        @pl.when(mez < nz - 1)
        def _():
            act(0, R + 1)

        @pl.when(mez > 0)
        def _():
            act(1, 0)

    edge_sets = [
        (0, (x_hbm.at[:, 0], x_hbm.at[:, R - 1]), (xpad.at[:, R + 1], xpad.at[:, 0]), None),
        (1, (es.at[0], es.at[1]), (hs.at[0], hs.at[1]), None),
        (2, (eg.at[0], eg.at[1]), (hg.at[0], hg.at[1]), None),
        (3, (ea.at[0], ea.at[1]), (ha.at[0], ha.at[1]), None),
        (0, (ces.at[0, 0], ces.at[0, 1]), (cer.at[0, 0], cer.at[0, 1]), (ce_s, ce_r)),
        (1, (ces.at[1, 0], ces.at[1, 1]), (cer.at[1, 0], cer.at[1, 1]), (ce_s, ce_r)),
    ]

    def do_edges(n, what):
        stage, srcs, dsts, sems = edge_sets[n]
        edges(stage, srcs, dsts, what, sems)

    do_edges(0, "start")

    def decay_copy(k):
        return to_tm(dsend, dall.at[me], dec_s.at[k], dec_r.at[me], k)

    others(me, nt, lambda k: decay_copy(k).start())

    def send1(q, k):
        return to_tm(snd1.at[q, k], rcv1.at[q, me], p1_s.at[q, k], p1_r.at[q, me], k)

    def send2(q, k):
        return to_rows(
            snd2.at[q, pl.ds(k * BR, BR)], rcv2.at[q, mez], p2_s.at[q, k], p2_r.at[q, mez], k
        )

    def send3(q, k):
        return to_dp(x3.at[q, mex], x3.at[q, mex], p3_s.at[q, k], p3_r.at[q, mex], k)

    def send4(q, k):
        here = f4.at[q, pl.ds(mez * BR, BR)]
        return to_rows(here, here, p4_s.at[q, k], p4_r.at[q, mez], k)

    def send5(q, k):
        return to_tm(f4.at[q], g5.at[q, me], p5_s.at[q, k], p5_r.at[q, me], k)

    def got(ref, q, k, r, copy):
        return copy(ref.at[q, k], ref.at[q, k], r.at[q, k], r.at[q, k], 0).wait_recv()

    def not_me(k, act):
        @pl.when(k != mez)
        def _():
            act(k)

    def sum1(q):
        for k in range(nt):
            snd1[q, k] = acc[q, k * CH : (k + 1) * CH].astype(BF16)
        others(me, nt, lambda k: send1(q, k).start())

    def sum2(q, extra):
        def step(o, total):
            k = lax.rem(me + o, nt)
            got(rcv1, q, k, p1_r, to_tm)
            return total + rcv1[q, k].astype(F32)

        total = lax.fori_loop(1, nt, step, acc[q, pl.ds(pl.multiple_of(me * CH, 16), CH)])
        for j in range(TAPS):
            snd2[q, j * CH : (j + 1) * CH] = total[:, j * C : (j + 1) * C].astype(BF16)
        snd2[q, TAPS * CH : SR] = extra.astype(BF16)
        if NB * BR > SR:
            snd2[q, SR:] = jnp.zeros((NB * BR - SR, C), BF16)
        each(0, NB, lambda k: not_me(k, lambda k: send2(q, k).start()))

    def sum3(q):
        @pl.when(mez < NB)
        def _():
            def step(o, total):
                k = lax.rem(mez + o, nz)
                got(rcv2, q, k, p2_r, to_rows)
                return total + rcv2[q, k].astype(F32)

            mine = snd2[q, pl.ds(pl.multiple_of(mez * BR, 16), BR)].astype(F32)
            x3[q, mex] = lax.fori_loop(1, nz, step, mine)
            others(mex, nx, lambda k: send3(q, k).start())

    def sum4(q):
        @pl.when(mez < NB)
        def _():
            others(mex, nx, lambda k: got(x3, q, k, p3_r, to_dp))
            total = x3[q, 0]
            for k in range(1, nx):
                total = total + x3[q, k]
            f4[q, pl.ds(pl.multiple_of(mez * BR, 16), BR)] = total.astype(BF16)
            others(mez, nz, lambda k: send4(q, k).start())

    def sum5(q):
        def wait(k):
            there = f4.at[q, pl.ds(k * BR, BR)]
            to_rows(there, there, p4_s.at[q, k], p4_r.at[q, k], 0).wait_recv()

        each(0, NB, lambda k: not_me(k, wait))
        g5[q, me] = f4[q]
        others(me, nt, lambda k: send5(q, k).start())

    weight_scale = 1.0 / math.sqrt(total_positions)

    def sum6(q, out):
        others(me, nt, lambda k: got(g5, q, k, p5_r, to_tm))
        for k in range(nt):
            for u in range(0, CH, 16):
                i, c = divmod(k * CH + u, C)
                for j in range(TAPS):
                    piece = g5[q, k, j * CH + u : j * CH + u + 16]
                    out[i, j, c : c + 16] = piece.astype(F32) * weight_scale

    def sums_sent(q):
        others(me, nt, lambda k: send1(q, k).wait_send())
        each(0, NB, lambda k: not_me(k, lambda k: send2(q, k).wait_send()))

        @pl.when(mez < NB)
        def _():
            others(mex, nx, lambda k: send3(q, k).wait_send())
            others(mez, nz, lambda k: send4(q, k).wait_send())

        others(me, nt, lambda k: send5(q, k).wait_send())

    def inner(act):
        each(0, 2, lambda f: act(pl.ds(f * half, half), 1, R - 2))

    def outer(act):
        each(0, 1, lambda f: act(all_frames, 0, 1))
        each(0, 1, lambda f: act(all_frames, R - 1, 1))

    def drive(frames, r0, nr):
        y = forward_rows(xpad, w_in, frames, r0, nr)
        ag[frames, r0 : r0 + nr] = y.reshape(frames.size, nr, W, C)

    load_x.wait()
    inner(drive)
    do_edges(0, "recv")
    outer(drive)

    def forward_step(t, state):
        state = lam[pl.ds(t, 1)].reshape(1, 1, C) * state + ag[t]
        st[t + 1] = state
        es[0, t] = state[0].astype(BF16)
        es[1, t] = state[R - 1].astype(BF16)
        return state

    last = lax.fori_loop(0, T, forward_step, jnp.zeros((R, W, C), F32))
    csend[0] = last.astype(BF16)

    def carry_copy(way, k):
        return to_tm(csend.at[way], crecv.at[way, me], car_s.at[way, k], car_r.at[way, me], k)

    each(me + 1, nt, lambda k: carry_copy(0, k).start())
    do_edges(1, "start")

    others(me, nt, lambda k: to_tm(dsend, dall.at[k], dec_s.at[k], dec_r.at[k], 0).wait_recv())

    def join_earlier(k, state):
        got(crecv, 0, k, car_r, to_tm)
        return dall[k, 0:1].reshape(1, 1, C) * state + crecv[0, k].astype(F32)

    carry = lax.fori_loop(0, me, join_earlier, jnp.zeros((R, W, C), F32))
    ces[0, 0] = carry[0].astype(BF16)
    ces[0, 1] = carry[R - 1].astype(BF16)
    do_edges(4, "start")
    st[0] = carry
    cin[...] = carry

    def finish_state(t):
        state = st[t + 1] + ecum[pl.ds(t, 1)].reshape(1, 1, C) * cin[...]
        st[t + 1] = state
        spad[t, 1 : R + 1] = state.astype(BF16)

    each(0, T, finish_state)

    load_ct.wait()

    def output(frames, r0, nr):
        n = frames.size * nr
        x = xpad[frames, r0 + 1 : r0 + 1 + nr].reshape(n, W, C).astype(F32)
        pre = forward_rows(spad, w_out, frames, r0, nr) + gain[...].reshape(1, 1, C) * x
        square = pre * pre
        bend = jnp.tanh(GELU_A * (pre + GELU_B * (square * pre)))
        rise = 0.5 * (1.0 + bend)
        lo[frames, r0 : r0 + nr] = (pre * rise).astype(BF16).reshape(frames.size, nr, W, C)
        slope = rise + 0.5 * pre * (1.0 - bend * bend) * (GELU_A * (1.0 + 3.0 * GELU_B * square))
        grad = ct[frames, r0 : r0 + nr].reshape(n, W, C).astype(F32) * slope
        gp[frames, r0 : r0 + nr] = grad.reshape(frames.size, nr, W, C)
        gsum[...] += jnp.sum((grad * x).reshape(n * W // 8, 8, C), axis=0)
        widen(g3, frames, r0 + 1, nr, grad)

    inner(output)
    do_edges(1, "recv")
    do_edges(4, "recv")

    def state_edge(way, row):
        def step(t):
            value = hs[way, t].astype(F32) + ecum[pl.ds(t, 1)] * cer[0, way].astype(F32)
            spad[t, row] = value.astype(BF16)

        each(0, T, step)

    received(state_edge)
    outer(output)
    eg[0] = gp[:, 0].astype(BF16)
    eg[1] = gp[:, R - 1].astype(BF16)
    do_edges(2, "start")
    store_lo = pltpu.make_async_copy(lo, lo_hbm, loc.at[2])
    store_lo.start()

    def kernel_grad(q, pad, wide):
        acc[q] = jnp.zeros((LANES, LANES), F32)
        part = T // 4

        def step(f):
            frames = pl.ds(f * part, part)
            n = part * R * W
            lhs = jnp.concatenate(
                [pad[frames, i : i + R].reshape(n, C) for i in range(TAPS)], axis=-1
            )
            rhs = wide[frames, 1 : R + 1].reshape(n, LANES)
            acc[q] += lax.dot_general(
                lhs, rhs, (((0,), (0,)), ((), ())), preferred_element_type=F32
            )

        each(0, 4, step)

    kernel_grad(0, spad, g3)
    sum1(0)

    def state_grad(frames, r0, nr):
        ag[frames, r0 : r0 + nr] = adjoint_rows(g3, w_out, frames, r0, nr).reshape(
            frames.size, nr, W, C
        )

    inner(state_grad)
    do_edges(2, "recv")
    received(lambda way, row: widen(g3, all_frames, row, 1, hg[way].astype(F32)))
    outer(state_grad)

    def backward_step(o, carried):
        t = T - 1 - o
        adjoint = ag[t] + carried
        ag[t] = adjoint
        ea[0, t] = adjoint[0].astype(BF16)
        ea[1, t] = adjoint[R - 1].astype(BF16)
        return lam[pl.ds(t, 1)].reshape(1, 1, C) * adjoint

    first = lax.fori_loop(0, T, backward_step, jnp.zeros((R, W, C), F32))
    csend[1] = first.astype(BF16)
    each(0, me, lambda k: carry_copy(1, k).start())
    do_edges(3, "start")

    zeros8 = jnp.zeros((8, C), F32)
    sum2(0, jnp.concatenate([gsum[...], zeros8], axis=0))

    def join_later(o, adjoint):
        k = nt - 1 - o
        got(crecv, 1, k, car_r, to_tm)
        return dall[k, 0:1].reshape(1, 1, C) * adjoint + crecv[1, k].astype(F32)

    back = lax.fori_loop(0, nt - 1 - me, join_later, jnp.zeros((R, W, C), F32))
    ces[1, 0] = back[0].astype(BF16)
    ces[1, 1] = back[R - 1].astype(BF16)
    do_edges(5, "start")
    bin_[...] = back

    def finish_adjoint(t):
        adjoint = ag[t] + erev[pl.ds(t, 1)].reshape(1, 1, C) * bin_[...]
        product = jnp.sum((adjoint * st[t]).reshape(R * W, C), axis=0, keepdims=True)
        dpart[pl.ds(t, 1)] = product * lam[pl.ds(t, 1)]
        for j, part in enumerate((at_next(adjoint), adjoint, at_previous(adjoint))):
            a3[t, 1 : R + 1, :, j * C : (j + 1) * C] = part.astype(BF16)

    each(0, T, finish_adjoint)
    kernel_grad(1, xpad, a3)
    sum1(1)
    sum3(0)

    def video_grad(frames, r0, nr):
        skip = gain[...].reshape(1, 1, C) * gp[frames, r0 : r0 + nr].reshape(-1, W, C)
        value = adjoint_rows(a3, w_in, frames, r0, nr) + skip
        vg[frames, r0 : r0 + nr] = value.astype(BF16).reshape(frames.size, nr, W, C)

    inner(video_grad)
    sum2(1, dpart[...])
    sum4(0)
    do_edges(3, "recv")
    do_edges(5, "recv")

    def adjoint_edge(way, row):
        def step(t):
            value = ha[way, t].astype(F32) + erev[pl.ds(t, 1)] * cer[1, way].astype(F32)
            widen(a3, pl.ds(t, 1), row, 1, value.reshape(1, W, C))

        each(0, T, step)

    received(adjoint_edge)
    sum3(1)
    sum5(0)
    outer(video_grad)
    store_vg = pltpu.make_async_copy(vg, vg_hbm, loc.at[3])
    store_vg.start()
    sum4(1)
    sum6(0, og_out)
    sum5(1)
    dg_out[...] = f4[1, TAPS * CH : SR].astype(F32) * (1.0 / math.sqrt(total_cells))
    total_gain = jnp.zeros((8, C), F32)
    for k in range(nt):
        total_gain = total_gain + g5[0, k, TAPS * CH : SR].astype(F32)[0:8]
    gg_out[...] = jnp.sum(total_gain, axis=0, keepdims=True) * weight_scale
    sum6(1, ig_out)

    for n in range(6):
        do_edges(n, "send")
    others(me, nt, lambda k: decay_copy(k).wait_send())
    each(me + 1, nt, lambda k: carry_copy(0, k).wait_send())
    each(0, me, lambda k: carry_copy(1, k).wait_send())
    for q in range(2):
        sums_sent(q)
    store_lo.wait()
    store_vg.wait()


def on_device(nt, nz, nx, video, cotangent, in_kernel, out_kernel, skip_gain, log_decay):
    seqs, T, R, W, _ = video.shape
    field = (T, R, W, C)
    CH = LANES // nt
    SR = TAPS * CH + 16
    BR = -(-SR // (nz * 16)) * 16
    NB = -(-SR // BR)
    dma = pltpu.SemaphoreType.DMA
    vmem = pltpu.VMEM
    scratch = [
        vmem((T, R + 2, W, C), BF16),
        vmem((T, R + 2, W, C), BF16),
        vmem((T, R + 2, W, LANES), BF16),
        vmem((T, R + 2, W, LANES), BF16),
        vmem((T + 1, R, W, C), F32),
        vmem(field, F32),
        vmem(field, F32),
        vmem(field, BF16),
        vmem(field, BF16),
        vmem(field, BF16),
        *[vmem((2, T, W, C), BF16)] * 6,
        *[vmem((2, 2, W, C), BF16)] * 2,
        *[vmem((T, C), F32)] * 3,
        vmem((8, C), F32),
        vmem((nt, 8, C), F32),
        vmem((2, R, W, C), BF16),
        vmem((2, nt, R, W, C), BF16),
        vmem((R, W, C), F32),
        vmem((R, W, C), F32),
        vmem((8, C), F32),
        vmem((T, C), F32),
        vmem((2, LANES, LANES), F32),
        vmem((2, nt, CH, LANES), BF16),
        vmem((2, nt, CH, LANES), BF16),
        vmem((2, NB * BR, C), BF16),
        vmem((2, nz, BR, C), BF16),
        vmem((2, nx, BR, C), F32),
        vmem((2, NB * BR, C), BF16),
        vmem((2, nt, NB * BR, C), BF16),
        dma((4,)),
        dma((4, 2)),
        dma((4, 2)),
        dma((2, 2)),
        dma((2, 2)),
        dma((nt,)),
        dma((nt,)),
        *[dma((2, nt))] * 4,
        *[dma((2, nz))] * 2,
        *[dma((2, nx))] * 2,
        *[dma((2, nz))] * 2,
        *[dma((2, nt))] * 2,
    ]
    any_, whole = pl.BlockSpec(memory_space=pl.ANY), pl.BlockSpec(memory_space=pltpu.VMEM)
    cells = seqs * nx * R * nz * W
    outs = pl.pallas_call(
        functools.partial(body, nt, nz, nx, cells, cells * T * nt),
        out_shape=(
            jax.ShapeDtypeStruct(field, BF16),
            jax.ShapeDtypeStruct(field, BF16),
            jax.ShapeDtypeStruct((TAPS, TAPS, C, C), F32),
            jax.ShapeDtypeStruct((TAPS, TAPS, C, C), F32),
            jax.ShapeDtypeStruct((1, C), F32),
            jax.ShapeDtypeStruct((T, C), F32),
        ),
        in_specs=[any_, any_, whole, whole, whole, whole],
        out_specs=(any_, any_, whole, whole, whole, whole),
        scratch_shapes=scratch,
        compiler_params=pltpu.CompilerParams(
            collective_id=0, has_side_effects=True, vmem_limit_bytes=48 * 2**20
        ),
    )(
        video.reshape(field),
        cotangent.reshape(field),
        in_kernel,
        out_kernel,
        skip_gain.reshape(1, C),
        log_decay,
    )
    layer_out, video_grad, in_grad, out_grad, gain_grad, decay_grad = outs
    return (
        layer_out.reshape(video.shape),
        video_grad.reshape(video.shape),
        in_grad,
        out_grad,
        gain_grad.reshape(C),
        decay_grad,
    )


def solution(mesh):
    field = P("dp", "tm", "rows", None, None)
    nt, nz, nx = mesh.shape["tm"], mesh.shape["rows"], mesh.shape["dp"]
    return jax.shard_map(
        functools.partial(on_device, nt, nz, nx),
        mesh=mesh,
        in_specs=(field, field, P(), P(), P(), P("tm", None)),
        out_specs=(field, field, P(), P(), P(), P("tm", None)),
        check_vma=False,
    )
```

```python
import functools
import math

import jax
import jax.numpy as jnp
from jax import lax
from jax.experimental import pallas as pl
from jax.experimental.pallas import tpu as pltpu
from jax.sharding import PartitionSpec as P

MESH = pl.DeviceIdType.MESH
F32, BF16 = jnp.float32, jnp.bfloat16
C = 128
TAPS = 3
LANES = TAPS * C
GELU_A = math.sqrt(2.0 / math.pi)
GELU_B = 0.044715
VMEM_BYTES = 59 * 10**6


def at_next(field):
    cols = field.shape[1]
    col = lax.broadcasted_iota(jnp.int32, field.shape, 1)
    return jnp.where(col == cols - 1, 0.0, pltpu.roll(field, cols - 1, 1))


def at_previous(field):
    col = lax.broadcasted_iota(jnp.int32, field.shape, 1)
    return jnp.where(col == 0, 0.0, pltpu.roll(field, 1, 1))


def taps(w_ref, i):
    return jnp.concatenate([w_ref[i, j] for j in range(TAPS)], axis=-1)


def forward_rows(pad, w_ref, frames, r0, nr):
    n, cols = frames.size * nr, pad.shape[2]
    lhs = jnp.concatenate(
        [pad[frames, r0 + i : r0 + i + nr].reshape(n * cols, C) for i in range(TAPS)], axis=-1
    )
    rhs = jnp.concatenate([taps(w_ref, i) for i in range(TAPS)], axis=0)
    y = jnp.dot(lhs, rhs, preferred_element_type=F32).reshape(n, cols, LANES)
    return at_previous(y[..., :C]) + y[..., C : 2 * C] + at_next(y[..., 2 * C :])


def adjoint_rows(wide, w_ref, frames, r0, nr):
    n, cols = frames.size * nr, wide.shape[2]
    lhs = jnp.concatenate(
        [wide[frames, r0 + 2 - i : r0 + 2 - i + nr].reshape(n * cols, LANES) for i in range(TAPS)],
        axis=-1,
    )
    rhs = jnp.concatenate([taps(w_ref, i) for i in range(TAPS)], axis=-1)
    y = lax.dot_general(lhs, rhs, (((1,), (1,)), ((), ())), preferred_element_type=F32)
    return y.reshape(n, cols, C)


def widen(wide, frames, r0, nr, value):
    shape = (frames.size, nr) + value.shape[1:]
    for j, part in enumerate((at_next(value), value, at_previous(value))):
        wide[frames, r0 : r0 + nr, :, j * C : (j + 1) * C] = part.astype(BF16).reshape(shape)


def body(
    nt, nz, nx, total_cells, total_positions,
    x_hbm, ct_hbm, w_in_hbm, w_out_hbm, gain_hbm, ld_hbm,
    lo_hbm, vg_hbm, g5_hbm, gg_hbm, dg_hbm,
    xpad, spad, g3, a3, st, ag, gp, ct, w_in, w_out, gain, ld, lo, vg, gg_out, dg_out,
    es, eg, ea, hs, hg, ha, ces, cer,
    lam, ecum, erev, dsend, dall, csend, crecv, cin, bin_, gsum, dpart,
    acc, snd1, rcv1, snd2, rcv2, x3, f4, g5,
    loc, out_s, hal_s, hal_r, ce_s, ce_r, dec_s, dec_r, car_s, car_r,
    p1_s, p1_r, p2_s, p2_r, p3_s, p3_r, p4_s, p4_r, p5_s, p5_r,
):
    T, R, W, _ = x_hbm.shape
    CH = LANES // nt
    SR = TAPS * CH + 16
    BR = snd2.shape[1] // (-(-SR // rcv2.shape[2]))
    NB = snd2.shape[1] // BR
    half = T // 2
    all_frames = pl.ds(0, T)
    me, mez, mex = lax.axis_index("tm"), lax.axis_index("rows"), lax.axis_index("dp")

    def to_tm(src, dst, s, r, k):
        return pltpu.make_async_remote_copy(src, dst, s, r, device_id={"tm": k}, device_id_type=MESH)

    def to_rows(src, dst, s, r, k):
        return pltpu.make_async_remote_copy(src, dst, s, r, device_id={"rows": k}, device_id_type=MESH)

    def to_dp(src, dst, s, r, k):
        return pltpu.make_async_remote_copy(src, dst, s, r, device_id={"dp": k}, device_id_type=MESH)

    def others(mine, count, act):
        def step(o, _):
            act(lax.rem(mine + o, count))
            return 0

        lax.fori_loop(1, count, step, 0)

    def each(low, high, act):
        def step(k, _):
            act(k)
            return 0

        lax.fori_loop(low, high, step, 0)

    barrier = pltpu.get_barrier_semaphore()
    for axis, mine, count in (("tm", me, nt), ("rows", mez, nz), ("dp", mex, nx)):
        others(
            mine, count,
            lambda k, axis=axis: pl.semaphore_signal(
                barrier, inc=1, device_id={axis: k}, device_id_type=MESH
            ),
        )
    loads = [
        pltpu.make_async_copy(src, dst, loc.at[n])
        for n, (src, dst) in enumerate(
            (
                (ld_hbm, ld),
                (x_hbm, xpad.at[:, 1 : R + 1]),
                (w_in_hbm, w_in),
                (ct_hbm, ct),
                (w_out_hbm, w_out),
                (gain_hbm, gain),
            )
        )
    ]
    for load in loads:
        load.start()
    loads[0].wait()

    run = jnp.zeros((1, C), F32)
    for t in range(T):
        run = run + ld[t : t + 1]
        ecum[t : t + 1] = run
    erev[...] = jnp.exp(run - ecum[...])
    ecum[...] = jnp.exp(ecum[...])
    lam[...] = jnp.exp(ld[...])
    dsend[...] = jnp.broadcast_to(jnp.exp(run), dsend.shape)
    gsum[...] = jnp.zeros_like(gsum)

    @pl.when(mez == 0)
    def _():
        for ref in (xpad, spad, g3, a3):
            ref[:, 0] = jnp.zeros((T, W, ref.shape[3]), BF16)

    @pl.when(mez == nz - 1)
    def _():
        for ref in (xpad, spad, g3, a3):
            ref[:, R + 1] = jnp.zeros((T, W, ref.shape[3]), BF16)

    pl.semaphore_wait(barrier, nt + nz + nx - 3)

    def edge(stage, way, src, dst, sems=None):
        s, r = sems or (hal_s, hal_r)
        return to_rows(
            src, dst, s.at[stage, way], r.at[stage, way],
            jnp.maximum(mez - 1, 0) if way == 0 else jnp.minimum(mez + 1, nz - 1),
        )

    def edges(stage, srcs, dsts, what, sems=None):
        for way in range(2):
            from_there = (mez < nz - 1) if way == 0 else (mez > 0)
            to_there = (mez > 0) if way == 0 else (mez < nz - 1)

            @pl.when(from_there if what == "recv" else to_there)
            def _(way=way):
                copy = edge(stage, way, srcs[way], dsts[way], sems)
                {"start": copy.start, "recv": copy.wait_recv, "send": copy.wait_send}[what]()

    def received(act):
        @pl.when(mez < nz - 1)
        def _():
            act(0, R + 1)

        @pl.when(mez > 0)
        def _():
            act(1, 0)

    edge_sets = [
        (0, (x_hbm.at[:, 0], x_hbm.at[:, R - 1]), (xpad.at[:, R + 1], xpad.at[:, 0]), None),
        (1, (es.at[0], es.at[1]), (hs.at[0], hs.at[1]), None),
        (2, (eg.at[0], eg.at[1]), (hg.at[0], hg.at[1]), None),
        (3, (ea.at[0], ea.at[1]), (ha.at[0], ha.at[1]), None),
        (0, (ces.at[0, 0], ces.at[0, 1]), (cer.at[0, 0], cer.at[0, 1]), (ce_s, ce_r)),
        (1, (ces.at[1, 0], ces.at[1, 1]), (cer.at[1, 0], cer.at[1, 1]), (ce_s, ce_r)),
    ]

    def do_edges(n, what):
        stage, srcs, dsts, sems = edge_sets[n]
        edges(stage, srcs, dsts, what, sems)

    do_edges(0, "start")

    def decay_copy(k):
        return to_tm(dsend, dall.at[me], dec_s.at[k], dec_r.at[me], k)

    others(me, nt, lambda k: decay_copy(k).start())

    def store(n, src, dst):
        copy = pltpu.make_async_copy(src, dst, out_s.at[n])
        copy.start()
        return copy

    def send1(q, k):
        return to_tm(snd1.at[q, k], rcv1.at[q, me], p1_s.at[q, k], p1_r.at[q, me], k)

    def send2(q, k):
        return to_rows(
            snd2.at[q, pl.ds(k * BR, BR)], rcv2.at[q, mez], p2_s.at[q, k], p2_r.at[q, mez], k
        )

    def send3(q, k):
        return to_dp(x3.at[q, mex], x3.at[q, mex], p3_s.at[q, k], p3_r.at[q, mex], k)

    def send4(q, k):
        here = f4.at[q, pl.ds(mez * BR, BR)]
        return to_rows(here, here, p4_s.at[q, k], p4_r.at[q, mez], k)

    def send5(q, k):
        return to_tm(f4.at[q], g5.at[q, me], p5_s.at[q, k], p5_r.at[q, me], k)

    def got(ref, q, k, r, copy):
        return copy(ref.at[q, k], ref.at[q, k], r.at[q, k], r.at[q, k], 0).wait_recv()

    def not_me(k, act):
        @pl.when(k != mez)
        def _():
            act(k)

    def sum1(q):
        for k in range(nt):
            snd1[q, k] = acc[q, k * CH : (k + 1) * CH].astype(BF16)
        others(me, nt, lambda k: send1(q, k).start())

    def sum2(q, extra):
        def step(o, total):
            k = lax.rem(me + o, nt)
            got(rcv1, q, k, p1_r, to_tm)
            return total + rcv1[q, k].astype(F32)

        total = lax.fori_loop(1, nt, step, acc[q, pl.ds(pl.multiple_of(me * CH, 16), CH)])
        for j in range(TAPS):
            snd2[q, j * CH : (j + 1) * CH] = total[:, j * C : (j + 1) * C].astype(BF16)
        snd2[q, TAPS * CH : SR] = extra.astype(BF16)
        if NB * BR > SR:
            snd2[q, SR:] = jnp.zeros((NB * BR - SR, C), BF16)
        each(0, NB, lambda k: not_me(k, lambda k: send2(q, k).start()))

    def sum3(q):
        @pl.when(mez < NB)
        def _():
            def step(o, total):
                k = lax.rem(mez + o, nz)
                got(rcv2, q, k, p2_r, to_rows)
                return total + rcv2[q, k].astype(F32)

            mine = snd2[q, pl.ds(pl.multiple_of(mez * BR, 16), BR)].astype(F32)
            x3[q, mex] = lax.fori_loop(1, nz, step, mine)
            others(mex, nx, lambda k: send3(q, k).start())

    def sum4(q):
        @pl.when(mez < NB)
        def _():
            others(mex, nx, lambda k: got(x3, q, k, p3_r, to_dp))
            total = x3[q, 0]
            for k in range(1, nx):
                total = total + x3[q, k]
            f4[q, pl.ds(pl.multiple_of(mez * BR, 16), BR)] = total.astype(BF16)
            others(mez, nz, lambda k: send4(q, k).start())

    def sum5(q):
        def wait(k):
            there = f4.at[q, pl.ds(k * BR, BR)]
            to_rows(there, there, p4_s.at[q, k], p4_r.at[q, k], 0).wait_recv()

        each(0, NB, lambda k: not_me(k, wait))
        g5[q, me] = f4[q]
        others(me, nt, lambda k: send5(q, k).start())

    def sum6(q):
        others(me, nt, lambda k: got(g5, q, k, p5_r, to_tm))

    def sums_sent(q):
        others(me, nt, lambda k: send1(q, k).wait_send())
        each(0, NB, lambda k: not_me(k, lambda k: send2(q, k).wait_send()))

        @pl.when(mez < NB)
        def _():
            others(mex, nx, lambda k: send3(q, k).wait_send())
            others(mez, nz, lambda k: send4(q, k).wait_send())

        others(me, nt, lambda k: send5(q, k).wait_send())

    def inner(act):
        each(0, 2, lambda f: act(pl.ds(f * half, half), 1, R - 2))

    def outer(act):
        each(0, 1, lambda f: act(all_frames, 0, 1))
        each(0, 1, lambda f: act(all_frames, R - 1, 1))

    def drive(frames, r0, nr):
        y = forward_rows(xpad, w_in, frames, r0, nr)
        ag[frames, r0 : r0 + nr] = y.reshape(frames.size, nr, W, C)

    loads[1].wait()
    loads[2].wait()
    inner(drive)
    do_edges(0, "recv")
    outer(drive)

    def forward_step(t, state):
        state = lam[pl.ds(t, 1)].reshape(1, 1, C) * state + ag[t]
        st[t + 1] = state
        es[0, t] = state[0].astype(BF16)
        es[1, t] = state[R - 1].astype(BF16)
        return state

    last = lax.fori_loop(0, T, forward_step, jnp.zeros((R, W, C), F32))
    csend[0] = last.astype(BF16)

    def carry_copy(way, k):
        return to_tm(csend.at[way], crecv.at[way, me], car_s.at[way, k], car_r.at[way, me], k)

    each(me + 1, nt, lambda k: carry_copy(0, k).start())
    do_edges(1, "start")

    others(me, nt, lambda k: to_tm(dsend, dall.at[k], dec_s.at[k], dec_r.at[k], 0).wait_recv())

    def join_earlier(k, state):
        got(crecv, 0, k, car_r, to_tm)
        return dall[k, 0:1].reshape(1, 1, C) * state + crecv[0, k].astype(F32)

    carry = lax.fori_loop(0, me, join_earlier, jnp.zeros((R, W, C), F32))
    ces[0, 0] = carry[0].astype(BF16)
    ces[0, 1] = carry[R - 1].astype(BF16)
    do_edges(4, "start")
    st[0] = carry
    cin[...] = carry

    def finish_state(t):
        state = st[t + 1] + ecum[pl.ds(t, 1)].reshape(1, 1, C) * cin[...]
        st[t + 1] = state
        spad[t, 1 : R + 1] = state.astype(BF16)

    each(0, T, finish_state)

    for load in loads[3:]:
        load.wait()

    def output(frames, r0, nr):
        n = frames.size * nr
        x = xpad[frames, r0 + 1 : r0 + 1 + nr].reshape(n, W, C).astype(F32)
        pre = forward_rows(spad, w_out, frames, r0, nr) + gain[...].reshape(1, 1, C) * x
        square = pre * pre
        bend = jnp.tanh(GELU_A * (pre + GELU_B * (square * pre)))
        rise = 0.5 * (1.0 + bend)
        lo[frames, r0 : r0 + nr] = (pre * rise).astype(BF16).reshape(frames.size, nr, W, C)
        slope = rise + 0.5 * pre * (1.0 - bend * bend) * (GELU_A * (1.0 + 3.0 * GELU_B * square))
        grad = ct[frames, r0 : r0 + nr].reshape(n, W, C).astype(F32) * slope
        gp[frames, r0 : r0 + nr] = grad.reshape(frames.size, nr, W, C)
        gsum[...] += jnp.sum((grad * x).reshape(n * W // 8, 8, C), axis=0)
        widen(g3, frames, r0 + 1, nr, grad)

    inner(output)
    do_edges(1, "recv")
    do_edges(4, "recv")

    def state_edge(way, row):
        def step(t):
            value = hs[way, t].astype(F32) + ecum[pl.ds(t, 1)] * cer[0, way].astype(F32)
            spad[t, row] = value.astype(BF16)

        each(0, T, step)

    received(state_edge)
    outer(output)
    eg[0] = gp[:, 0].astype(BF16)
    eg[1] = gp[:, R - 1].astype(BF16)
    do_edges(2, "start")

    def kernel_grad(q, pad, wide):
        acc[q] = jnp.zeros((LANES, LANES), F32)
        part = T // 4

        def step(f):
            frames = pl.ds(f * part, part)
            n = part * R * W
            lhs = jnp.concatenate(
                [pad[frames, i : i + R].reshape(n, C) for i in range(TAPS)], axis=-1
            )
            rhs = wide[frames, 1 : R + 1].reshape(n, LANES)
            acc[q] += lax.dot_general(
                lhs, rhs, (((0,), (0,)), ((), ())), preferred_element_type=F32
            )

        each(0, 4, step)

    store_lo = store(0, lo, lo_hbm)
    kernel_grad(0, spad, g3)
    sum1(0)

    def state_grad(frames, r0, nr):
        ag[frames, r0 : r0 + nr] = adjoint_rows(g3, w_out, frames, r0, nr).reshape(
            frames.size, nr, W, C
        )

    inner(state_grad)
    do_edges(2, "recv")
    received(lambda way, row: widen(g3, all_frames, row, 1, hg[way].astype(F32)))
    outer(state_grad)

    def backward_step(o, carried):
        t = T - 1 - o
        adjoint = ag[t] + carried
        ag[t] = adjoint
        ea[0, t] = adjoint[0].astype(BF16)
        ea[1, t] = adjoint[R - 1].astype(BF16)
        return lam[pl.ds(t, 1)].reshape(1, 1, C) * adjoint

    first = lax.fori_loop(0, T, backward_step, jnp.zeros((R, W, C), F32))
    csend[1] = first.astype(BF16)
    each(0, me, lambda k: carry_copy(1, k).start())
    do_edges(3, "start")

    zeros8 = jnp.zeros((8, C), F32)
    sum2(0, jnp.concatenate([gsum[...], zeros8], axis=0))

    def join_later(o, adjoint):
        k = nt - 1 - o
        got(crecv, 1, k, car_r, to_tm)
        return dall[k, 0:1].reshape(1, 1, C) * adjoint + crecv[1, k].astype(F32)

    back = lax.fori_loop(0, nt - 1 - me, join_later, jnp.zeros((R, W, C), F32))
    ces[1, 0] = back[0].astype(BF16)
    ces[1, 1] = back[R - 1].astype(BF16)
    do_edges(5, "start")
    bin_[...] = back

    def finish_adjoint(t):
        adjoint = ag[t] + erev[pl.ds(t, 1)].reshape(1, 1, C) * bin_[...]
        product = jnp.sum((adjoint * st[t]).reshape(R * W, C), axis=0, keepdims=True)
        dpart[pl.ds(t, 1)] = product * lam[pl.ds(t, 1)]
        for j, part in enumerate((at_next(adjoint), adjoint, at_previous(adjoint))):
            a3[t, 1 : R + 1, :, j * C : (j + 1) * C] = part.astype(BF16)

    each(0, T, finish_adjoint)
    kernel_grad(1, xpad, a3)
    sum1(1)
    sum3(0)

    def video_grad(frames, r0, nr):
        skip = gain[...].reshape(1, 1, C) * gp[frames, r0 : r0 + nr].reshape(-1, W, C)
        value = adjoint_rows(a3, w_in, frames, r0, nr) + skip
        vg[frames, r0 : r0 + nr] = value.astype(BF16).reshape(frames.size, nr, W, C)

    inner(video_grad)
    sum2(1, dpart[...])
    sum4(0)
    do_edges(3, "recv")
    do_edges(5, "recv")

    def adjoint_edge(way, row):
        def step(t):
            value = ha[way, t].astype(F32) + erev[pl.ds(t, 1)] * cer[1, way].astype(F32)
            widen(a3, pl.ds(t, 1), row, 1, value.reshape(1, W, C))

        each(0, T, step)

    received(adjoint_edge)
    sum3(1)
    sum5(0)
    outer(video_grad)
    store_vg = store(1, vg, vg_hbm)
    sum4(1)
    sum6(0)
    store_og = store(2, g5.at[0], g5_hbm.at[0])
    sum5(1)
    dg_out[...] = f4[1, TAPS * CH : SR].astype(F32) * (1.0 / math.sqrt(total_cells))
    total_gain = jnp.zeros((8, C), F32)
    for k in range(nt):
        total_gain = total_gain + g5[0, k, TAPS * CH : SR].astype(F32)[0:8]
    gg_out[...] = jnp.sum(total_gain, axis=0, keepdims=True) * (1.0 / math.sqrt(total_positions))
    store_small = (store(4, gg_out, gg_hbm), store(5, dg_out, dg_hbm))
    sum6(1)
    store_ig = store(3, g5.at[1], g5_hbm.at[1])

    for n in range(6):
        do_edges(n, "send")
    others(me, nt, lambda k: decay_copy(k).wait_send())
    each(me + 1, nt, lambda k: carry_copy(0, k).wait_send())
    each(0, me, lambda k: carry_copy(1, k).wait_send())
    for q in range(2):
        sums_sent(q)
    for copy in (store_lo, store_vg, store_og, store_ig, *store_small):
        copy.wait()


def finish(
    scale, lo, vg, g5_hbm, gg, dg, lo_hbm, vg_hbm, ig_hbm, og_hbm, gg_hbm, dg_hbm, g5, grads, sems
):
    nt = g5.shape[1]
    CH = LANES // nt

    def store(n, src, dst):
        copy = pltpu.make_async_copy(src, dst, sems.at[n])
        copy.start()
        return copy

    load = store(6, g5_hbm, g5)
    copies = [store(0, vg, vg_hbm), store(1, lo, lo_hbm)]
    copies += [store(2, gg, gg_hbm), store(3, dg, dg_hbm)]
    load.wait()
    for q, out in ((0, og_hbm), (1, ig_hbm)):
        for k in range(nt):
            for u in range(0, CH, 16):
                i, c = divmod(k * CH + u, C)
                for j in range(TAPS):
                    piece = g5[q, k, j * CH + u : j * CH + u + 16]
                    grads[q, i, j, c : c + 16] = piece.astype(F32) * scale
        copies.append(store(4 + q, grads.at[q], out))
    for copy in copies:
        copy.wait()


def on_device(nt, nz, nx, video, cotangent, in_kernel, out_kernel, skip_gain, log_decay):
    seqs, T, R, W, _ = video.shape
    field = (T, R, W, C)
    CH = LANES // nt
    SR = TAPS * CH + 16
    BR = -(-SR // (nz * 16)) * 16
    NB = -(-SR // BR)
    dma = pltpu.SemaphoreType.DMA
    vmem = pltpu.VMEM
    scratch = [
        vmem((T, R + 2, W, C), BF16),
        vmem((T, R + 2, W, C), BF16),
        vmem((T, R + 2, W, LANES), BF16),
        vmem((T, R + 2, W, LANES), BF16),
        vmem((T + 1, R, W, C), F32),
        vmem(field, F32),
        vmem(field, F32),
        vmem(field, BF16),
        vmem((TAPS, TAPS, C, C), BF16),
        vmem((TAPS, TAPS, C, C), BF16),
        vmem((1, C), F32),
        vmem((T, C), F32),
        vmem(field, BF16),
        vmem(field, BF16),
        vmem((1, C), F32),
        vmem((T, C), F32),
        *[vmem((2, T, W, C), BF16)] * 6,
        *[vmem((2, 2, W, C), BF16)] * 2,
        *[vmem((T, C), F32)] * 3,
        vmem((8, C), F32),
        vmem((nt, 8, C), F32),
        vmem((2, R, W, C), BF16),
        vmem((2, nt, R, W, C), BF16),
        vmem((R, W, C), F32),
        vmem((R, W, C), F32),
        vmem((8, C), F32),
        vmem((T, C), F32),
        vmem((2, LANES, LANES), F32),
        vmem((2, nt, CH, LANES), BF16),
        vmem((2, nt, CH, LANES), BF16),
        vmem((2, NB * BR, C), BF16),
        vmem((2, nz, BR, C), BF16),
        vmem((2, nx, BR, C), F32),
        vmem((2, NB * BR, C), BF16),
        vmem((2, nt, NB * BR, C), BF16),
        dma((6,)),
        dma((6,)),
        dma((4, 2)),
        dma((4, 2)),
        dma((2, 2)),
        dma((2, 2)),
        dma((nt,)),
        dma((nt,)),
        *[dma((2, nt))] * 4,
        *[dma((2, nz))] * 2,
        *[dma((2, nx))] * 2,
        *[dma((2, nz))] * 2,
        *[dma((2, nt))] * 2,
    ]
    hbm = pl.BlockSpec(memory_space=pltpu.HBM)
    cells = seqs * nx * R * nz * W
    parts = pl.pallas_call(
        functools.partial(body, nt, nz, nx, cells, cells * T * nt),
        out_shape=(
            jax.ShapeDtypeStruct(field, BF16),
            jax.ShapeDtypeStruct(field, BF16),
            jax.ShapeDtypeStruct((2, nt, NB * BR, C), BF16),
            jax.ShapeDtypeStruct((1, C), F32),
            jax.ShapeDtypeStruct((T, C), F32),
        ),
        in_specs=[hbm] * 6,
        out_specs=(hbm,) * 5,
        scratch_shapes=scratch,
        compiler_params=pltpu.CompilerParams(
            collective_id=0, has_side_effects=True, vmem_limit_bytes=VMEM_BYTES
        ),
    )(
        video.reshape(field),
        cotangent.reshape(field),
        in_kernel,
        out_kernel,
        skip_gain.reshape(1, C),
        log_decay,
    )
    outs = pl.pallas_call(
        functools.partial(finish, 1.0 / math.sqrt(cells * T * nt)),
        out_shape=(
            jax.ShapeDtypeStruct(field, BF16),
            jax.ShapeDtypeStruct(field, BF16),
            jax.ShapeDtypeStruct((TAPS, TAPS, C, C), F32),
            jax.ShapeDtypeStruct((TAPS, TAPS, C, C), F32),
            jax.ShapeDtypeStruct((1, C), F32),
            jax.ShapeDtypeStruct((T, C), F32),
        ),
        in_specs=[hbm] * 5,
        out_specs=(hbm,) * 6,
        scratch_shapes=[
            vmem((2, nt, NB * BR, C), BF16),
            vmem((2, TAPS, TAPS, C, C), F32),
            dma((7,)),
        ],
        compiler_params=pltpu.CompilerParams(vmem_limit_bytes=VMEM_BYTES),
    )(*parts)
    layer_out, video_grad, in_grad, out_grad, gain_grad, decay_grad = outs
    return (
        layer_out.reshape(video.shape),
        video_grad.reshape(video.shape),
        in_grad,
        out_grad,
        gain_grad.reshape(C),
        decay_grad,
    )


def solution(mesh):
    field = P("dp", "tm", "rows", None, None)
    nt, nz, nx = mesh.shape["tm"], mesh.shape["rows"], mesh.shape["dp"]
    return jax.shard_map(
        functools.partial(on_device, nt, nz, nx),
        mesh=mesh,
        in_specs=(field, field, P(), P(), P(), P("tm", None)),
        out_specs=(field, field, P(), P(), P(), P("tm", None)),
        check_vma=False,
    )
```

```python
import functools
import math

import jax
import jax.numpy as jnp
from jax import lax
from jax.experimental import pallas as pl
from jax.experimental.pallas import tpu as pltpu
from jax.sharding import PartitionSpec as P

MESH = pl.DeviceIdType.MESH
F32, BF16 = jnp.float32, jnp.bfloat16
C = 128
TAPS = 3
LANES = TAPS * C
GELU_A = math.sqrt(2.0 / math.pi)
GELU_B = 0.044715


def at_next(field):
    cols = field.shape[1]
    col = lax.broadcasted_iota(jnp.int32, field.shape, 1)
    return jnp.where(col == cols - 1, 0.0, pltpu.roll(field, cols - 1, 1))


def at_previous(field):
    col = lax.broadcasted_iota(jnp.int32, field.shape, 1)
    return jnp.where(col == 0, 0.0, pltpu.roll(field, 1, 1))


def taps(w_ref, i):
    return jnp.concatenate([w_ref[i, j] for j in range(TAPS)], axis=-1)


def forward_rows(pad, w_ref, frames, r0, nr):
    n, cols = frames.size * nr, pad.shape[2]
    lhs = jnp.concatenate(
        [pad[frames, r0 + i : r0 + i + nr].reshape(n * cols, C) for i in range(TAPS)], axis=-1
    )
    rhs = jnp.concatenate([taps(w_ref, i) for i in range(TAPS)], axis=0)
    y = jnp.dot(lhs, rhs, preferred_element_type=F32).reshape(n, cols, LANES)
    return at_previous(y[..., :C]) + y[..., C : 2 * C] + at_next(y[..., 2 * C :])


def adjoint_rows(wide, w_ref, frames, r0, nr):
    n, cols = frames.size * nr, wide.shape[2]
    lhs = jnp.concatenate(
        [wide[frames, r0 + 2 - i : r0 + 2 - i + nr].reshape(n * cols, LANES) for i in range(TAPS)],
        axis=-1,
    )
    rhs = jnp.concatenate([taps(w_ref, i) for i in range(TAPS)], axis=-1)
    y = lax.dot_general(lhs, rhs, (((1,), (1,)), ((), ())), preferred_element_type=F32)
    return y.reshape(n, cols, C)


def widen(wide, frames, r0, nr, value):
    shape = (frames.size, nr) + value.shape[1:]
    for j, part in enumerate((at_next(value), value, at_previous(value))):
        wide[frames, r0 : r0 + nr, :, j * C : (j + 1) * C] = part.astype(BF16).reshape(shape)


def body(
    nt, nz, nx, total_cells, total_positions,
    x_hbm, ct_hbm, w_in_hbm, w_out_hbm, gain_hbm, ld_hbm,
    lo, vg, g5, gg_out, dg_out,
    xpad, spad, g3, a3, st, ag, gp, ct, w_in, w_out, gain, ld,
    es, eg, ea, hs, hg, ha, ces, cer,
    lam, ecum, erev, dsend, dall, csend, crecv, cin, bin_, gsum, dpart,
    acc, snd1, rcv1, snd2, rcv2, x3, f4,
    loc, hal_s, hal_r, ce_s, ce_r, dec_s, dec_r, car_s, car_r,
    p1_s, p1_r, p2_s, p2_r, p3_s, p3_r, p4_s, p4_r, p5_s, p5_r,
):
    T, R, W, _ = x_hbm.shape
    CH = LANES // nt
    SR = TAPS * CH + 16
    BR = snd2.shape[1] // (-(-SR // rcv2.shape[2]))
    NB = snd2.shape[1] // BR
    half = T // 2
    all_frames = pl.ds(0, T)
    me, mez, mex = lax.axis_index("tm"), lax.axis_index("rows"), lax.axis_index("dp")

    def to_tm(src, dst, s, r, k):
        return pltpu.make_async_remote_copy(src, dst, s, r, device_id={"tm": k}, device_id_type=MESH)

    def to_rows(src, dst, s, r, k):
        return pltpu.make_async_remote_copy(src, dst, s, r, device_id={"rows": k}, device_id_type=MESH)

    def to_dp(src, dst, s, r, k):
        return pltpu.make_async_remote_copy(src, dst, s, r, device_id={"dp": k}, device_id_type=MESH)

    def others(mine, count, act):
        def step(o, _):
            act(lax.rem(mine + o, count))
            return 0

        lax.fori_loop(1, count, step, 0)

    def each(low, high, act):
        def step(k, _):
            act(k)
            return 0

        lax.fori_loop(low, high, step, 0)

    barrier = pltpu.get_barrier_semaphore()
    for axis, mine, count in (("tm", me, nt), ("rows", mez, nz), ("dp", mex, nx)):
        others(
            mine, count,
            lambda k, axis=axis: pl.semaphore_signal(
                barrier, inc=1, device_id={axis: k}, device_id_type=MESH
            ),
        )
    loads = [
        pltpu.make_async_copy(src, dst, loc.at[n])
        for n, (src, dst) in enumerate(
            (
                (ld_hbm, ld),
                (x_hbm, xpad.at[:, 1 : R + 1]),
                (w_in_hbm, w_in),
                (ct_hbm, ct),
                (w_out_hbm, w_out),
                (gain_hbm, gain),
            )
        )
    ]
    for load in loads:
        load.start()
    loads[0].wait()

    run = jnp.zeros((1, C), F32)
    for t in range(T):
        run = run + ld[t : t + 1]
        ecum[t : t + 1] = run
    erev[...] = jnp.exp(run - ecum[...])
    ecum[...] = jnp.exp(ecum[...])
    lam[...] = jnp.exp(ld[...])
    dsend[...] = jnp.broadcast_to(jnp.exp(run), dsend.shape)
    gsum[...] = jnp.zeros_like(gsum)

    @pl.when(mez == 0)
    def _():
        for ref in (xpad, spad, g3, a3):
            ref[:, 0] = jnp.zeros((T, W, ref.shape[3]), BF16)

    @pl.when(mez == nz - 1)
    def _():
        for ref in (xpad, spad, g3, a3):
            ref[:, R + 1] = jnp.zeros((T, W, ref.shape[3]), BF16)

    pl.semaphore_wait(barrier, nt + nz + nx - 3)

    def edge(stage, way, src, dst, sems=None):
        s, r = sems or (hal_s, hal_r)
        return to_rows(
            src, dst, s.at[stage, way], r.at[stage, way],
            jnp.maximum(mez - 1, 0) if way == 0 else jnp.minimum(mez + 1, nz - 1),
        )

    def edges(stage, srcs, dsts, what, sems=None):
        for way in range(2):
            from_there = (mez < nz - 1) if way == 0 else (mez > 0)
            to_there = (mez > 0) if way == 0 else (mez < nz - 1)

            @pl.when(from_there if what == "recv" else to_there)
            def _(way=way):
                copy = edge(stage, way, srcs[way], dsts[way], sems)
                {"start": copy.start, "recv": copy.wait_recv, "send": copy.wait_send}[what]()

    def received(act):
        @pl.when(mez < nz - 1)
        def _():
            act(0, R + 1)

        @pl.when(mez > 0)
        def _():
            act(1, 0)

    edge_sets = [
        (0, (x_hbm.at[:, 0], x_hbm.at[:, R - 1]), (xpad.at[:, R + 1], xpad.at[:, 0]), None),
        (1, (es.at[0], es.at[1]), (hs.at[0], hs.at[1]), None),
        (2, (eg.at[0], eg.at[1]), (hg.at[0], hg.at[1]), None),
        (3, (ea.at[0], ea.at[1]), (ha.at[0], ha.at[1]), None),
        (0, (ces.at[0, 0], ces.at[0, 1]), (cer.at[0, 0], cer.at[0, 1]), (ce_s, ce_r)),
        (1, (ces.at[1, 0], ces.at[1, 1]), (cer.at[1, 0], cer.at[1, 1]), (ce_s, ce_r)),
    ]

    def do_edges(n, what):
        stage, srcs, dsts, sems = edge_sets[n]
        edges(stage, srcs, dsts, what, sems)

    do_edges(0, "start")

    def decay_copy(k):
        return to_tm(dsend, dall.at[me], dec_s.at[k], dec_r.at[me], k)

    others(me, nt, lambda k: decay_copy(k).start())

    def send1(q, k):
        return to_tm(snd1.at[q, k], rcv1.at[q, me], p1_s.at[q, k], p1_r.at[q, me], k)

    def send2(q, k):
        return to_rows(
            snd2.at[q, pl.ds(k * BR, BR)], rcv2.at[q, mez], p2_s.at[q, k], p2_r.at[q, mez], k
        )

    def send3(q, k):
        return to_dp(x3.at[q, mex], x3.at[q, mex], p3_s.at[q, k], p3_r.at[q, mex], k)

    def send4(q, k):
        here = f4.at[q, pl.ds(mez * BR, BR)]
        return to_rows(here, here, p4_s.at[q, k], p4_r.at[q, mez], k)

    def send5(q, k):
        return to_tm(f4.at[q], g5.at[q, me], p5_s.at[q, k], p5_r.at[q, me], k)

    def got(ref, q, k, r, copy):
        return copy(ref.at[q, k], ref.at[q, k], r.at[q, k], r.at[q, k], 0).wait_recv()

    def not_me(k, act):
        @pl.when(k != mez)
        def _():
            act(k)

    def sum1(q):
        for k in range(nt):
            snd1[q, k] = acc[q, k * CH : (k + 1) * CH].astype(BF16)
        others(me, nt, lambda k: send1(q, k).start())

    def sum2(q, extra):
        def step(o, total):
            k = lax.rem(me + o, nt)
            got(rcv1, q, k, p1_r, to_tm)
            return total + rcv1[q, k].astype(F32)

        total = lax.fori_loop(1, nt, step, acc[q, pl.ds(pl.multiple_of(me * CH, 16), CH)])
        for j in range(TAPS):
            snd2[q, j * CH : (j + 1) * CH] = total[:, j * C : (j + 1) * C].astype(BF16)
        snd2[q, TAPS * CH : SR] = extra.astype(BF16)
        if NB * BR > SR:
            snd2[q, SR:] = jnp.zeros((NB * BR - SR, C), BF16)
        each(0, NB, lambda k: not_me(k, lambda k: send2(q, k).start()))

    def sum3(q):
        @pl.when(mez < NB)
        def _():
            def step(o, total):
                k = lax.rem(mez + o, nz)
                got(rcv2, q, k, p2_r, to_rows)
                return total + rcv2[q, k].astype(F32)

            mine = snd2[q, pl.ds(pl.multiple_of(mez * BR, 16), BR)].astype(F32)
            x3[q, mex] = lax.fori_loop(1, nz, step, mine)
            others(mex, nx, lambda k: send3(q, k).start())

    def sum4(q):
        @pl.when(mez < NB)
        def _():
            others(mex, nx, lambda k: got(x3, q, k, p3_r, to_dp))
            total = x3[q, 0]
            for k in range(1, nx):
                total = total + x3[q, k]
            f4[q, pl.ds(pl.multiple_of(mez * BR, 16), BR)] = total.astype(BF16)
            others(mez, nz, lambda k: send4(q, k).start())

    def sum5(q):
        def wait(k):
            there = f4.at[q, pl.ds(k * BR, BR)]
            to_rows(there, there, p4_s.at[q, k], p4_r.at[q, k], 0).wait_recv()

        each(0, NB, lambda k: not_me(k, wait))
        g5[q, me] = f4[q]
        others(me, nt, lambda k: send5(q, k).start())

    def sum6(q):
        others(me, nt, lambda k: got(g5, q, k, p5_r, to_tm))

    def sums_sent(q):
        others(me, nt, lambda k: send1(q, k).wait_send())
        each(0, NB, lambda k: not_me(k, lambda k: send2(q, k).wait_send()))

        @pl.when(mez < NB)
        def _():
            others(mex, nx, lambda k: send3(q, k).wait_send())
            others(mez, nz, lambda k: send4(q, k).wait_send())

        others(me, nt, lambda k: send5(q, k).wait_send())

    def inner(act):
        each(0, 2, lambda f: act(pl.ds(f * half, half), 1, R - 2))

    def outer(act):
        each(0, 1, lambda f: act(all_frames, 0, 1))
        each(0, 1, lambda f: act(all_frames, R - 1, 1))

    def drive(frames, r0, nr):
        y = forward_rows(xpad, w_in, frames, r0, nr)
        ag[frames, r0 : r0 + nr] = y.reshape(frames.size, nr, W, C)

    loads[1].wait()
    loads[2].wait()
    inner(drive)
    do_edges(0, "recv")
    outer(drive)

    def forward_step(t, state):
        state = lam[pl.ds(t, 1)].reshape(1, 1, C) * state + ag[t]
        st[t + 1] = state
        es[0, t] = state[0].astype(BF16)
        es[1, t] = state[R - 1].astype(BF16)
        return state

    last = lax.fori_loop(0, T, forward_step, jnp.zeros((R, W, C), F32))
    csend[0] = last.astype(BF16)

    def carry_copy(way, k):
        return to_tm(csend.at[way], crecv.at[way, me], car_s.at[way, k], car_r.at[way, me], k)

    each(me + 1, nt, lambda k: carry_copy(0, k).start())
    do_edges(1, "start")

    others(me, nt, lambda k: to_tm(dsend, dall.at[k], dec_s.at[k], dec_r.at[k], 0).wait_recv())

    def join_earlier(k, state):
        got(crecv, 0, k, car_r, to_tm)
        return dall[k, 0:1].reshape(1, 1, C) * state + crecv[0, k].astype(F32)

    carry = lax.fori_loop(0, me, join_earlier, jnp.zeros((R, W, C), F32))
    ces[0, 0] = carry[0].astype(BF16)
    ces[0, 1] = carry[R - 1].astype(BF16)
    do_edges(4, "start")
    st[0] = carry
    cin[...] = carry

    def finish_state(t):
        state = st[t + 1] + ecum[pl.ds(t, 1)].reshape(1, 1, C) * cin[...]
        st[t + 1] = state
        spad[t, 1 : R + 1] = state.astype(BF16)

    each(0, T, finish_state)

    for load in loads[3:]:
        load.wait()

    def output(frames, r0, nr):
        n = frames.size * nr
        x = xpad[frames, r0 + 1 : r0 + 1 + nr].reshape(n, W, C).astype(F32)
        pre = forward_rows(spad, w_out, frames, r0, nr) + gain[...].reshape(1, 1, C) * x
        square = pre * pre
        bend = jnp.tanh(GELU_A * (pre + GELU_B * (square * pre)))
        rise = 0.5 * (1.0 + bend)
        lo[frames, r0 : r0 + nr] = (pre * rise).astype(BF16).reshape(frames.size, nr, W, C)
        slope = rise + 0.5 * pre * (1.0 - bend * bend) * (GELU_A * (1.0 + 3.0 * GELU_B * square))
        grad = ct[frames, r0 : r0 + nr].reshape(n, W, C).astype(F32) * slope
        gp[frames, r0 : r0 + nr] = grad.reshape(frames.size, nr, W, C)
        gsum[...] += jnp.sum((grad * x).reshape(n * W // 8, 8, C), axis=0)
        widen(g3, frames, r0 + 1, nr, grad)

    inner(output)
    do_edges(1, "recv")
    do_edges(4, "recv")

    def state_edge(way, row):
        def step(t):
            value = hs[way, t].astype(F32) + ecum[pl.ds(t, 1)] * cer[0, way].astype(F32)
            spad[t, row] = value.astype(BF16)

        each(0, T, step)

    received(state_edge)
    outer(output)
    eg[0] = gp[:, 0].astype(BF16)
    eg[1] = gp[:, R - 1].astype(BF16)
    do_edges(2, "start")

    def kernel_grad(q, pad, wide):
        acc[q] = jnp.zeros((LANES, LANES), F32)
        part = T // 4

        def step(f):
            frames = pl.ds(f * part, part)
            n = part * R * W
            lhs = jnp.concatenate(
                [pad[frames, i : i + R].reshape(n, C) for i in range(TAPS)], axis=-1
            )
            rhs = wide[frames, 1 : R + 1].reshape(n, LANES)
            acc[q] += lax.dot_general(
                lhs, rhs, (((0,), (0,)), ((), ())), preferred_element_type=F32
            )

        each(0, 4, step)

    kernel_grad(0, spad, g3)
    sum1(0)

    def state_grad(frames, r0, nr):
        ag[frames, r0 : r0 + nr] = adjoint_rows(g3, w_out, frames, r0, nr).reshape(
            frames.size, nr, W, C
        )

    inner(state_grad)
    do_edges(2, "recv")
    received(lambda way, row: widen(g3, all_frames, row, 1, hg[way].astype(F32)))
    outer(state_grad)

    def backward_step(o, carried):
        t = T - 1 - o
        adjoint = ag[t] + carried
        ag[t] = adjoint
        ea[0, t] = adjoint[0].astype(BF16)
        ea[1, t] = adjoint[R - 1].astype(BF16)
        return lam[pl.ds(t, 1)].reshape(1, 1, C) * adjoint

    first = lax.fori_loop(0, T, backward_step, jnp.zeros((R, W, C), F32))
    csend[1] = first.astype(BF16)
    each(0, me, lambda k: carry_copy(1, k).start())
    do_edges(3, "start")

    zeros8 = jnp.zeros((8, C), F32)
    sum2(0, jnp.concatenate([gsum[...], zeros8], axis=0))

    def join_later(o, adjoint):
        k = nt - 1 - o
        got(crecv, 1, k, car_r, to_tm)
        return dall[k, 0:1].reshape(1, 1, C) * adjoint + crecv[1, k].astype(F32)

    back = lax.fori_loop(0, nt - 1 - me, join_later, jnp.zeros((R, W, C), F32))
    ces[1, 0] = back[0].astype(BF16)
    ces[1, 1] = back[R - 1].astype(BF16)
    do_edges(5, "start")
    bin_[...] = back

    def finish_adjoint(t):
        adjoint = ag[t] + erev[pl.ds(t, 1)].reshape(1, 1, C) * bin_[...]
        product = jnp.sum((adjoint * st[t]).reshape(R * W, C), axis=0, keepdims=True)
        dpart[pl.ds(t, 1)] = product * lam[pl.ds(t, 1)]
        for j, part in enumerate((at_next(adjoint), adjoint, at_previous(adjoint))):
            a3[t, 1 : R + 1, :, j * C : (j + 1) * C] = part.astype(BF16)

    each(0, T, finish_adjoint)
    kernel_grad(1, xpad, a3)
    sum1(1)
    sum3(0)

    def video_grad(frames, r0, nr):
        skip = gain[...].reshape(1, 1, C) * gp[frames, r0 : r0 + nr].reshape(-1, W, C)
        value = adjoint_rows(a3, w_in, frames, r0, nr) + skip
        vg[frames, r0 : r0 + nr] = value.astype(BF16).reshape(frames.size, nr, W, C)

    inner(video_grad)
    sum2(1, dpart[...])
    sum4(0)
    do_edges(3, "recv")
    do_edges(5, "recv")

    def adjoint_edge(way, row):
        def step(t):
            value = ha[way, t].astype(F32) + erev[pl.ds(t, 1)] * cer[1, way].astype(F32)
            widen(a3, pl.ds(t, 1), row, 1, value.reshape(1, W, C))

        each(0, T, step)

    received(adjoint_edge)
    sum3(1)
    sum5(0)
    outer(video_grad)
    sum4(1)
    sum6(0)
    sum5(1)
    dg_out[...] = f4[1, TAPS * CH : SR].astype(F32) * (1.0 / math.sqrt(total_cells))
    total_gain = jnp.zeros((8, C), F32)
    for k in range(nt):
        total_gain = total_gain + g5[0, k, TAPS * CH : SR].astype(F32)[0:8]
    gg_out[...] = jnp.sum(total_gain, axis=0, keepdims=True) * (1.0 / math.sqrt(total_positions))
    sum6(1)

    for n in range(6):
        do_edges(n, "send")
    others(me, nt, lambda k: decay_copy(k).wait_send())
    each(me + 1, nt, lambda k: carry_copy(0, k).wait_send())
    each(0, me, lambda k: carry_copy(1, k).wait_send())
    for q in range(2):
        sums_sent(q)


def finish(scale, lo, vg, g5, gg, dg, lo_hbm, vg_hbm, ig_hbm, og_hbm, gg_hbm, dg_hbm, grads, sems):
    nt = g5.shape[1]
    CH = LANES // nt

    def store(n, src, dst):
        copy = pltpu.make_async_copy(src, dst, sems.at[n])
        copy.start()
        return copy

    copies = [store(0, vg, vg_hbm), store(1, lo, lo_hbm)]
    copies += [store(2, gg, gg_hbm), store(3, dg, dg_hbm)]
    for q, out in ((0, og_hbm), (1, ig_hbm)):
        for k in range(nt):
            for u in range(0, CH, 16):
                i, c = divmod(k * CH + u, C)
                for j in range(TAPS):
                    piece = g5[q, k, j * CH + u : j * CH + u + 16]
                    grads[q, i, j, c : c + 16] = piece.astype(F32) * scale
        copies.append(store(4 + q, grads.at[q], out))
    for copy in copies:
        copy.wait()


def on_device(nt, nz, nx, video, cotangent, in_kernel, out_kernel, skip_gain, log_decay):
    seqs, T, R, W, _ = video.shape
    field = (T, R, W, C)
    CH = LANES // nt
    SR = TAPS * CH + 16
    BR = -(-SR // (nz * 16)) * 16
    NB = -(-SR // BR)
    dma = pltpu.SemaphoreType.DMA
    vmem = pltpu.VMEM
    scratch = [
        vmem((T, R + 2, W, C), BF16),
        vmem((T, R + 2, W, C), BF16),
        vmem((T, R + 2, W, LANES), BF16),
        vmem((T, R + 2, W, LANES), BF16),
        vmem((T + 1, R, W, C), F32),
        vmem(field, F32),
        vmem(field, F32),
        vmem(field, BF16),
        vmem((TAPS, TAPS, C, C), BF16),
        vmem((TAPS, TAPS, C, C), BF16),
        vmem((1, C), F32),
        vmem((T, C), F32),
        *[vmem((2, T, W, C), BF16)] * 6,
        *[vmem((2, 2, W, C), BF16)] * 2,
        *[vmem((T, C), F32)] * 3,
        vmem((8, C), F32),
        vmem((nt, 8, C), F32),
        vmem((2, R, W, C), BF16),
        vmem((2, nt, R, W, C), BF16),
        vmem((R, W, C), F32),
        vmem((R, W, C), F32),
        vmem((8, C), F32),
        vmem((T, C), F32),
        vmem((2, LANES, LANES), F32),
        vmem((2, nt, CH, LANES), BF16),
        vmem((2, nt, CH, LANES), BF16),
        vmem((2, NB * BR, C), BF16),
        vmem((2, nz, BR, C), BF16),
        vmem((2, nx, BR, C), F32),
        vmem((2, NB * BR, C), BF16),
        dma((6,)),
        dma((4, 2)),
        dma((4, 2)),
        dma((2, 2)),
        dma((2, 2)),
        dma((nt,)),
        dma((nt,)),
        *[dma((2, nt))] * 4,
        *[dma((2, nz))] * 2,
        *[dma((2, nx))] * 2,
        *[dma((2, nz))] * 2,
        *[dma((2, nt))] * 2,
    ]
    hbm, whole = pl.BlockSpec(memory_space=pltpu.HBM), pl.BlockSpec(memory_space=pltpu.VMEM)
    cells = seqs * nx * R * nz * W
    parts = pl.pallas_call(
        functools.partial(body, nt, nz, nx, cells, cells * T * nt),
        out_shape=(
            vmem(field, BF16),
            vmem(field, BF16),
            vmem((2, nt, NB * BR, C), BF16),
            vmem((1, C), F32),
            vmem((T, C), F32),
        ),
        in_specs=[hbm] * 6,
        out_specs=(whole,) * 5,
        scratch_shapes=scratch,
        compiler_params=pltpu.CompilerParams(
            collective_id=0, has_side_effects=True, vmem_limit_bytes=48 * 2**20
        ),
    )(
        *[
            pltpu.with_memory_space_constraint(operand, pltpu.HBM)
            for operand in (
                video.reshape(field),
                cotangent.reshape(field),
                in_kernel,
                out_kernel,
                skip_gain.reshape(1, C),
                log_decay,
            )
        ]
    )
    outs = pl.pallas_call(
        functools.partial(finish, 1.0 / math.sqrt(cells * T * nt)),
        out_shape=(
            jax.ShapeDtypeStruct(field, BF16),
            jax.ShapeDtypeStruct(field, BF16),
            jax.ShapeDtypeStruct((TAPS, TAPS, C, C), F32),
            jax.ShapeDtypeStruct((TAPS, TAPS, C, C), F32),
            jax.ShapeDtypeStruct((1, C), F32),
            jax.ShapeDtypeStruct((T, C), F32),
        ),
        in_specs=[whole] * 5,
        out_specs=(hbm,) * 6,
        scratch_shapes=[vmem((2, TAPS, TAPS, C, C), F32), dma((6,))],
        compiler_params=pltpu.CompilerParams(vmem_limit_bytes=16 * 2**20),
    )(*parts)
    layer_out, video_grad, in_grad, out_grad, gain_grad, decay_grad = outs
    return (
        layer_out.reshape(video.shape),
        video_grad.reshape(video.shape),
        in_grad,
        out_grad,
        gain_grad.reshape(C),
        decay_grad,
    )


def solution(mesh):
    field = P("dp", "tm", "rows", None, None)
    nt, nz, nx = mesh.shape["tm"], mesh.shape["rows"], mesh.shape["dp"]
    return jax.shard_map(
        functools.partial(on_device, nt, nz, nx),
        mesh=mesh,
        in_specs=(field, field, P(), P(), P(), P("tm", None)),
        out_specs=(field, field, P(), P(), P(), P("tm", None)),
        check_vma=False,
    )
```

```python
import functools
import math

import jax
import jax.numpy as jnp
from jax import lax
from jax.experimental import pallas as pl
from jax.experimental.pallas import tpu as pltpu
from jax.sharding import PartitionSpec as P

MESH = pl.DeviceIdType.MESH
F32, BF16 = jnp.float32, jnp.bfloat16
C = 128
TAPS = 3
LANES = TAPS * C
GELU_A = math.sqrt(2.0 / math.pi)
GELU_B = 0.044715


UNIT = 16
UNITS = LANES // UNIT


def share_of(nt, nx):
    return -(-(UNITS + 1) // (nt * nx)) * UNIT


def owners_of(grad, share):
    return -(-(UNITS + 1 - grad) * UNIT // share)


def at_next(field):
    cols = field.shape[1]
    col = lax.broadcasted_iota(jnp.int32, field.shape, 1)
    return jnp.where(col == cols - 1, 0.0, pltpu.roll(field, cols - 1, 1))


def at_previous(field):
    col = lax.broadcasted_iota(jnp.int32, field.shape, 1)
    return jnp.where(col == 0, 0.0, pltpu.roll(field, 1, 1))


def taps(w_ref, i):
    return jnp.concatenate([w_ref[i, j] for j in range(TAPS)], axis=-1)


def forward_rows(pad, w_ref, frames, r0, nr, which=range(TAPS)):
    n, cols = frames.size * nr, pad.shape[2]
    lhs = jnp.concatenate(
        [pad[frames, r0 + i : r0 + i + nr].reshape(n * cols, C) for i in which], axis=-1
    )
    rhs = jnp.concatenate([taps(w_ref, i) for i in which], axis=0)
    y = jnp.dot(lhs, rhs, preferred_element_type=F32).reshape(n, cols, LANES)
    return at_previous(y[..., :C]) + y[..., C : 2 * C] + at_next(y[..., 2 * C :])


def adjoint_rows(wide, w_ref, frames, r0, nr, which=range(TAPS)):
    n, cols = frames.size * nr, wide.shape[2]
    lhs = jnp.concatenate(
        [wide[frames, r0 + 2 - i : r0 + 2 - i + nr].reshape(n * cols, LANES) for i in which],
        axis=-1,
    )
    rhs = jnp.concatenate([taps(w_ref, i) for i in which], axis=-1)
    y = lax.dot_general(lhs, rhs, (((1,), (1,)), ((), ())), preferred_element_type=F32)
    return y.reshape(n, cols, C)


def widen(wide, frames, r0, nr, value):
    shape = (frames.size, nr) + value.shape[1:]
    for j, part in enumerate((at_next(value), value, at_previous(value))):
        wide[frames, r0 : r0 + nr, :, j * C : (j + 1) * C] = part.astype(BF16).reshape(shape)


def body(
    nt, nz, nx, total_cells, total_positions,
    x_hbm, ct_hbm, w_in_hbm, w_out_hbm, gain_hbm, ld_hbm,
    lo, vg, g5_0, g5_1, gg_out, dg_out,
    xpad, spad, g3, a3, st, ag, gp, ct, w_in, w_out, gain, ld,
    es, eg, ea, hs, hg, ha, ces, cer, nbs, nbr, nbd,
    lam, ecum, erev, dsend, dall, csend, crecv, cin, bin_, gsum, dpart,
    acc, loc, hal_s, hal_r, ce_s, ce_r, dec_s, dec_r, car_s, car_r,
    rcv1_0, rcv1_1, snd1_0, snd1_1, box_0, box_1, decays, sum_s, sum_r,
):
    T, R, W, _ = x_hbm.shape
    snd1, rcv1, box, g5 = (snd1_0, snd1_1), (rcv1_0, rcv1_1), (box_0, box_1), (g5_0, g5_1)
    group, share = nt * nx, rcv1_0.shape[1]
    owners = [owners_of(q, share) for q in range(2)]
    half = T // 2
    all_frames = pl.ds(0, T)
    me, mez, mex = lax.axis_index("tm"), lax.axis_index("rows"), lax.axis_index("dp")

    def to_tm(src, dst, s, r, k):
        return pltpu.make_async_remote_copy(src, dst, s, r, device_id={"tm": k}, device_id_type=MESH)

    def to_rows(src, dst, s, r, k):
        return pltpu.make_async_remote_copy(src, dst, s, r, device_id={"rows": k}, device_id_type=MESH)

    def to_dp(src, dst, s, r, k):
        return pltpu.make_async_remote_copy(src, dst, s, r, device_id={"dp": k}, device_id_type=MESH)

    def others(mine, count, act):
        def step(o, _):
            act(lax.rem(mine + o, count))
            return 0

        lax.fori_loop(1, count, step, 0)

    def each(low, high, act):
        def step(k, _):
            act(k)
            return 0

        lax.fori_loop(low, high, step, 0)

    barrier = pltpu.get_barrier_semaphore()
    mine = me * nx + mex

    def member(k):
        return {"tm": k // nx, "dp": lax.rem(k, nx)}

    def greet(place):
        pl.semaphore_signal(barrier, inc=1, device_id=place, device_id_type=MESH)

    others(mez, nz, lambda k: greet({"rows": k}))
    others(mine, group, lambda k: greet(member(k)))
    loads = [
        pltpu.make_async_copy(src, dst, loc.at[n])
        for n, (src, dst) in enumerate(
            (
                (ld_hbm, ld),
                (x_hbm, xpad.at[:, 1 : R + 1]),
                (w_in_hbm, w_in),
                (ct_hbm, ct),
                (w_out_hbm, w_out),
                (gain_hbm, gain),
            )
        )
    ]
    for load in loads:
        load.start()
    loads[0].wait()

    run = jnp.zeros((1, C), F32)
    for t in range(T):
        run = run + ld[t : t + 1]
        ecum[t : t + 1] = run
    erev[...] = jnp.exp(run - ecum[...])
    ecum[...] = jnp.exp(ecum[...])
    lam[...] = jnp.exp(ld[...])
    dsend[...] = jnp.broadcast_to(jnp.exp(run), dsend.shape)
    gsum[...] = jnp.zeros_like(gsum)

    @pl.when(mez == 0)
    def _():
        for ref in (xpad, spad, g3, a3):
            ref[:, 0] = jnp.zeros((T, W, ref.shape[3]), BF16)
        nbr[:, 1] = jnp.zeros((2, W, C), BF16)

    @pl.when(mez == nz - 1)
    def _():
        for ref in (xpad, spad, g3, a3):
            ref[:, R + 1] = jnp.zeros((T, W, ref.shape[3]), BF16)
        nbr[:, 0] = jnp.zeros((2, W, C), BF16)

    def inner(act):
        each(0, 2, lambda f: act(pl.ds(f * half, half), 1, R - 2))

    def outer(act):
        each(0, 1, lambda f: act(all_frames, 0, 1))
        each(0, 1, lambda f: act(all_frames, R - 1, 1))

    loads[1].wait()
    loads[2].wait()

    def own_part(rows_of, wide, w_ref, top, bottom):
        def some(frames, r0, nr, which=range(TAPS)):
            return rows_of(wide, w_ref, frames, r0, nr, which).reshape(frames.size, nr, W, C)

        def inner_rows(frames, r0, nr):
            ag[frames, r0 : r0 + nr] = some(frames, r0, nr)

        inner(inner_rows)
        ag[:, 0:1] = some(all_frames, 0, 1, top[1])
        ag[:, R - 1 : R] = some(all_frames, R - 1, 1, bottom[0])
        nbd[0] = some(all_frames, -1, 1, top[0]).reshape(T, W, C)
        nbd[1] = some(all_frames, R, 1, bottom[1]).reshape(T, W, C)

    own_part(forward_rows, xpad, w_in, ((2,), (1, 2)), ((0, 1), (0,)))

    def own_forward_step(t, carried):
        rate = lam[pl.ds(t, 1)]
        state = rate.reshape(1, 1, C) * carried[0] + ag[t]
        above, below = rate * carried[1] + nbd[0, t], rate * carried[2] + nbd[1, t]
        st[t + 1, 1 : R - 1] = state[1 : R - 1]
        es[0, t] = state[0].astype(BF16)
        es[1, t] = state[R - 1].astype(BF16)
        nbd[0, t] = above
        nbd[1, t] = below
        return state, above, below

    nothing = (jnp.zeros((R, W, C), F32), jnp.zeros((W, C), F32), jnp.zeros((W, C), F32))
    last, above, below = lax.fori_loop(0, T, own_forward_step, nothing)
    nbs[0, 0] = above.astype(BF16)
    nbs[0, 1] = below.astype(BF16)

    pl.semaphore_wait(barrier, nz + group - 2)

    def edge(stage, way, src, dst, sems=None):
        s, r = sems or (hal_s, hal_r)
        return to_rows(
            src, dst, s.at[stage, way], r.at[stage, way],
            jnp.maximum(mez - 1, 0) if way == 0 else jnp.minimum(mez + 1, nz - 1),
        )

    def edges(stage, srcs, dsts, what, sems=None):
        for way in range(2):
            from_there = (mez < nz - 1) if way == 0 else (mez > 0)
            to_there = (mez > 0) if way == 0 else (mez < nz - 1)

            @pl.when(from_there if what == "recv" else to_there)
            def _(way=way):
                copy = edge(stage, way, srcs[way], dsts[way], sems)
                {"start": copy.start, "recv": copy.wait_recv, "send": copy.wait_send}[what]()

    def received(act):
        @pl.when(mez < nz - 1)
        def _():
            act(0, R + 1)

        @pl.when(mez > 0)
        def _():
            act(1, 0)

    edge_sets = [
        (0, (x_hbm.at[:, 0], x_hbm.at[:, R - 1]), (xpad.at[:, R + 1], xpad.at[:, 0]), None),
        (1, (es.at[0], es.at[1]), (hs.at[0], hs.at[1]), None),
        (2, (eg.at[0], eg.at[1]), (hg.at[0], hg.at[1]), None),
        (3, (ea.at[0], ea.at[1]), (ha.at[0], ha.at[1]), None),
        (0, (ces.at[0, 0], ces.at[0, 1]), (cer.at[0, 0], cer.at[0, 1]), (ce_s, ce_r)),
        (1, (ces.at[1, 0], ces.at[1, 1]), (cer.at[1, 0], cer.at[1, 1]), (ce_s, ce_r)),
        (2, (nbs.at[0, 0], nbs.at[0, 1]), (nbr.at[0, 0], nbr.at[0, 1]), (ce_s, ce_r)),
        (3, (nbs.at[1, 0], nbs.at[1, 1]), (nbr.at[1, 0], nbr.at[1, 1]), (ce_s, ce_r)),
    ]

    def do_edges(n, what):
        stage, srcs, dsts, sems = edge_sets[n]
        edges(stage, srcs, dsts, what, sems)

    do_edges(6, "start")
    do_edges(0, "start")
    do_edges(1, "start")

    def with_neighbours(way, rows):
        return jnp.concatenate(
            [
                rows[:1] + nbr[way, 1].astype(F32)[None],
                rows[1 : R - 1],
                rows[R - 1 :] + nbr[way, 0].astype(F32)[None],
            ],
            axis=0,
        )

    def decay_copy(k):
        return to_tm(dsend, dall.at[me], dec_s.at[k], dec_r.at[me], k)

    others(me, nt, lambda k: decay_copy(k).start())

    def got(ref, q, k, r, copy):
        return copy(ref.at[q, k], ref.at[q, k], r.at[q, k], r.at[q, k], 0).wait_recv()

    def to_member(src, dst, n, q, k):
        return pltpu.make_async_remote_copy(
            src, dst, sum_s.at[n, q], sum_r.at[n, q], device_id=member(k), device_id_type=MESH
        )

    def send1(q, k):
        return to_member(snd1[q].at[k], rcv1[q].at[mine], 0, q, k)

    def send2(q, k):
        here = box[q].at[mez]
        return to_rows(here, here, sum_s.at[1, q], sum_r.at[1, q], k)

    def send3(q, k):
        here = g5[q].at[mine]
        return to_member(here, here, 2, q, k)

    def send_decay(k):
        here = decays.at[mex]
        return to_dp(here, here, sum_s.at[3, 0], sum_r.at[3, 0], k)

    def passed(n, q, ref, count, way):
        if count:
            whole = ref.at[pl.ds(0, count)]
            copy = to_member(whole, whole, n, q, 0)
            {"recv": copy.wait_recv, "send": copy.wait_send}[way]()

    def owning(q, own, other):
        pl.when(mine < owners[q])(own)
        if owners[q] < group:
            pl.when(mine >= owners[q])(other)

    def not_me(k, act):
        @pl.when(k != mine)
        def _():
            act(k)

    def sum1(q, extra=None):
        for k in range(owners[q]):
            r0 = k * share
            rows = min(share, LANES - r0)
            if rows > 0:
                snd1[q][k, 0:rows] = acc[q, r0 : r0 + rows].astype(BF16)
            if rows < share:
                snd1[q][k, max(rows, 0) :] = jnp.zeros((share - max(rows, 0), LANES), BF16)
        if extra is not None:
            k, r = divmod(LANES, share)
            snd1[q][k, r : r + UNIT, 0:C] = extra.astype(BF16)
        each(0, owners[q], lambda k: not_me(k, lambda k: send1(q, k).start()))

    def sum2(q):
        def own():
            rcv1[q][mine] = snd1[q][mine]
            passed(0, q, rcv1[q], group - 1, "recv")

            def step(k, total):
                return total + rcv1[q][k].astype(F32)

            total = lax.fori_loop(1, group, step, rcv1[q][0].astype(F32))
            for j in range(TAPS):
                part = total[:, j * C : (j + 1) * C].astype(BF16)
                box[q][mez, j * share : (j + 1) * share] = part

        def other():
            box[q][mez, 0 : TAPS * share] = jnp.zeros((TAPS * share, C), BF16)

        owning(q, own, other)
        if q == 1:
            passed(3, 0, decays, nx - 1, "recv")
            total = decays[0]
            for k in range(1, nx):
                total = total + decays[k]
            box[q][mez, TAPS * share :] = total.astype(BF16)
            others(mez, nz, lambda k: send2(q, k).start())
        else:
            owning(q, lambda: others(mez, nz, lambda k: send2(q, k).start()), lambda: None)

    def sum3(q):
        def total(r0, r1):
            value = box[q][0, r0:r1].astype(F32)
            for k in range(1, nz):
                value = value + box[q][k, r0:r1].astype(F32)
            return value

        if q == 1:
            passed(1, q, box[q], nz - 1, "recv")

        def own():
            if q == 0:
                passed(1, q, box[q], nz - 1, "recv")
            for j in range(TAPS):
                part = total(j * share, (j + 1) * share).astype(BF16)
                g5[q][mine, :, j * C : (j + 1) * C] = part
            others(mine, group, lambda k: send3(q, k).start())

        owning(q, own, lambda: None)
        if q == 1:
            dg_out[...] = total(TAPS * share, TAPS * share + T) * (1.0 / math.sqrt(total_cells))

    def sum4(q):
        owning(
            q,
            lambda: passed(2, q, g5[q], owners[q] - 1, "recv"),
            lambda: passed(2, q, g5[q], owners[q], "recv"),
        )

    def sums_sent():
        for q in range(2):
            owning(
                q,
                lambda q=q: passed(0, q, snd1[q], owners[q] - 1, "send"),
                lambda q=q: passed(0, q, snd1[q], owners[q], "send"),
            )
            owning(q, lambda q=q: passed(2, q, rcv1[q], group - 1, "send"), lambda: None)
        owning(0, lambda: passed(1, 0, box[0], nz - 1, "send"), lambda: None)
        passed(1, 1, box[1], nz - 1, "send")
        passed(3, 0, decays, nx - 1, "send")

    def carry_copy(way, k):
        return to_tm(csend.at[way], crecv.at[way, me], car_s.at[way, k], car_r.at[way, me], k)

    do_edges(6, "recv")
    csend[0] = with_neighbours(0, last).astype(BF16)
    each(me + 1, nt, lambda k: carry_copy(0, k).start())

    do_edges(0, "recv")

    def add_drive(way, row):
        r, tap = (R - 1, 2) if way == 0 else (0, 0)
        more = forward_rows(xpad, w_in, all_frames, r, 1, (tap,))
        ag[:, r : r + 1] += more.reshape(T, 1, W, C)

    received(add_drive)

    def forward_step(t, carried):
        rate = lam[pl.ds(t, 1)]
        top, bottom = rate * carried[0] + ag[t, 0], rate * carried[1] + ag[t, R - 1]
        st[t + 1, 0] = top
        st[t + 1, R - 1] = bottom
        return top, bottom

    lax.fori_loop(0, T, forward_step, nothing[1:])

    others(me, nt, lambda k: to_tm(dsend, dall.at[k], dec_s.at[k], dec_r.at[k], 0).wait_recv())

    def join_earlier(k, state):
        got(crecv, 0, k, car_r, to_tm)
        return dall[k, 0:1].reshape(1, 1, C) * state + crecv[0, k].astype(F32)

    carry = lax.fori_loop(0, me, join_earlier, jnp.zeros((R, W, C), F32))
    ces[0, 0] = carry[0].astype(BF16)
    ces[0, 1] = carry[R - 1].astype(BF16)
    do_edges(4, "start")
    st[0] = carry
    cin[...] = carry

    def finish_state(t):
        state = st[t + 1] + ecum[pl.ds(t, 1)].reshape(1, 1, C) * cin[...]
        st[t + 1] = state
        spad[t, 1 : R + 1] = state.astype(BF16)

    each(0, T, finish_state)

    for load in loads[3:]:
        load.wait()

    def output(frames, r0, nr):
        n = frames.size * nr
        x = xpad[frames, r0 + 1 : r0 + 1 + nr].reshape(n, W, C).astype(F32)
        pre = forward_rows(spad, w_out, frames, r0, nr) + gain[...].reshape(1, 1, C) * x
        square = pre * pre
        bend = jnp.tanh(GELU_A * (pre + GELU_B * (square * pre)))
        rise = 0.5 * (1.0 + bend)
        lo[frames, r0 : r0 + nr] = (pre * rise).astype(BF16).reshape(frames.size, nr, W, C)
        slope = rise + 0.5 * pre * (1.0 - bend * bend) * (GELU_A * (1.0 + 3.0 * GELU_B * square))
        grad = ct[frames, r0 : r0 + nr].reshape(n, W, C).astype(F32) * slope
        gp[frames, r0 : r0 + nr] = grad.reshape(frames.size, nr, W, C)
        gsum[...] += jnp.sum((grad * x).reshape(n * W // 8, 8, C), axis=0)
        widen(g3, frames, r0 + 1, nr, grad)

    inner(output)
    do_edges(1, "recv")
    do_edges(4, "recv")

    def state_edge(way, row):
        def step(t):
            value = hs[way, t].astype(F32) + nbd[1 - way, t]
            value = value + ecum[pl.ds(t, 1)] * cer[0, way].astype(F32)
            spad[t, row] = value.astype(BF16)

        each(0, T, step)

    received(state_edge)
    outer(output)
    eg[0] = gp[:, 0].astype(BF16)
    eg[1] = gp[:, R - 1].astype(BF16)
    def kernel_grad(q, pad, wide):
        acc[q] = jnp.zeros((LANES, LANES), F32)
        part = T // 4

        def step(f):
            frames = pl.ds(f * part, part)
            n = part * R * W
            lhs = jnp.concatenate(
                [pad[frames, i : i + R].reshape(n, C) for i in range(TAPS)], axis=-1
            )
            rhs = wide[frames, 1 : R + 1].reshape(n, LANES)
            acc[q] += lax.dot_general(
                lhs, rhs, (((0,), (0,)), ((), ())), preferred_element_type=F32
            )

        each(0, 4, step)

    own_part(adjoint_rows, g3, w_out, ((0,), (0, 1)), ((1, 2), (2,)))

    def own_backward_step(o, carried):
        t = T - 1 - o
        rate = lam[pl.ds(t, 1)]
        adjoint = ag[t] + carried[0]
        above, below = nbd[0, t] + carried[1], nbd[1, t] + carried[2]
        ag[t, 1 : R - 1] = adjoint[1 : R - 1]
        ea[0, t] = adjoint[0].astype(BF16)
        ea[1, t] = adjoint[R - 1].astype(BF16)
        nbd[0, t] = above
        nbd[1, t] = below
        return rate.reshape(1, 1, C) * adjoint, rate * above, rate * below

    first, above, below = lax.fori_loop(0, T, own_backward_step, nothing)
    nbs[1, 0] = above.astype(BF16)
    nbs[1, 1] = below.astype(BF16)
    do_edges(7, "start")
    do_edges(2, "start")
    do_edges(3, "start")
    kernel_grad(0, spad, g3)
    do_edges(7, "recv")
    csend[1] = with_neighbours(1, first).astype(BF16)
    each(0, me, lambda k: carry_copy(1, k).start())
    sum1(0, jnp.concatenate([gsum[...], jnp.zeros((8, C), F32)], axis=0))

    do_edges(2, "recv")

    def add_state_grad(way, row):
        widen(g3, all_frames, row, 1, hg[way].astype(F32))
        r, tap = (R - 1, 0) if way == 0 else (0, 2)
        more = adjoint_rows(g3, w_out, all_frames, r, 1, (tap,))
        ag[:, r : r + 1] += more.reshape(T, 1, W, C)

    received(add_state_grad)

    def backward_step(o, carried):
        t = T - 1 - o
        rate = lam[pl.ds(t, 1)]
        top, bottom = ag[t, 0] + carried[0], ag[t, R - 1] + carried[1]
        ag[t, 0] = top
        ag[t, R - 1] = bottom
        return rate * top, rate * bottom

    lax.fori_loop(0, T, backward_step, nothing[1:])

    def join_later(o, adjoint):
        k = nt - 1 - o
        got(crecv, 1, k, car_r, to_tm)
        return dall[k, 0:1].reshape(1, 1, C) * adjoint + crecv[1, k].astype(F32)

    back = lax.fori_loop(0, nt - 1 - me, join_later, jnp.zeros((R, W, C), F32))
    ces[1, 0] = back[0].astype(BF16)
    ces[1, 1] = back[R - 1].astype(BF16)
    do_edges(5, "start")
    bin_[...] = back

    def finish_adjoint(t):
        adjoint = ag[t] + erev[pl.ds(t, 1)].reshape(1, 1, C) * bin_[...]
        product = jnp.sum((adjoint * st[t]).reshape(R * W, C), axis=0, keepdims=True)
        dpart[pl.ds(t, 1)] = product * lam[pl.ds(t, 1)]
        for j, part in enumerate((at_next(adjoint), adjoint, at_previous(adjoint))):
            a3[t, 1 : R + 1, :, j * C : (j + 1) * C] = part.astype(BF16)

    each(0, T, finish_adjoint)
    kernel_grad(1, xpad, a3)
    sum1(1)
    decays[mex] = dpart[...]
    others(mex, nx, lambda k: send_decay(k).start())
    sum2(0)

    def video_grad(frames, r0, nr):
        skip = gain[...].reshape(1, 1, C) * gp[frames, r0 : r0 + nr].reshape(-1, W, C)
        value = adjoint_rows(a3, w_in, frames, r0, nr) + skip
        vg[frames, r0 : r0 + nr] = value.astype(BF16).reshape(frames.size, nr, W, C)

    inner(video_grad)
    do_edges(3, "recv")
    do_edges(5, "recv")

    def adjoint_edge(way, row):
        def step(t):
            value = ha[way, t].astype(F32) + nbd[1 - way, t]
            value = value + erev[pl.ds(t, 1)] * cer[1, way].astype(F32)
            widen(a3, pl.ds(t, 1), row, 1, value.reshape(1, W, C))

        each(0, T, step)

    received(adjoint_edge)
    outer(video_grad)
    sum3(0)
    sum2(1)
    sum4(0)
    k, r = divmod(LANES, share)
    total_gain = jnp.sum(g5[0][k, r : r + UNIT, 0:C].astype(F32), axis=0, keepdims=True)
    gg_out[...] = total_gain * (1.0 / math.sqrt(total_positions))
    sum3(1)
    sum4(1)

    for n in range(8):
        do_edges(n, "send")
    others(me, nt, lambda k: decay_copy(k).wait_send())
    each(me + 1, nt, lambda k: carry_copy(0, k).wait_send())
    each(0, me, lambda k: carry_copy(1, k).wait_send())
    sums_sent()


def finish(
    scale, lo, vg, g5_0, g5_1, gg, dg, lo_hbm, vg_hbm, ig_hbm, og_hbm, gg_hbm, dg_hbm, grads, sems
):
    def store(n, src, dst):
        copy = pltpu.make_async_copy(src, dst, sems.at[n])
        copy.start()
        return copy

    copies = [store(0, vg, vg_hbm), store(1, lo, lo_hbm)]
    copies += [store(2, gg, gg_hbm), store(3, dg, dg_hbm)]
    share = g5_0.shape[1]
    for q, g5, out in ((0, g5_0, og_hbm), (1, g5_1, ig_hbm)):
        for row in range(0, LANES, UNIT):
            k, r = divmod(row, share)
            i, c = divmod(row, C)
            for j in range(TAPS):
                piece = g5[k, r : r + UNIT, j * C : (j + 1) * C]
                grads[q, i, j, c : c + UNIT] = piece.astype(F32) * scale
        copies.append(store(4 + q, grads.at[q], out))
    for copy in copies:
        copy.wait()


def on_device(nt, nz, nx, video, cotangent, in_kernel, out_kernel, skip_gain, log_decay):
    seqs, T, R, W, _ = video.shape
    field = (T, R, W, C)
    share = share_of(nt, nx)
    owners = [owners_of(q, share) for q in range(2)]
    dma = pltpu.SemaphoreType.DMA
    vmem = pltpu.VMEM
    scratch = [
        vmem((T, R + 2, W, C), BF16),
        vmem((T, R + 2, W, C), BF16),
        vmem((T, R + 2, W, LANES), BF16),
        vmem((T, R + 2, W, LANES), BF16),
        vmem((T + 1, R, W, C), F32),
        vmem(field, F32),
        vmem(field, F32),
        vmem(field, BF16),
        vmem((TAPS, TAPS, C, C), BF16),
        vmem((TAPS, TAPS, C, C), BF16),
        vmem((1, C), F32),
        vmem((T, C), F32),
        *[vmem((2, T, W, C), BF16)] * 6,
        *[vmem((2, 2, W, C), BF16)] * 4,
        vmem((2, T, W, C), F32),
        *[vmem((T, C), F32)] * 3,
        vmem((8, C), F32),
        vmem((nt, 8, C), F32),
        vmem((2, R, W, C), BF16),
        vmem((2, nt, R, W, C), BF16),
        vmem((R, W, C), F32),
        vmem((R, W, C), F32),
        vmem((8, C), F32),
        vmem((T, C), F32),
        vmem((2, LANES, LANES), F32),
        dma((6,)),
        dma((4, 2)),
        dma((4, 2)),
        dma((4, 2)),
        dma((4, 2)),
        dma((nt,)),
        dma((nt,)),
        *[dma((2, nt))] * 2,
    ]
    scratch += [vmem((nt * nx, share, LANES), BF16)] * 2
    scratch += [vmem((n, share, LANES), BF16) for n in owners]
    scratch += [vmem((nz, TAPS * share, C), BF16), vmem((nz, TAPS * share + T, C), BF16)]
    scratch += [vmem((nx, T, C), F32), dma((4, 2)), dma((4, 2))]
    hbm, whole = pl.BlockSpec(memory_space=pltpu.HBM), pl.BlockSpec(memory_space=pltpu.VMEM)
    cells = seqs * nx * R * nz * W
    pieces = pl.pallas_call(
        functools.partial(body, nt, nz, nx, cells, cells * T * nt),
        out_shape=(
            vmem(field, BF16),
            vmem(field, BF16),
            *[vmem((n, share, LANES), BF16) for n in owners],
            vmem((1, C), F32),
            vmem((T, C), F32),
        ),
        in_specs=[hbm] * 6,
        out_specs=(whole,) * 6,
        scratch_shapes=scratch,
        compiler_params=pltpu.CompilerParams(
            collective_id=0, has_side_effects=True, vmem_limit_bytes=48 * 2**20
        ),
    )(
        *[
            pltpu.with_memory_space_constraint(operand, pltpu.HBM)
            for operand in (
                video.reshape(field),
                cotangent.reshape(field),
                in_kernel,
                out_kernel,
                skip_gain.reshape(1, C),
                log_decay,
            )
        ]
    )
    outs = pl.pallas_call(
        functools.partial(finish, 1.0 / math.sqrt(cells * T * nt)),
        out_shape=(
            jax.ShapeDtypeStruct(field, BF16),
            jax.ShapeDtypeStruct(field, BF16),
            jax.ShapeDtypeStruct((TAPS, TAPS, C, C), F32),
            jax.ShapeDtypeStruct((TAPS, TAPS, C, C), F32),
            jax.ShapeDtypeStruct((1, C), F32),
            jax.ShapeDtypeStruct((T, C), F32),
        ),
        in_specs=[whole] * 6,
        out_specs=(hbm,) * 6,
        scratch_shapes=[vmem((2, TAPS, TAPS, C, C), F32), dma((6,))],
        compiler_params=pltpu.CompilerParams(vmem_limit_bytes=16 * 2**20),
    )(*pieces)
    layer_out, video_grad, in_grad, out_grad, gain_grad, decay_grad = outs
    return (
        layer_out.reshape(video.shape),
        video_grad.reshape(video.shape),
        in_grad,
        out_grad,
        gain_grad.reshape(C),
        decay_grad,
    )


def solution(mesh):
    field = P("dp", "tm", "rows", None, None)
    nt, nz, nx = mesh.shape["tm"], mesh.shape["rows"], mesh.shape["dp"]
    return jax.shard_map(
        functools.partial(on_device, nt, nz, nx),
        mesh=mesh,
        in_specs=(field, field, P(), P(), P(), P("tm", None)),
        out_specs=(field, field, P(), P(), P(), P("tm", None)),
        check_vma=False,
    )
```

```python
import functools
import math

import jax
import jax.numpy as jnp
from jax import lax
from jax.experimental import pallas as pl
from jax.experimental.pallas import tpu as pltpu
from jax.sharding import PartitionSpec as P

MESH = pl.DeviceIdType.MESH
F32, BF16 = jnp.float32, jnp.bfloat16
C = 128
TAPS = 3
LANES = TAPS * C
GELU_A = math.sqrt(2.0 / math.pi)
GELU_B = 0.044715


UNIT = 16
UNITS = LANES // UNIT


def share_of(nt, nx):
    return -(-(UNITS + 1) // (nt * nx)) * UNIT


def owners_of(grad, share):
    return -(-(UNITS + 1 - grad) * UNIT // share)


def at_next(field):
    cols = field.shape[1]
    col = lax.broadcasted_iota(jnp.int32, field.shape, 1)
    return jnp.where(col == cols - 1, 0.0, pltpu.roll(field, cols - 1, 1))


def at_previous(field):
    col = lax.broadcasted_iota(jnp.int32, field.shape, 1)
    return jnp.where(col == 0, 0.0, pltpu.roll(field, 1, 1))


def taps(w_ref, i):
    return jnp.concatenate([w_ref[i, j] for j in range(TAPS)], axis=-1)


def forward_rows(pad, w_ref, frames, r0, nr, which=range(TAPS)):
    n, cols = frames.size * nr, pad.shape[2]
    lhs = jnp.concatenate(
        [pad[frames, r0 + i : r0 + i + nr].reshape(n * cols, C) for i in which], axis=-1
    )
    rhs = jnp.concatenate([taps(w_ref, i) for i in which], axis=0)
    y = jnp.dot(lhs, rhs, preferred_element_type=F32).reshape(n, cols, LANES)
    return at_previous(y[..., :C]) + y[..., C : 2 * C] + at_next(y[..., 2 * C :])


def adjoint_rows(wide, w_ref, frames, r0, nr, which=range(TAPS)):
    n, cols = frames.size * nr, wide.shape[2]
    lhs = jnp.concatenate(
        [wide[frames, r0 + 2 - i : r0 + 2 - i + nr].reshape(n * cols, LANES) for i in which],
        axis=-1,
    )
    rhs = jnp.concatenate([taps(w_ref, i) for i in which], axis=-1)
    y = lax.dot_general(lhs, rhs, (((1,), (1,)), ((), ())), preferred_element_type=F32)
    return y.reshape(n, cols, C)


def widen(wide, frames, r0, nr, value):
    shape = (frames.size, nr) + value.shape[1:]
    for j, part in enumerate((at_next(value), value, at_previous(value))):
        wide[frames, r0 : r0 + nr, :, j * C : (j + 1) * C] = part.astype(BF16).reshape(shape)


def body(
    nt, nz, nx, total_cells, total_positions,
    x_hbm, ct_hbm, w_in_hbm, w_out_hbm, gain_hbm, ld_hbm,
    lo, vg, g5_0, g5_1, gg_out, dg_out,
    xpad, spad, g3, a3, st, ag, gp, ct, w_in, w_out, gain, ld,
    es, eg, ea, hs, hg, ha, ces, cer, nbs, nbr, nbd,
    lam, ecum, erev, dsend, dall, csend, crecv, cin, bin_, gsum, dpart,
    acc, loc, hal_s, hal_r, ce_s, ce_r, dec_s, dec_r, car_s, car_r,
    rcv1_0, rcv1_1, snd1_0, snd1_1, box_0, box_1, decays, dbox, sum_s, sum_r,
):
    T, R, W, _ = x_hbm.shape
    snd1, rcv1, box, g5 = (snd1_0, snd1_1), (rcv1_0, rcv1_1), (box_0, box_1), (g5_0, g5_1)
    group, share = nt * nx, rcv1_0.shape[1]
    owners = [owners_of(q, share) for q in range(2)]
    half = T // 2
    all_frames = pl.ds(0, T)
    me, mez, mex = lax.axis_index("tm"), lax.axis_index("rows"), lax.axis_index("dp")

    def to_tm(src, dst, s, r, k):
        return pltpu.make_async_remote_copy(src, dst, s, r, device_id={"tm": k}, device_id_type=MESH)

    def to_rows(src, dst, s, r, k):
        return pltpu.make_async_remote_copy(src, dst, s, r, device_id={"rows": k}, device_id_type=MESH)

    def to_dp(src, dst, s, r, k):
        return pltpu.make_async_remote_copy(src, dst, s, r, device_id={"dp": k}, device_id_type=MESH)

    def others(mine, count, act):
        def step(o, _):
            act(lax.rem(mine + o, count))
            return 0

        lax.fori_loop(1, count, step, 0)

    def each(low, high, act):
        def step(k, _):
            act(k)
            return 0

        lax.fori_loop(low, high, step, 0)

    barrier = pltpu.get_barrier_semaphore()
    mine = me * nx + mex

    def member(k):
        return {"tm": k // nx, "dp": lax.rem(k, nx)}

    def greet(place):
        pl.semaphore_signal(barrier, inc=1, device_id=place, device_id_type=MESH)

    others(mez, nz, lambda k: greet({"rows": k}))
    others(mine, group, lambda k: greet(member(k)))
    loads = [
        pltpu.make_async_copy(src, dst, loc.at[n])
        for n, (src, dst) in enumerate(
            (
                (ld_hbm, ld),
                (x_hbm, xpad.at[:, 1 : R + 1]),
                (w_in_hbm, w_in),
                (ct_hbm, ct),
                (w_out_hbm, w_out),
                (gain_hbm, gain),
            )
        )
    ]
    for load in loads:
        load.start()
    loads[0].wait()

    run = jnp.zeros((1, C), F32)
    for t in range(T):
        run = run + ld[t : t + 1]
        ecum[t : t + 1] = run
    erev[...] = jnp.exp(run - ecum[...])
    ecum[...] = jnp.exp(ecum[...])
    lam[...] = jnp.exp(ld[...])
    dsend[...] = jnp.broadcast_to(jnp.exp(run), dsend.shape)
    gsum[...] = jnp.zeros_like(gsum)

    @pl.when(mez == 0)
    def _():
        for ref in (xpad, spad, g3, a3):
            ref[:, 0] = jnp.zeros((T, W, ref.shape[3]), BF16)
        nbr[:, 1] = jnp.zeros((2, W, C), BF16)

    @pl.when(mez == nz - 1)
    def _():
        for ref in (xpad, spad, g3, a3):
            ref[:, R + 1] = jnp.zeros((T, W, ref.shape[3]), BF16)
        nbr[:, 0] = jnp.zeros((2, W, C), BF16)

    def inner(act):
        each(0, 2, lambda f: act(pl.ds(f * half, half), 1, R - 2))

    def outer(act):
        each(0, 1, lambda f: act(all_frames, 0, 1))
        each(0, 1, lambda f: act(all_frames, R - 1, 1))

    loads[1].wait()
    loads[2].wait()

    def own_part(rows_of, wide, w_ref, top, bottom):
        def some(frames, r0, nr, which=range(TAPS)):
            return rows_of(wide, w_ref, frames, r0, nr, which).reshape(frames.size, nr, W, C)

        def inner_rows(frames, r0, nr):
            ag[frames, r0 : r0 + nr] = some(frames, r0, nr)

        inner(inner_rows)
        ag[:, 0:1] = some(all_frames, 0, 1, top[1])
        ag[:, R - 1 : R] = some(all_frames, R - 1, 1, bottom[0])
        nbd[0] = some(all_frames, -1, 1, top[0]).reshape(T, W, C)
        nbd[1] = some(all_frames, R, 1, bottom[1]).reshape(T, W, C)

    own_part(forward_rows, xpad, w_in, ((2,), (1, 2)), ((0, 1), (0,)))

    def own_forward_step(t, carried):
        rate = lam[pl.ds(t, 1)]
        state = rate.reshape(1, 1, C) * carried[0] + ag[t]
        above, below = rate * carried[1] + nbd[0, t], rate * carried[2] + nbd[1, t]
        st[t + 1, 1 : R - 1] = state[1 : R - 1]
        es[0, t] = state[0].astype(BF16)
        es[1, t] = state[R - 1].astype(BF16)
        nbd[0, t] = above
        nbd[1, t] = below
        return state, above, below

    nothing = (jnp.zeros((R, W, C), F32), jnp.zeros((W, C), F32), jnp.zeros((W, C), F32))
    last, above, below = lax.fori_loop(0, T, own_forward_step, nothing)
    nbs[0, 0] = above.astype(BF16)
    nbs[0, 1] = below.astype(BF16)

    pl.semaphore_wait(barrier, nz + group - 2)

    def edge(stage, way, src, dst, sems=None):
        s, r = sems or (hal_s, hal_r)
        return to_rows(
            src, dst, s.at[stage, way], r.at[stage, way],
            jnp.maximum(mez - 1, 0) if way == 0 else jnp.minimum(mez + 1, nz - 1),
        )

    def edges(stage, srcs, dsts, what, sems=None):
        for way in range(2):
            from_there = (mez < nz - 1) if way == 0 else (mez > 0)
            to_there = (mez > 0) if way == 0 else (mez < nz - 1)

            @pl.when(from_there if what == "recv" else to_there)
            def _(way=way):
                copy = edge(stage, way, srcs[way], dsts[way], sems)
                {"start": copy.start, "recv": copy.wait_recv, "send": copy.wait_send}[what]()

    def received(act):
        @pl.when(mez < nz - 1)
        def _():
            act(0, R + 1)

        @pl.when(mez > 0)
        def _():
            act(1, 0)

    edge_sets = [
        (0, (x_hbm.at[:, 0], x_hbm.at[:, R - 1]), (xpad.at[:, R + 1], xpad.at[:, 0]), None),
        (1, (es.at[0], es.at[1]), (hs.at[0], hs.at[1]), None),
        (2, (eg.at[0], eg.at[1]), (hg.at[0], hg.at[1]), None),
        (3, (ea.at[0], ea.at[1]), (ha.at[0], ha.at[1]), None),
        (0, (ces.at[0, 0], ces.at[0, 1]), (cer.at[0, 0], cer.at[0, 1]), (ce_s, ce_r)),
        (1, (ces.at[1, 0], ces.at[1, 1]), (cer.at[1, 0], cer.at[1, 1]), (ce_s, ce_r)),
        (2, (nbs.at[0, 0], nbs.at[0, 1]), (nbr.at[0, 0], nbr.at[0, 1]), (ce_s, ce_r)),
        (3, (nbs.at[1, 0], nbs.at[1, 1]), (nbr.at[1, 0], nbr.at[1, 1]), (ce_s, ce_r)),
    ]

    def do_edges(n, what):
        stage, srcs, dsts, sems = edge_sets[n]
        edges(stage, srcs, dsts, what, sems)

    do_edges(6, "start")
    do_edges(0, "start")
    do_edges(1, "start")

    def with_neighbours(way, rows):
        return jnp.concatenate(
            [
                rows[:1] + nbr[way, 1].astype(F32)[None],
                rows[1 : R - 1],
                rows[R - 1 :] + nbr[way, 0].astype(F32)[None],
            ],
            axis=0,
        )

    def decay_copy(k):
        return to_tm(dsend, dall.at[me], dec_s.at[k], dec_r.at[me], k)

    others(me, nt, lambda k: decay_copy(k).start())

    def got(ref, q, k, r, copy):
        return copy(ref.at[q, k], ref.at[q, k], r.at[q, k], r.at[q, k], 0).wait_recv()

    def to_member(src, dst, n, q, k):
        return pltpu.make_async_remote_copy(
            src, dst, sum_s.at[n, q], sum_r.at[n, q], device_id=member(k), device_id_type=MESH
        )

    def send1(q, k):
        return to_member(snd1[q].at[k], rcv1[q].at[mine], 0, q, k)

    def send2(q, k):
        here = box[q].at[mez]
        return to_rows(here, here, sum_s.at[1, q], sum_r.at[1, q], k)

    def send3(q, k):
        here = g5[q].at[mine]
        return to_member(here, here, 2, q, k)

    def send_decay(k):
        here = decays.at[mex]
        return to_dp(here, here, sum_s.at[3, 0], sum_r.at[3, 0], k)

    def send_decay_band(k):
        here = dbox.at[mez]
        return to_rows(here, here, sum_s.at[3, 1], sum_r.at[3, 1], k)

    def passed(n, q, ref, count, way):
        if count:
            whole = ref.at[pl.ds(0, count)]
            copy = to_member(whole, whole, n, q, 0)
            {"recv": copy.wait_recv, "send": copy.wait_send}[way]()

    def owning(q, own, other):
        pl.when(mine < owners[q])(own)
        if owners[q] < group:
            pl.when(mine >= owners[q])(other)

    def not_me(k, act):
        @pl.when(k != mine)
        def _():
            act(k)

    def sum1(q, extra=None):
        for k in range(owners[q]):
            r0 = k * share
            rows = min(share, LANES - r0)
            if rows > 0:
                snd1[q][k, 0:rows] = acc[q, r0 : r0 + rows].astype(BF16)
            if rows < share:
                snd1[q][k, max(rows, 0) :] = jnp.zeros((share - max(rows, 0), LANES), BF16)
        if extra is not None:
            k, r = divmod(LANES, share)
            snd1[q][k, r : r + UNIT, 0:C] = extra.astype(BF16)
        each(0, owners[q], lambda k: not_me(k, lambda k: send1(q, k).start()))

    def sum2(q):
        def own():
            rcv1[q][mine] = snd1[q][mine]
            passed(0, q, rcv1[q], group - 1, "recv")

            def step(k, total):
                return total + rcv1[q][k].astype(F32)

            total = lax.fori_loop(1, group, step, rcv1[q][0].astype(F32))
            for j in range(TAPS):
                part = total[:, j * C : (j + 1) * C].astype(BF16)
                box[q][mez, j * share : (j + 1) * share] = part

            others(mez, nz, lambda k: send2(q, k).start())

        owning(q, own, lambda: None)

    def sum3(q):
        def own():
            passed(1, q, box[q], nz - 1, "recv")
            total = box[q][0].astype(F32)
            for k in range(1, nz):
                total = total + box[q][k].astype(F32)
            for j in range(TAPS):
                part = total[j * share : (j + 1) * share].astype(BF16)
                g5[q][mine, :, j * C : (j + 1) * C] = part
            others(mine, group, lambda k: send3(q, k).start())

        owning(q, own, lambda: None)

    def decay1():
        decays[mex] = dpart[...]
        others(mex, nx, lambda k: send_decay(k).start())

    def decay2():
        passed(3, 0, decays, nx - 1, "recv")
        total = decays[0]
        for k in range(1, nx):
            total = total + decays[k]
        dbox[mez] = total.astype(BF16)
        others(mez, nz, lambda k: send_decay_band(k).start())

    def decay3():
        passed(3, 1, dbox, nz - 1, "recv")
        total = dbox[0].astype(F32)
        for k in range(1, nz):
            total = total + dbox[k].astype(F32)
        dg_out[...] = total * (1.0 / math.sqrt(total_cells))

    def sum4(q):
        owning(
            q,
            lambda: passed(2, q, g5[q], owners[q] - 1, "recv"),
            lambda: passed(2, q, g5[q], owners[q], "recv"),
        )

    def sums_sent():
        for q in range(2):
            owning(
                q,
                lambda q=q: passed(0, q, snd1[q], owners[q] - 1, "send"),
                lambda q=q: passed(0, q, snd1[q], owners[q], "send"),
            )
            owning(q, lambda q=q: passed(2, q, rcv1[q], group - 1, "send"), lambda: None)
            owning(q, lambda q=q: passed(1, q, box[q], nz - 1, "send"), lambda: None)
        passed(3, 1, dbox, nz - 1, "send")
        passed(3, 0, decays, nx - 1, "send")

    def carry_copy(way, k):
        return to_tm(csend.at[way], crecv.at[way, me], car_s.at[way, k], car_r.at[way, me], k)

    do_edges(6, "recv")
    csend[0] = with_neighbours(0, last).astype(BF16)
    each(me + 1, nt, lambda k: carry_copy(0, k).start())

    do_edges(0, "recv")

    def add_drive(way, row):
        r, tap = (R - 1, 2) if way == 0 else (0, 0)
        more = forward_rows(xpad, w_in, all_frames, r, 1, (tap,))
        ag[:, r : r + 1] += more.reshape(T, 1, W, C)

    received(add_drive)

    def forward_step(t, carried):
        rate = lam[pl.ds(t, 1)]
        top, bottom = rate * carried[0] + ag[t, 0], rate * carried[1] + ag[t, R - 1]
        st[t + 1, 0] = top
        st[t + 1, R - 1] = bottom
        return top, bottom

    lax.fori_loop(0, T, forward_step, nothing[1:])

    others(me, nt, lambda k: to_tm(dsend, dall.at[k], dec_s.at[k], dec_r.at[k], 0).wait_recv())

    def join_earlier(k, state):
        got(crecv, 0, k, car_r, to_tm)
        return dall[k, 0:1].reshape(1, 1, C) * state + crecv[0, k].astype(F32)

    carry = lax.fori_loop(0, me, join_earlier, jnp.zeros((R, W, C), F32))
    ces[0, 0] = carry[0].astype(BF16)
    ces[0, 1] = carry[R - 1].astype(BF16)
    do_edges(4, "start")
    st[0] = carry
    cin[...] = carry

    def finish_state(t):
        state = st[t + 1] + ecum[pl.ds(t, 1)].reshape(1, 1, C) * cin[...]
        st[t + 1] = state
        spad[t, 1 : R + 1] = state.astype(BF16)

    each(0, T, finish_state)

    for load in loads[3:]:
        load.wait()

    def output(frames, r0, nr):
        n = frames.size * nr
        x = xpad[frames, r0 + 1 : r0 + 1 + nr].reshape(n, W, C).astype(F32)
        pre = forward_rows(spad, w_out, frames, r0, nr) + gain[...].reshape(1, 1, C) * x
        square = pre * pre
        bend = jnp.tanh(GELU_A * (pre + GELU_B * (square * pre)))
        rise = 0.5 * (1.0 + bend)
        lo[frames, r0 : r0 + nr] = (pre * rise).astype(BF16).reshape(frames.size, nr, W, C)
        slope = rise + 0.5 * pre * (1.0 - bend * bend) * (GELU_A * (1.0 + 3.0 * GELU_B * square))
        grad = ct[frames, r0 : r0 + nr].reshape(n, W, C).astype(F32) * slope
        gp[frames, r0 : r0 + nr] = grad.reshape(frames.size, nr, W, C)
        gsum[...] += jnp.sum((grad * x).reshape(n * W // 8, 8, C), axis=0)
        widen(g3, frames, r0 + 1, nr, grad)

    inner(output)
    do_edges(1, "recv")
    do_edges(4, "recv")

    def state_edge(way, row):
        def step(t):
            value = hs[way, t].astype(F32) + nbd[1 - way, t]
            value = value + ecum[pl.ds(t, 1)] * cer[0, way].astype(F32)
            spad[t, row] = value.astype(BF16)

        each(0, T, step)

    received(state_edge)
    outer(output)
    eg[0] = gp[:, 0].astype(BF16)
    eg[1] = gp[:, R - 1].astype(BF16)
    def kernel_grad(q, pad, wide):
        acc[q] = jnp.zeros((LANES, LANES), F32)
        part = T // 4

        def step(f):
            frames = pl.ds(f * part, part)
            n = part * R * W
            lhs = jnp.concatenate(
                [pad[frames, i : i + R].reshape(n, C) for i in range(TAPS)], axis=-1
            )
            rhs = wide[frames, 1 : R + 1].reshape(n, LANES)
            acc[q] += lax.dot_general(
                lhs, rhs, (((0,), (0,)), ((), ())), preferred_element_type=F32
            )

        each(0, 4, step)

    own_part(adjoint_rows, g3, w_out, ((0,), (0, 1)), ((1, 2), (2,)))

    def own_backward_step(o, carried):
        t = T - 1 - o
        rate = lam[pl.ds(t, 1)]
        adjoint = ag[t] + carried[0]
        above, below = nbd[0, t] + carried[1], nbd[1, t] + carried[2]
        ag[t, 1 : R - 1] = adjoint[1 : R - 1]
        ea[0, t] = adjoint[0].astype(BF16)
        ea[1, t] = adjoint[R - 1].astype(BF16)
        nbd[0, t] = above
        nbd[1, t] = below
        return rate.reshape(1, 1, C) * adjoint, rate * above, rate * below

    first, above, below = lax.fori_loop(0, T, own_backward_step, nothing)
    nbs[1, 0] = above.astype(BF16)
    nbs[1, 1] = below.astype(BF16)
    do_edges(7, "start")
    do_edges(2, "start")
    do_edges(3, "start")
    kernel_grad(0, spad, g3)
    do_edges(7, "recv")
    csend[1] = with_neighbours(1, first).astype(BF16)
    each(0, me, lambda k: carry_copy(1, k).start())
    sum1(0, jnp.concatenate([gsum[...], jnp.zeros((8, C), F32)], axis=0))

    do_edges(2, "recv")

    def add_state_grad(way, row):
        widen(g3, all_frames, row, 1, hg[way].astype(F32))
        r, tap = (R - 1, 0) if way == 0 else (0, 2)
        more = adjoint_rows(g3, w_out, all_frames, r, 1, (tap,))
        ag[:, r : r + 1] += more.reshape(T, 1, W, C)

    received(add_state_grad)

    def backward_step(o, carried):
        t = T - 1 - o
        rate = lam[pl.ds(t, 1)]
        top, bottom = ag[t, 0] + carried[0], ag[t, R - 1] + carried[1]
        ag[t, 0] = top
        ag[t, R - 1] = bottom
        return rate * top, rate * bottom

    lax.fori_loop(0, T, backward_step, nothing[1:])

    def join_later(o, adjoint):
        k = nt - 1 - o
        got(crecv, 1, k, car_r, to_tm)
        return dall[k, 0:1].reshape(1, 1, C) * adjoint + crecv[1, k].astype(F32)

    back = lax.fori_loop(0, nt - 1 - me, join_later, jnp.zeros((R, W, C), F32))
    ces[1, 0] = back[0].astype(BF16)
    ces[1, 1] = back[R - 1].astype(BF16)
    do_edges(5, "start")
    bin_[...] = back

    def finish_adjoint(t):
        adjoint = ag[t] + erev[pl.ds(t, 1)].reshape(1, 1, C) * bin_[...]
        product = jnp.sum((adjoint * st[t]).reshape(R * W, C), axis=0, keepdims=True)
        dpart[pl.ds(t, 1)] = product * lam[pl.ds(t, 1)]
        for j, part in enumerate((at_next(adjoint), adjoint, at_previous(adjoint))):
            a3[t, 1 : R + 1, :, j * C : (j + 1) * C] = part.astype(BF16)

    each(0, T, finish_adjoint)
    kernel_grad(1, xpad, a3)
    sum1(1)
    decay1()
    sum2(0)

    def video_grad(frames, r0, nr):
        skip = gain[...].reshape(1, 1, C) * gp[frames, r0 : r0 + nr].reshape(-1, W, C)
        value = adjoint_rows(a3, w_in, frames, r0, nr) + skip
        vg[frames, r0 : r0 + nr] = value.astype(BF16).reshape(frames.size, nr, W, C)

    inner(video_grad)
    do_edges(3, "recv")
    do_edges(5, "recv")

    def adjoint_edge(way, row):
        def step(t):
            value = ha[way, t].astype(F32) + nbd[1 - way, t]
            value = value + erev[pl.ds(t, 1)] * cer[1, way].astype(F32)
            widen(a3, pl.ds(t, 1), row, 1, value.reshape(1, W, C))

        each(0, T, step)

    received(adjoint_edge)
    outer(video_grad)
    sum2(1)
    decay2()
    sum3(0)
    sum3(1)
    sum4(0)
    k, r = divmod(LANES, share)
    total_gain = jnp.sum(g5[0][k, r : r + UNIT, 0:C].astype(F32), axis=0, keepdims=True)
    gg_out[...] = total_gain * (1.0 / math.sqrt(total_positions))
    decay3()
    sum4(1)

    for n in range(8):
        do_edges(n, "send")
    others(me, nt, lambda k: decay_copy(k).wait_send())
    each(me + 1, nt, lambda k: carry_copy(0, k).wait_send())
    each(0, me, lambda k: carry_copy(1, k).wait_send())
    sums_sent()


def finish(
    scale, lo, vg, g5_0, g5_1, gg, dg, lo_hbm, vg_hbm, ig_hbm, og_hbm, gg_hbm, dg_hbm, grads, sems
):
    def store(n, src, dst):
        copy = pltpu.make_async_copy(src, dst, sems.at[n])
        copy.start()
        return copy

    copies = [store(0, vg, vg_hbm), store(1, lo, lo_hbm)]
    copies += [store(2, gg, gg_hbm), store(3, dg, dg_hbm)]
    share = g5_0.shape[1]
    for q, g5, out in ((0, g5_0, og_hbm), (1, g5_1, ig_hbm)):
        for row in range(0, LANES, UNIT):
            k, r = divmod(row, share)
            i, c = divmod(row, C)
            for j in range(TAPS):
                piece = g5[k, r : r + UNIT, j * C : (j + 1) * C]
                grads[q, i, j, c : c + UNIT] = piece.astype(F32) * scale
        copies.append(store(4 + q, grads.at[q], out))
    for copy in copies:
        copy.wait()


def on_device(nt, nz, nx, video, cotangent, in_kernel, out_kernel, skip_gain, log_decay):
    seqs, T, R, W, _ = video.shape
    field = (T, R, W, C)
    share = share_of(nt, nx)
    owners = [owners_of(q, share) for q in range(2)]
    dma = pltpu.SemaphoreType.DMA
    vmem = pltpu.VMEM
    scratch = [
        vmem((T, R + 2, W, C), BF16),
        vmem((T, R + 2, W, C), BF16),
        vmem((T, R + 2, W, LANES), BF16),
        vmem((T, R + 2, W, LANES), BF16),
        vmem((T + 1, R, W, C), F32),
        vmem(field, F32),
        vmem(field, F32),
        vmem(field, BF16),
        vmem((TAPS, TAPS, C, C), BF16),
        vmem((TAPS, TAPS, C, C), BF16),
        vmem((1, C), F32),
        vmem((T, C), F32),
        *[vmem((2, T, W, C), BF16)] * 6,
        *[vmem((2, 2, W, C), BF16)] * 4,
        vmem((2, T, W, C), F32),
        *[vmem((T, C), F32)] * 3,
        vmem((8, C), F32),
        vmem((nt, 8, C), F32),
        vmem((2, R, W, C), BF16),
        vmem((2, nt, R, W, C), BF16),
        vmem((R, W, C), F32),
        vmem((R, W, C), F32),
        vmem((8, C), F32),
        vmem((T, C), F32),
        vmem((2, LANES, LANES), F32),
        dma((6,)),
        dma((4, 2)),
        dma((4, 2)),
        dma((4, 2)),
        dma((4, 2)),
        dma((nt,)),
        dma((nt,)),
        *[dma((2, nt))] * 2,
    ]
    scratch += [vmem((nt * nx, share, LANES), BF16)] * 2
    scratch += [vmem((n, share, LANES), BF16) for n in owners]
    scratch += [vmem((nz, TAPS * share, C), BF16)] * 2
    scratch += [vmem((nx, T, C), F32), vmem((nz, T, C), BF16), dma((4, 2)), dma((4, 2))]
    hbm, whole = pl.BlockSpec(memory_space=pltpu.HBM), pl.BlockSpec(memory_space=pltpu.VMEM)
    cells = seqs * nx * R * nz * W
    pieces = pl.pallas_call(
        functools.partial(body, nt, nz, nx, cells, cells * T * nt),
        out_shape=(
            vmem(field, BF16),
            vmem(field, BF16),
            *[vmem((n, share, LANES), BF16) for n in owners],
            vmem((1, C), F32),
            vmem((T, C), F32),
        ),
        in_specs=[hbm] * 6,
        out_specs=(whole,) * 6,
        scratch_shapes=scratch,
        compiler_params=pltpu.CompilerParams(
            collective_id=0, has_side_effects=True, vmem_limit_bytes=48 * 2**20
        ),
    )(
        *[
            pltpu.with_memory_space_constraint(operand, pltpu.HBM)
            for operand in (
                video.reshape(field),
                cotangent.reshape(field),
                in_kernel,
                out_kernel,
                skip_gain.reshape(1, C),
                log_decay,
            )
        ]
    )
    outs = pl.pallas_call(
        functools.partial(finish, 1.0 / math.sqrt(cells * T * nt)),
        out_shape=(
            jax.ShapeDtypeStruct(field, BF16),
            jax.ShapeDtypeStruct(field, BF16),
            jax.ShapeDtypeStruct((TAPS, TAPS, C, C), F32),
            jax.ShapeDtypeStruct((TAPS, TAPS, C, C), F32),
            jax.ShapeDtypeStruct((1, C), F32),
            jax.ShapeDtypeStruct((T, C), F32),
        ),
        in_specs=[whole] * 6,
        out_specs=(hbm,) * 6,
        scratch_shapes=[vmem((2, TAPS, TAPS, C, C), F32), dma((6,))],
        compiler_params=pltpu.CompilerParams(vmem_limit_bytes=16 * 2**20),
    )(*pieces)
    layer_out, video_grad, in_grad, out_grad, gain_grad, decay_grad = outs
    return (
        layer_out.reshape(video.shape),
        video_grad.reshape(video.shape),
        in_grad,
        out_grad,
        gain_grad.reshape(C),
        decay_grad,
    )


def solution(mesh):
    field = P("dp", "tm", "rows", None, None)
    nt, nz, nx = mesh.shape["tm"], mesh.shape["rows"], mesh.shape["dp"]
    return jax.shard_map(
        functools.partial(on_device, nt, nz, nx),
        mesh=mesh,
        in_specs=(field, field, P(), P(), P(), P("tm", None)),
        out_specs=(field, field, P(), P(), P(), P("tm", None)),
        check_vma=False,
    )
```

```python
import functools
import math

import jax
import jax.numpy as jnp
from jax import lax
from jax.experimental import pallas as pl
from jax.experimental.pallas import tpu as pltpu
from jax.sharding import PartitionSpec as P

MESH = pl.DeviceIdType.MESH
F32, BF16 = jnp.float32, jnp.bfloat16
C = 128
TAPS = 3
LANES = TAPS * C
GELU_A = math.sqrt(2.0 / math.pi)
GELU_B = 0.044715


UNIT = 16
UNITS = LANES // UNIT


def share_of(nt, nx):
    return -(-(UNITS + 1) // (nt * nx)) * UNIT


def owners_of(grad, share):
    return -(-(UNITS + 1 - grad) * UNIT // share)


def at_next(field):
    cols = field.shape[1]
    col = lax.broadcasted_iota(jnp.int32, field.shape, 1)
    return jnp.where(col == cols - 1, 0.0, pltpu.roll(field, cols - 1, 1))


def at_previous(field):
    col = lax.broadcasted_iota(jnp.int32, field.shape, 1)
    return jnp.where(col == 0, 0.0, pltpu.roll(field, 1, 1))


def taps(w_ref, i):
    return jnp.concatenate([w_ref[i, j] for j in range(TAPS)], axis=-1)


def forward_rows(pad, w_ref, frames, r0, nr, which=range(TAPS)):
    n, cols = frames.size * nr, pad.shape[2]
    lhs = jnp.concatenate(
        [pad[frames, r0 + i : r0 + i + nr].reshape(n * cols, C) for i in which], axis=-1
    )
    rhs = jnp.concatenate([taps(w_ref, i) for i in which], axis=0)
    y = jnp.dot(lhs, rhs, preferred_element_type=F32).reshape(n, cols, LANES)
    return at_previous(y[..., :C]) + y[..., C : 2 * C] + at_next(y[..., 2 * C :])


def adjoint_rows(wide, w_ref, frames, r0, nr, which=range(TAPS)):
    n, cols = frames.size * nr, wide.shape[2]
    lhs = jnp.concatenate(
        [wide[frames, r0 + 2 - i : r0 + 2 - i + nr].reshape(n * cols, LANES) for i in which],
        axis=-1,
    )
    rhs = jnp.concatenate([taps(w_ref, i) for i in which], axis=-1)
    y = lax.dot_general(lhs, rhs, (((1,), (1,)), ((), ())), preferred_element_type=F32)
    return y.reshape(n, cols, C)


def widen(wide, frames, r0, nr, value):
    shape = (frames.size, nr) + value.shape[1:]
    for j, part in enumerate((at_next(value), value, at_previous(value))):
        wide[frames, r0 : r0 + nr, :, j * C : (j + 1) * C] = part.astype(BF16).reshape(shape)


def body(
    nt, nz, nx, total_cells, total_positions,
    x_hbm, ct_hbm, w_in_hbm, w_out_hbm, gain_hbm, ld_hbm,
    lo, vg, g5_0, g5_1, gg_out, dg_out,
    xpad, spad, g3, a3, st, ag, gp, ct, w_in, w_out, gain, ld,
    es, eg, ea, hs, hg, ha, ces, cer, nbs, nbr, nbd,
    lam, ecum, erev, dsend, dall, csend, crecv, cin, bin_, gsum, dpart,
    acc, loc, hal_s, hal_r, ce_s, ce_r, dec_s, dec_r, car_s, car_r,
    rcv1_0, rcv1_1, snd1_0, snd1_1, box_0, box_1, decays, dbox, sum_s, sum_r,
):
    T, R, W, _ = x_hbm.shape
    snd1, rcv1, box, g5 = (snd1_0, snd1_1), (rcv1_0, rcv1_1), (box_0, box_1), (g5_0, g5_1)
    group, share = nt * nx, rcv1_0.shape[1]
    owners = [owners_of(q, share) for q in range(2)]
    half = T // 2
    all_frames = pl.ds(0, T)
    me, mez, mex = lax.axis_index("tm"), lax.axis_index("rows"), lax.axis_index("dp")

    def to_tm(src, dst, s, r, k):
        return pltpu.make_async_remote_copy(src, dst, s, r, device_id={"tm": k}, device_id_type=MESH)

    def to_rows(src, dst, s, r, k):
        return pltpu.make_async_remote_copy(src, dst, s, r, device_id={"rows": k}, device_id_type=MESH)

    def to_dp(src, dst, s, r, k):
        return pltpu.make_async_remote_copy(src, dst, s, r, device_id={"dp": k}, device_id_type=MESH)

    def others(mine, count, act):
        def step(o, _):
            act(lax.rem(mine + o, count))
            return 0

        lax.fori_loop(1, count, step, 0)

    def each(low, high, act):
        def step(k, _):
            act(k)
            return 0

        lax.fori_loop(low, high, step, 0)

    barrier = pltpu.get_barrier_semaphore()
    mine = me * nx + mex

    def member(k):
        return {"tm": k // nx, "dp": lax.rem(k, nx)}

    def greet(place):
        pl.semaphore_signal(barrier, inc=1, device_id=place, device_id_type=MESH)

    others(mez, nz, lambda k: greet({"rows": k}))
    others(mine, group, lambda k: greet(member(k)))
    loads = [
        pltpu.make_async_copy(src, dst, loc.at[n])
        for n, (src, dst) in enumerate(
            (
                (ld_hbm, ld),
                (x_hbm, xpad.at[:, 1 : R + 1]),
                (w_in_hbm, w_in),
                (ct_hbm, ct),
                (w_out_hbm, w_out),
                (gain_hbm, gain),
            )
        )
    ]
    for load in loads:
        load.start()
    loads[0].wait()

    run = jnp.zeros((1, C), F32)
    for t in range(T):
        run = run + ld[t : t + 1]
        ecum[t : t + 1] = run
    erev[...] = jnp.exp(run - ecum[...])
    ecum[...] = jnp.exp(ecum[...])
    lam[...] = jnp.exp(ld[...])
    dsend[...] = jnp.broadcast_to(jnp.exp(run), dsend.shape)
    gsum[...] = jnp.zeros_like(gsum)

    @pl.when(mez == 0)
    def _():
        for ref in (xpad, spad, g3, a3):
            ref[:, 0] = jnp.zeros((T, W, ref.shape[3]), BF16)
        nbr[:, 1] = jnp.zeros((2, W, C), BF16)

    @pl.when(mez == nz - 1)
    def _():
        for ref in (xpad, spad, g3, a3):
            ref[:, R + 1] = jnp.zeros((T, W, ref.shape[3]), BF16)
        nbr[:, 0] = jnp.zeros((2, W, C), BF16)

    def inner(act):
        each(0, 2, lambda f: act(pl.ds(f * half, half), 1, R - 2))

    def outer(act):
        each(0, 1, lambda f: act(all_frames, 0, 1))
        each(0, 1, lambda f: act(all_frames, R - 1, 1))

    loads[1].wait()
    loads[2].wait()

    def some_rows(rows_of, wide, w_ref, frames, r0, nr, which=range(TAPS)):
        return rows_of(wide, w_ref, frames, r0, nr, which).reshape(frames.size, nr, W, C)

    def own_rows(rows_of, wide, w_ref, top, bottom):
        def inner_rows(frames, r0, nr):
            ag[frames, r0 : r0 + nr] = some_rows(rows_of, wide, w_ref, frames, r0, nr)

        inner(inner_rows)
        ag[:, 0:1] = some_rows(rows_of, wide, w_ref, all_frames, 0, 1, top)
        ag[:, R - 1 : R] = some_rows(rows_of, wide, w_ref, all_frames, R - 1, 1, bottom)

    def next_rows(rows_of, wide, w_ref, above, below):
        for n, (r0, tap) in enumerate(((-1, above), (R, below))):
            part = some_rows(rows_of, wide, w_ref, all_frames, r0, 1, (tap,))
            nbd[n] = part.reshape(T, W, C)

    own_rows(forward_rows, xpad, w_in, (1, 2), (0, 1))
    next_rows(forward_rows, xpad, w_in, 2, 0)

    def own_forward_step(t, carried):
        rate = lam[pl.ds(t, 1)]
        state = rate.reshape(1, 1, C) * carried[0] + ag[t]
        above, below = rate * carried[1] + nbd[0, t], rate * carried[2] + nbd[1, t]
        st[t + 1, 1 : R - 1] = state[1 : R - 1]
        es[0, t] = state[0].astype(BF16)
        es[1, t] = state[R - 1].astype(BF16)
        nbd[0, t] = above
        nbd[1, t] = below
        return state, above, below

    nothing = (jnp.zeros((R, W, C), F32), jnp.zeros((W, C), F32), jnp.zeros((W, C), F32))
    last, above, below = lax.fori_loop(0, T, own_forward_step, nothing)
    nbs[0, 0] = above.astype(BF16)
    nbs[0, 1] = below.astype(BF16)

    pl.semaphore_wait(barrier, nz + group - 2)

    def edge(stage, way, src, dst, sems=None):
        s, r = sems or (hal_s, hal_r)
        return to_rows(
            src, dst, s.at[stage, way], r.at[stage, way],
            jnp.maximum(mez - 1, 0) if way == 0 else jnp.minimum(mez + 1, nz - 1),
        )

    def edges(stage, srcs, dsts, what, sems=None):
        for way in range(2):
            from_there = (mez < nz - 1) if way == 0 else (mez > 0)
            to_there = (mez > 0) if way == 0 else (mez < nz - 1)

            @pl.when(from_there if what == "recv" else to_there)
            def _(way=way):
                copy = edge(stage, way, srcs[way], dsts[way], sems)
                {"start": copy.start, "recv": copy.wait_recv, "send": copy.wait_send}[what]()

    def received(act):
        @pl.when(mez < nz - 1)
        def _():
            act(0, R + 1)

        @pl.when(mez > 0)
        def _():
            act(1, 0)

    edge_sets = [
        (0, (x_hbm.at[:, 0], x_hbm.at[:, R - 1]), (xpad.at[:, R + 1], xpad.at[:, 0]), None),
        (1, (es.at[0], es.at[1]), (hs.at[0], hs.at[1]), None),
        (2, (eg.at[0], eg.at[1]), (hg.at[0], hg.at[1]), None),
        (3, (ea.at[0], ea.at[1]), (ha.at[0], ha.at[1]), None),
        (0, (ces.at[0, 0], ces.at[0, 1]), (cer.at[0, 0], cer.at[0, 1]), (ce_s, ce_r)),
        (1, (ces.at[1, 0], ces.at[1, 1]), (cer.at[1, 0], cer.at[1, 1]), (ce_s, ce_r)),
        (2, (nbs.at[0, 0], nbs.at[0, 1]), (nbr.at[0, 0], nbr.at[0, 1]), (ce_s, ce_r)),
        (3, (nbs.at[1, 0], nbs.at[1, 1]), (nbr.at[1, 0], nbr.at[1, 1]), (ce_s, ce_r)),
    ]

    def do_edges(n, what):
        stage, srcs, dsts, sems = edge_sets[n]
        edges(stage, srcs, dsts, what, sems)

    do_edges(6, "start")
    do_edges(0, "start")
    do_edges(1, "start")

    def with_neighbours(way, rows):
        return jnp.concatenate(
            [
                rows[:1] + nbr[way, 1].astype(F32)[None],
                rows[1 : R - 1],
                rows[R - 1 :] + nbr[way, 0].astype(F32)[None],
            ],
            axis=0,
        )

    def decay_copy(k):
        return to_tm(dsend, dall.at[me], dec_s.at[k], dec_r.at[me], k)

    others(me, nt, lambda k: decay_copy(k).start())

    def got(ref, q, k, r, copy):
        return copy(ref.at[q, k], ref.at[q, k], r.at[q, k], r.at[q, k], 0).wait_recv()

    def to_member(src, dst, n, q, k):
        return pltpu.make_async_remote_copy(
            src, dst, sum_s.at[n, q], sum_r.at[n, q], device_id=member(k), device_id_type=MESH
        )

    def send1(q, k):
        return to_member(snd1[q].at[k], rcv1[q].at[mine], 0, q, k)

    def send2(q, k):
        here = box[q].at[mez]
        return to_rows(here, here, sum_s.at[1, q], sum_r.at[1, q], k)

    def send3(q, k):
        here = g5[q].at[mine]
        return to_member(here, here, 2, q, k)

    def send_decay(k):
        here = decays.at[mex]
        return to_dp(here, here, sum_s.at[3, 0], sum_r.at[3, 0], k)

    def send_decay_band(k):
        here = dbox.at[mez]
        return to_rows(here, here, sum_s.at[3, 1], sum_r.at[3, 1], k)

    def passed(n, q, ref, count, way):
        if count:
            whole = ref.at[pl.ds(0, count)]
            copy = to_member(whole, whole, n, q, 0)
            {"recv": copy.wait_recv, "send": copy.wait_send}[way]()

    def owning(q, own, other):
        pl.when(mine < owners[q])(own)
        if owners[q] < group:
            pl.when(mine >= owners[q])(other)

    def sum1(q, extra=None):
        for k in range(owners[q]):
            r0 = k * share
            rows = min(share, LANES - r0)
            if rows > 0:
                snd1[q][k, 0:rows] = acc[q, r0 : r0 + rows].astype(BF16)
            if rows < share:
                snd1[q][k, max(rows, 0) :] = jnp.zeros((share - max(rows, 0), LANES), BF16)
        if extra is not None:
            k, r = divmod(LANES, share)
            snd1[q][k, r : r + UNIT, 0:C] = extra.astype(BF16)
        def to_owner(k):
            @pl.when(k < owners[q])
            def _():
                send1(q, k).start()

        others(mine, group, to_owner)

    def sum2(q):
        def own():
            rcv1[q][mine] = snd1[q][mine]
            passed(0, q, rcv1[q], group - 1, "recv")

            def step(k, total):
                return total + rcv1[q][k].astype(F32)

            total = lax.fori_loop(1, group, step, rcv1[q][0].astype(F32))
            for j in range(TAPS):
                part = total[:, j * C : (j + 1) * C].astype(BF16)
                box[q][mez, j * share : (j + 1) * share] = part

            others(mez, nz, lambda k: send2(q, k).start())

        owning(q, own, lambda: None)

    def sum3(q):
        def own():
            passed(1, q, box[q], nz - 1, "recv")
            total = box[q][0].astype(F32)
            for k in range(1, nz):
                total = total + box[q][k].astype(F32)
            for j in range(TAPS):
                part = total[j * share : (j + 1) * share].astype(BF16)
                g5[q][mine, :, j * C : (j + 1) * C] = part
            others(mine, group, lambda k: send3(q, k).start())

        owning(q, own, lambda: None)

    def decay1():
        decays[mex] = dpart[...]
        others(mex, nx, lambda k: send_decay(k).start())

    def decay2():
        passed(3, 0, decays, nx - 1, "recv")
        total = decays[0]
        for k in range(1, nx):
            total = total + decays[k]
        dbox[mez] = total.astype(BF16)
        others(mez, nz, lambda k: send_decay_band(k).start())

    def decay3():
        passed(3, 1, dbox, nz - 1, "recv")
        total = dbox[0].astype(F32)
        for k in range(1, nz):
            total = total + dbox[k].astype(F32)
        dg_out[...] = total * (1.0 / math.sqrt(total_cells))

    def sum4(q):
        owning(
            q,
            lambda: passed(2, q, g5[q], owners[q] - 1, "recv"),
            lambda: passed(2, q, g5[q], owners[q], "recv"),
        )

    def sums_sent():
        for q in range(2):
            owning(
                q,
                lambda q=q: passed(0, q, snd1[q], owners[q] - 1, "send"),
                lambda q=q: passed(0, q, snd1[q], owners[q], "send"),
            )
            owning(q, lambda q=q: passed(2, q, rcv1[q], group - 1, "send"), lambda: None)
            owning(q, lambda q=q: passed(1, q, box[q], nz - 1, "send"), lambda: None)
        passed(3, 1, dbox, nz - 1, "send")
        passed(3, 0, decays, nx - 1, "send")

    def carry_copy(way, k):
        return to_tm(csend.at[way], crecv.at[way, me], car_s.at[way, k], car_r.at[way, me], k)

    do_edges(6, "recv")
    csend[0] = with_neighbours(0, last).astype(BF16)
    each(me + 1, nt, lambda k: carry_copy(0, k).start())

    do_edges(0, "recv")

    def add_drive(way, row):
        r, tap = (R - 1, 2) if way == 0 else (0, 0)
        more = forward_rows(xpad, w_in, all_frames, r, 1, (tap,))
        ag[:, r : r + 1] += more.reshape(T, 1, W, C)

    received(add_drive)

    def forward_step(t, carried):
        rate = lam[pl.ds(t, 1)]
        top, bottom = rate * carried[0] + ag[t, 0], rate * carried[1] + ag[t, R - 1]
        st[t + 1, 0] = top
        st[t + 1, R - 1] = bottom
        return top, bottom

    lax.fori_loop(0, T, forward_step, nothing[1:])

    others(me, nt, lambda k: to_tm(dsend, dall.at[k], dec_s.at[k], dec_r.at[k], 0).wait_recv())

    def join_earlier(k, state):
        got(crecv, 0, k, car_r, to_tm)
        return dall[k, 0:1].reshape(1, 1, C) * state + crecv[0, k].astype(F32)

    carry = lax.fori_loop(0, me, join_earlier, jnp.zeros((R, W, C), F32))
    ces[0, 0] = carry[0].astype(BF16)
    ces[0, 1] = carry[R - 1].astype(BF16)
    do_edges(4, "start")
    st[0] = carry
    cin[...] = carry

    def finish_state(t):
        state = st[t + 1] + ecum[pl.ds(t, 1)].reshape(1, 1, C) * cin[...]
        st[t + 1] = state
        spad[t, 1 : R + 1] = state.astype(BF16)

    each(0, T, finish_state)

    for load in loads[3:]:
        load.wait()

    def output(frames, r0, nr):
        n = frames.size * nr
        x = xpad[frames, r0 + 1 : r0 + 1 + nr].reshape(n, W, C).astype(F32)
        pre = forward_rows(spad, w_out, frames, r0, nr) + gain[...].reshape(1, 1, C) * x
        square = pre * pre
        bend = jnp.tanh(GELU_A * (pre + GELU_B * (square * pre)))
        rise = 0.5 * (1.0 + bend)
        lo[frames, r0 : r0 + nr] = (pre * rise).astype(BF16).reshape(frames.size, nr, W, C)
        slope = rise + 0.5 * pre * (1.0 - bend * bend) * (GELU_A * (1.0 + 3.0 * GELU_B * square))
        grad = ct[frames, r0 : r0 + nr].reshape(n, W, C).astype(F32) * slope
        gp[frames, r0 : r0 + nr] = grad.reshape(frames.size, nr, W, C)
        gsum[...] += jnp.sum((grad * x).reshape(n * W // 8, 8, C), axis=0)
        widen(g3, frames, r0 + 1, nr, grad)

    inner(output)
    do_edges(1, "recv")
    do_edges(4, "recv")

    def state_edge(way, row):
        def step(t):
            value = hs[way, t].astype(F32) + nbd[1 - way, t]
            value = value + ecum[pl.ds(t, 1)] * cer[0, way].astype(F32)
            spad[t, row] = value.astype(BF16)

        each(0, T, step)

    received(state_edge)
    outer(output)
    eg[0] = gp[:, 0].astype(BF16)
    eg[1] = gp[:, R - 1].astype(BF16)
    def kernel_grad(q, pad, wide):
        acc[q] = jnp.zeros((LANES, LANES), F32)
        part = T // 4

        def step(f):
            frames = pl.ds(f * part, part)
            n = part * R * W
            lhs = jnp.concatenate(
                [pad[frames, i : i + R].reshape(n, C) for i in range(TAPS)], axis=-1
            )
            rhs = wide[frames, 1 : R + 1].reshape(n, LANES)
            acc[q] += lax.dot_general(
                lhs, rhs, (((0,), (0,)), ((), ())), preferred_element_type=F32
            )

        each(0, 4, step)

    next_rows(adjoint_rows, g3, w_out, 0, 2)

    def next_backward_step(o, carried):
        t = T - 1 - o
        rate = lam[pl.ds(t, 1)]
        above, below = nbd[0, t] + carried[0], nbd[1, t] + carried[1]
        nbd[0, t] = above
        nbd[1, t] = below
        return rate * above, rate * below

    above, below = lax.fori_loop(0, T, next_backward_step, nothing[1:])
    nbs[1, 0] = above.astype(BF16)
    nbs[1, 1] = below.astype(BF16)
    do_edges(7, "start")
    do_edges(2, "start")

    own_rows(adjoint_rows, g3, w_out, (0, 1), (1, 2))

    def own_backward_step(o, carried):
        t = T - 1 - o
        adjoint = ag[t] + carried
        ag[t, 1 : R - 1] = adjoint[1 : R - 1]
        ea[0, t] = adjoint[0].astype(BF16)
        ea[1, t] = adjoint[R - 1].astype(BF16)
        return lam[pl.ds(t, 1)].reshape(1, 1, C) * adjoint

    first = lax.fori_loop(0, T, own_backward_step, nothing[0])
    do_edges(7, "recv")
    csend[1] = with_neighbours(1, first).astype(BF16)
    each(0, me, lambda k: carry_copy(1, k).start())
    do_edges(3, "start")
    kernel_grad(0, spad, g3)

    do_edges(2, "recv")

    def add_state_grad(way, row):
        widen(g3, all_frames, row, 1, hg[way].astype(F32))
        r, tap = (R - 1, 0) if way == 0 else (0, 2)
        more = adjoint_rows(g3, w_out, all_frames, r, 1, (tap,))
        ag[:, r : r + 1] += more.reshape(T, 1, W, C)

    received(add_state_grad)

    def backward_step(o, carried):
        t = T - 1 - o
        rate = lam[pl.ds(t, 1)]
        top, bottom = ag[t, 0] + carried[0], ag[t, R - 1] + carried[1]
        ag[t, 0] = top
        ag[t, R - 1] = bottom
        return rate * top, rate * bottom

    lax.fori_loop(0, T, backward_step, nothing[1:])
    sum1(0, jnp.concatenate([gsum[...], jnp.zeros((8, C), F32)], axis=0))

    def join_later(o, adjoint):
        k = nt - 1 - o
        got(crecv, 1, k, car_r, to_tm)
        return dall[k, 0:1].reshape(1, 1, C) * adjoint + crecv[1, k].astype(F32)

    back = lax.fori_loop(0, nt - 1 - me, join_later, jnp.zeros((R, W, C), F32))
    ces[1, 0] = back[0].astype(BF16)
    ces[1, 1] = back[R - 1].astype(BF16)
    do_edges(5, "start")
    bin_[...] = back

    def finish_adjoint(t):
        adjoint = ag[t] + erev[pl.ds(t, 1)].reshape(1, 1, C) * bin_[...]
        product = jnp.sum((adjoint * st[t]).reshape(R * W, C), axis=0, keepdims=True)
        dpart[pl.ds(t, 1)] = product * lam[pl.ds(t, 1)]
        for j, part in enumerate((at_next(adjoint), adjoint, at_previous(adjoint))):
            a3[t, 1 : R + 1, :, j * C : (j + 1) * C] = part.astype(BF16)

    each(0, T, finish_adjoint)
    kernel_grad(1, xpad, a3)
    sum1(1)
    decay1()
    sum2(0)

    def video_grad(frames, r0, nr):
        skip = gain[...].reshape(1, 1, C) * gp[frames, r0 : r0 + nr].reshape(-1, W, C)
        value = adjoint_rows(a3, w_in, frames, r0, nr) + skip
        vg[frames, r0 : r0 + nr] = value.astype(BF16).reshape(frames.size, nr, W, C)

    inner(video_grad)
    do_edges(3, "recv")
    do_edges(5, "recv")

    def adjoint_edge(way, row):
        def step(t):
            value = ha[way, t].astype(F32) + nbd[1 - way, t]
            value = value + erev[pl.ds(t, 1)] * cer[1, way].astype(F32)
            widen(a3, pl.ds(t, 1), row, 1, value.reshape(1, W, C))

        each(0, T, step)

    received(adjoint_edge)
    outer(video_grad)
    sum2(1)
    decay2()
    sum3(0)
    sum3(1)
    sum4(0)
    k, r = divmod(LANES, share)
    total_gain = jnp.sum(g5[0][k, r : r + UNIT, 0:C].astype(F32), axis=0, keepdims=True)
    gg_out[...] = total_gain * (1.0 / math.sqrt(total_positions))
    decay3()
    sum4(1)

    for n in range(8):
        do_edges(n, "send")
    others(me, nt, lambda k: decay_copy(k).wait_send())
    each(me + 1, nt, lambda k: carry_copy(0, k).wait_send())
    each(0, me, lambda k: carry_copy(1, k).wait_send())
    sums_sent()


def finish(
    scale, lo, vg, g5_0, g5_1, gg, dg, lo_hbm, vg_hbm, ig_hbm, og_hbm, gg_hbm, dg_hbm, grads, sems
):
    def store(n, src, dst):
        copy = pltpu.make_async_copy(src, dst, sems.at[n])
        copy.start()
        return copy

    copies = [store(0, vg, vg_hbm), store(1, lo, lo_hbm)]
    copies += [store(2, gg, gg_hbm), store(3, dg, dg_hbm)]
    share = g5_0.shape[1]
    for q, g5, out in ((0, g5_0, og_hbm), (1, g5_1, ig_hbm)):
        for row in range(0, LANES, UNIT):
            k, r = divmod(row, share)
            i, c = divmod(row, C)
            for j in range(TAPS):
                piece = g5[k, r : r + UNIT, j * C : (j + 1) * C]
                grads[q, i, j, c : c + UNIT] = piece.astype(F32) * scale
        copies.append(store(4 + q, grads.at[q], out))
    for copy in copies:
        copy.wait()


def on_device(nt, nz, nx, video, cotangent, in_kernel, out_kernel, skip_gain, log_decay):
    seqs, T, R, W, _ = video.shape
    field = (T, R, W, C)
    share = share_of(nt, nx)
    owners = [owners_of(q, share) for q in range(2)]
    dma = pltpu.SemaphoreType.DMA
    vmem = pltpu.VMEM
    scratch = [
        vmem((T, R + 2, W, C), BF16),
        vmem((T, R + 2, W, C), BF16),
        vmem((T, R + 2, W, LANES), BF16),
        vmem((T, R + 2, W, LANES), BF16),
        vmem((T + 1, R, W, C), F32),
        vmem(field, F32),
        vmem(field, F32),
        vmem(field, BF16),
        vmem((TAPS, TAPS, C, C), BF16),
        vmem((TAPS, TAPS, C, C), BF16),
        vmem((1, C), F32),
        vmem((T, C), F32),
        *[vmem((2, T, W, C), BF16)] * 6,
        *[vmem((2, 2, W, C), BF16)] * 4,
        vmem((2, T, W, C), F32),
        *[vmem((T, C), F32)] * 3,
        vmem((8, C), F32),
        vmem((nt, 8, C), F32),
        vmem((2, R, W, C), BF16),
        vmem((2, nt, R, W, C), BF16),
        vmem((R, W, C), F32),
        vmem((R, W, C), F32),
        vmem((8, C), F32),
        vmem((T, C), F32),
        vmem((2, LANES, LANES), F32),
        dma((6,)),
        dma((4, 2)),
        dma((4, 2)),
        dma((4, 2)),
        dma((4, 2)),
        dma((nt,)),
        dma((nt,)),
        *[dma((2, nt))] * 2,
    ]
    scratch += [vmem((nt * nx, share, LANES), BF16)] * 2
    scratch += [vmem((n, share, LANES), BF16) for n in owners]
    scratch += [vmem((nz, TAPS * share, C), BF16)] * 2
    scratch += [vmem((nx, T, C), F32), vmem((nz, T, C), BF16), dma((4, 2)), dma((4, 2))]
    hbm, whole = pl.BlockSpec(memory_space=pltpu.HBM), pl.BlockSpec(memory_space=pltpu.VMEM)
    cells = seqs * nx * R * nz * W
    pieces = pl.pallas_call(
        functools.partial(body, nt, nz, nx, cells, cells * T * nt),
        out_shape=(
            vmem(field, BF16),
            vmem(field, BF16),
            *[vmem((n, share, LANES), BF16) for n in owners],
            vmem((1, C), F32),
            vmem((T, C), F32),
        ),
        in_specs=[hbm] * 6,
        out_specs=(whole,) * 6,
        scratch_shapes=scratch,
        compiler_params=pltpu.CompilerParams(
            collective_id=0, has_side_effects=True, vmem_limit_bytes=48 * 2**20
        ),
    )(
        *[
            pltpu.with_memory_space_constraint(operand, pltpu.HBM)
            for operand in (
                video.reshape(field),
                cotangent.reshape(field),
                in_kernel,
                out_kernel,
                skip_gain.reshape(1, C),
                log_decay,
            )
        ]
    )
    outs = pl.pallas_call(
        functools.partial(finish, 1.0 / math.sqrt(cells * T * nt)),
        out_shape=(
            jax.ShapeDtypeStruct(field, BF16),
            jax.ShapeDtypeStruct(field, BF16),
            jax.ShapeDtypeStruct((TAPS, TAPS, C, C), F32),
            jax.ShapeDtypeStruct((TAPS, TAPS, C, C), F32),
            jax.ShapeDtypeStruct((1, C), F32),
            jax.ShapeDtypeStruct((T, C), F32),
        ),
        in_specs=[whole] * 6,
        out_specs=(hbm,) * 6,
        scratch_shapes=[vmem((2, TAPS, TAPS, C, C), F32), dma((6,))],
        compiler_params=pltpu.CompilerParams(vmem_limit_bytes=16 * 2**20),
    )(*pieces)
    layer_out, video_grad, in_grad, out_grad, gain_grad, decay_grad = outs
    return (
        layer_out.reshape(video.shape),
        video_grad.reshape(video.shape),
        in_grad,
        out_grad,
        gain_grad.reshape(C),
        decay_grad,
    )


def solution(mesh):
    field = P("dp", "tm", "rows", None, None)
    nt, nz, nx = mesh.shape["tm"], mesh.shape["rows"], mesh.shape["dp"]
    return jax.shard_map(
        functools.partial(on_device, nt, nz, nx),
        mesh=mesh,
        in_specs=(field, field, P(), P(), P(), P("tm", None)),
        out_specs=(field, field, P(), P(), P(), P("tm", None)),
        check_vma=False,
    )
```

```python
import functools
import math

import jax
import jax.numpy as jnp
from jax import lax
from jax.experimental import pallas as pl
from jax.experimental.pallas import tpu as pltpu
from jax.sharding import PartitionSpec as P

MESH = pl.DeviceIdType.MESH
F32, BF16 = jnp.float32, jnp.bfloat16
C = 128
TAPS = 3
LANES = TAPS * C
GELU_A = math.sqrt(2.0 / math.pi)
GELU_B = 0.044715


UNIT = 16
UNITS = LANES // UNIT


def share_of(nt, nx):
    return -(-(UNITS + 1) // (nt * nx)) * UNIT


def owners_of(grad, share):
    return -(-(UNITS + 1 - grad) * UNIT // share)


def at_next(field):
    cols = field.shape[1]
    col = lax.broadcasted_iota(jnp.int32, field.shape, 1)
    return jnp.where(col == cols - 1, 0.0, pltpu.roll(field, cols - 1, 1))


def at_previous(field):
    col = lax.broadcasted_iota(jnp.int32, field.shape, 1)
    return jnp.where(col == 0, 0.0, pltpu.roll(field, 1, 1))


def taps(w_ref, i):
    return jnp.concatenate([w_ref[i, j] for j in range(TAPS)], axis=-1)


def forward_rows(pad, w_ref, frames, r0, nr, which=range(TAPS)):
    n, cols = frames.size * nr, pad.shape[2]
    lhs = jnp.concatenate(
        [pad[frames, r0 + i : r0 + i + nr].reshape(n * cols, C) for i in which], axis=-1
    )
    rhs = jnp.concatenate([taps(w_ref, i) for i in which], axis=0)
    y = jnp.dot(lhs, rhs, preferred_element_type=F32).reshape(n, cols, LANES)
    return at_previous(y[..., :C]) + y[..., C : 2 * C] + at_next(y[..., 2 * C :])


def adjoint_rows(wide, w_ref, frames, r0, nr, which=range(TAPS)):
    n, cols = frames.size * nr, wide.shape[2]
    lhs = jnp.concatenate(
        [wide[frames, r0 + 2 - i : r0 + 2 - i + nr].reshape(n * cols, LANES) for i in which],
        axis=-1,
    )
    rhs = jnp.concatenate([taps(w_ref, i) for i in which], axis=-1)
    y = lax.dot_general(lhs, rhs, (((1,), (1,)), ((), ())), preferred_element_type=F32)
    return y.reshape(n, cols, C)


def widen(wide, frames, r0, nr, value):
    shape = (frames.size, nr) + value.shape[1:]
    for j, part in enumerate((at_next(value), value, at_previous(value))):
        wide[frames, r0 : r0 + nr, :, j * C : (j + 1) * C] = part.astype(BF16).reshape(shape)


def body(
    nt, nz, nx, total_cells, total_positions,
    x_hbm, ct_hbm, w_in_hbm, w_out_hbm, gain_hbm, ld_hbm,
    lo, vg, g5_0, g5_1, gg_out, dg_out,
    xpad, spad, g3, a3, st, ag, gp, ct, w_in, w_out, gain, ld,
    es, eg, ea, hs, hg, ha, ces, cer, nbs, nbr, nbd,
    lam, ecum, erev, dsend, dall, csend, crecv, cin, bin_, gsum, dpart,
    acc, loc, hal_s, hal_r, ce_s, ce_r, dec_s, dec_r, car_s, car_r,
    rcv1_0, rcv1_1, snd1_0, snd1_1, box_0, box_1, decays, dbox, sum_s, sum_r,
):
    T, R, W, _ = x_hbm.shape
    snd1, rcv1, box, g5 = (snd1_0, snd1_1), (rcv1_0, rcv1_1), (box_0, box_1), (g5_0, g5_1)
    group, share = nt * nx, rcv1_0.shape[1]
    owners = [owners_of(q, share) for q in range(2)]
    half = T // 2
    all_frames = pl.ds(0, T)
    me, mez, mex = lax.axis_index("tm"), lax.axis_index("rows"), lax.axis_index("dp")

    def to_tm(src, dst, s, r, k):
        return pltpu.make_async_remote_copy(src, dst, s, r, device_id={"tm": k}, device_id_type=MESH)

    def to_rows(src, dst, s, r, k):
        return pltpu.make_async_remote_copy(src, dst, s, r, device_id={"rows": k}, device_id_type=MESH)

    def to_dp(src, dst, s, r, k):
        return pltpu.make_async_remote_copy(src, dst, s, r, device_id={"dp": k}, device_id_type=MESH)

    def others(mine, count, act):
        def step(o, _):
            act(lax.rem(mine + o, count))
            return 0

        lax.fori_loop(1, count, step, 0)

    def each(low, high, act):
        def step(k, _):
            act(k)
            return 0

        lax.fori_loop(low, high, step, 0)

    barrier = pltpu.get_barrier_semaphore()
    mine = me * nx + mex

    def member(k):
        return {"tm": k // nx, "dp": lax.rem(k, nx)}

    def greet(place):
        pl.semaphore_signal(barrier, inc=1, device_id=place, device_id_type=MESH)

    others(mez, nz, lambda k: greet({"rows": k}))
    others(mine, group, lambda k: greet(member(k)))
    loads = [
        pltpu.make_async_copy(src, dst, loc.at[n])
        for n, (src, dst) in enumerate(
            (
                (ld_hbm, ld),
                (x_hbm, xpad.at[:, 1 : R + 1]),
                (w_in_hbm, w_in),
                (ct_hbm, ct),
                (w_out_hbm, w_out),
                (gain_hbm, gain),
            )
        )
    ]
    for load in loads:
        load.start()
    loads[0].wait()

    run = jnp.zeros((1, C), F32)
    for t in range(T):
        run = run + ld[t : t + 1]
        ecum[t : t + 1] = run
    erev[...] = jnp.exp(run - ecum[...])
    ecum[...] = jnp.exp(ecum[...])
    lam[...] = jnp.exp(ld[...])
    dsend[...] = jnp.broadcast_to(jnp.exp(run), dsend.shape)
    gsum[...] = jnp.zeros_like(gsum)

    @pl.when(mez == 0)
    def _():
        for ref in (xpad, spad, g3, a3):
            ref[:, 0] = jnp.zeros((T, W, ref.shape[3]), BF16)
        nbr[:, 1] = jnp.zeros((2, W, C), BF16)

    @pl.when(mez == nz - 1)
    def _():
        for ref in (xpad, spad, g3, a3):
            ref[:, R + 1] = jnp.zeros((T, W, ref.shape[3]), BF16)
        nbr[:, 0] = jnp.zeros((2, W, C), BF16)

    def inner(act):
        each(0, 2, lambda f: act(pl.ds(f * half, half), 1, R - 2))

    def outer(act):
        each(0, 1, lambda f: act(all_frames, 0, 1))
        each(0, 1, lambda f: act(all_frames, R - 1, 1))

    loads[1].wait()
    loads[2].wait()

    def some_rows(rows_of, wide, w_ref, frames, r0, nr, which=range(TAPS)):
        return rows_of(wide, w_ref, frames, r0, nr, which).reshape(frames.size, nr, W, C)

    def own_rows(rows_of, wide, w_ref, top, bottom):
        def inner_rows(frames, r0, nr):
            ag[frames, r0 : r0 + nr] = some_rows(rows_of, wide, w_ref, frames, r0, nr)

        inner(inner_rows)
        ag[:, 0:1] = some_rows(rows_of, wide, w_ref, all_frames, 0, 1, top)
        ag[:, R - 1 : R] = some_rows(rows_of, wide, w_ref, all_frames, R - 1, 1, bottom)

    def next_rows(rows_of, wide, w_ref, above, below):
        for n, (r0, tap) in enumerate(((-1, above), (R, below))):
            part = some_rows(rows_of, wide, w_ref, all_frames, r0, 1, (tap,))
            nbd[n] = part.reshape(T, W, C)

    own_rows(forward_rows, xpad, w_in, (1, 2), (0, 1))
    next_rows(forward_rows, xpad, w_in, 2, 0)

    def own_forward_step(t, carried):
        rate = lam[pl.ds(t, 1)]
        state = rate.reshape(1, 1, C) * carried[0] + ag[t]
        above, below = rate * carried[1] + nbd[0, t], rate * carried[2] + nbd[1, t]
        st[t + 1, 1 : R - 1] = state[1 : R - 1]
        es[0, t] = state[0].astype(BF16)
        es[1, t] = state[R - 1].astype(BF16)
        nbd[0, t] = above
        nbd[1, t] = below
        return state, above, below

    nothing = (jnp.zeros((R, W, C), F32), jnp.zeros((W, C), F32), jnp.zeros((W, C), F32))
    last, above, below = lax.fori_loop(0, T, own_forward_step, nothing)
    nbs[0, 0] = above.astype(BF16)
    nbs[0, 1] = below.astype(BF16)

    pl.semaphore_wait(barrier, nz + group - 2)

    def edge(stage, way, src, dst, sems=None):
        s, r = sems or (hal_s, hal_r)
        return to_rows(
            src, dst, s.at[stage, way], r.at[stage, way],
            jnp.maximum(mez - 1, 0) if way == 0 else jnp.minimum(mez + 1, nz - 1),
        )

    def edges(stage, srcs, dsts, what, sems=None):
        for way in range(2):
            from_there = (mez < nz - 1) if way == 0 else (mez > 0)
            to_there = (mez > 0) if way == 0 else (mez < nz - 1)

            @pl.when(from_there if what == "recv" else to_there)
            def _(way=way):
                copy = edge(stage, way, srcs[way], dsts[way], sems)
                {"start": copy.start, "recv": copy.wait_recv, "send": copy.wait_send}[what]()

    def received(act):
        @pl.when(mez < nz - 1)
        def _():
            act(0, R + 1)

        @pl.when(mez > 0)
        def _():
            act(1, 0)

    edge_sets = [
        (0, (x_hbm.at[:, 0], x_hbm.at[:, R - 1]), (xpad.at[:, R + 1], xpad.at[:, 0]), None),
        (1, (es.at[0], es.at[1]), (hs.at[0], hs.at[1]), None),
        (2, (eg.at[0], eg.at[1]), (hg.at[0], hg.at[1]), None),
        (3, (ea.at[0], ea.at[1]), (ha.at[0], ha.at[1]), None),
        (0, (ces.at[0, 0], ces.at[0, 1]), (cer.at[0, 0], cer.at[0, 1]), (ce_s, ce_r)),
        (1, (ces.at[1, 0], ces.at[1, 1]), (cer.at[1, 0], cer.at[1, 1]), (ce_s, ce_r)),
        (2, (nbs.at[0, 0], nbs.at[0, 1]), (nbr.at[0, 0], nbr.at[0, 1]), (ce_s, ce_r)),
        (3, (nbs.at[1, 0], nbs.at[1, 1]), (nbr.at[1, 0], nbr.at[1, 1]), (ce_s, ce_r)),
    ]

    def do_edges(n, what):
        stage, srcs, dsts, sems = edge_sets[n]
        edges(stage, srcs, dsts, what, sems)

    do_edges(6, "start")
    do_edges(0, "start")
    do_edges(1, "start")

    def with_neighbours(way, rows):
        return jnp.concatenate(
            [
                rows[:1] + nbr[way, 1].astype(F32)[None],
                rows[1 : R - 1],
                rows[R - 1 :] + nbr[way, 0].astype(F32)[None],
            ],
            axis=0,
        )

    def decay_copy(k):
        return to_tm(dsend, dall.at[me], dec_s.at[k], dec_r.at[me], k)

    others(me, nt, lambda k: decay_copy(k).start())

    def got(ref, q, k, r, copy):
        return copy(ref.at[q, k], ref.at[q, k], r.at[q, k], r.at[q, k], 0).wait_recv()

    def to_member(src, dst, n, q, k):
        return pltpu.make_async_remote_copy(
            src, dst, sum_s.at[n, q], sum_r.at[n, q], device_id=member(k), device_id_type=MESH
        )

    def send1(q, k):
        return to_member(snd1[q].at[k], rcv1[q].at[mine], 0, q, k)

    def send2(q, k):
        here = box[q].at[mez]
        return to_rows(here, here, sum_s.at[1, q], sum_r.at[1, q], k)

    def send3(q, k):
        here = g5[q].at[mine]
        return to_member(here, here, 2, q, k)

    def send_decay(k):
        here = decays.at[mex]
        return to_dp(here, here, sum_s.at[3, 0], sum_r.at[3, 0], k)

    def send_decay_band(k):
        here = dbox.at[mez]
        return to_rows(here, here, sum_s.at[3, 1], sum_r.at[3, 1], k)

    def passed(n, q, ref, count, way):
        if count:
            whole = ref.at[pl.ds(0, count)]
            copy = to_member(whole, whole, n, q, 0)
            {"recv": copy.wait_recv, "send": copy.wait_send}[way]()

    def owning(q, own, other):
        pl.when(mine < owners[q])(own)
        if owners[q] < group:
            pl.when(mine >= owners[q])(other)

    def sum1(q, extra=None):
        for k in range(owners[q]):
            r0 = k * share
            rows = min(share, LANES - r0)
            if rows > 0:
                snd1[q][k, 0:rows] = acc[q, r0 : r0 + rows].astype(BF16)
            if rows < share:
                snd1[q][k, max(rows, 0) :] = jnp.zeros((share - max(rows, 0), LANES), BF16)
        if extra is not None:
            k, r = divmod(LANES, share)
            snd1[q][k, r : r + UNIT, 0:C] = extra.astype(BF16)
        def to_owner(k):
            @pl.when(k < owners[q])
            def _():
                send1(q, k).start()

        others(mine, group, to_owner)

    def sum2(q):
        def own():
            rcv1[q][mine] = snd1[q][mine]
            passed(0, q, rcv1[q], group - 1, "recv")

            def step(k, total):
                return total + rcv1[q][k].astype(F32)

            total = lax.fori_loop(1, group, step, rcv1[q][0].astype(F32))
            for j in range(TAPS):
                part = total[:, j * C : (j + 1) * C].astype(BF16)
                box[q][mez, j * share : (j + 1) * share] = part

            others(mez, nz, lambda k: send2(q, k).start())

        owning(q, own, lambda: None)

    def sum3(q):
        def own():
            passed(1, q, box[q], nz - 1, "recv")
            total = box[q][0].astype(F32)
            for k in range(1, nz):
                total = total + box[q][k].astype(F32)
            for j in range(TAPS):
                part = total[j * share : (j + 1) * share].astype(BF16)
                g5[q][mine, :, j * C : (j + 1) * C] = part
            others(mine, group, lambda k: send3(q, k).start())

        owning(q, own, lambda: None)

    def decay1():
        decays[mex] = dpart[...]
        others(mex, nx, lambda k: send_decay(k).start())

    def decay2():
        passed(3, 0, decays, nx - 1, "recv")
        total = decays[0]
        for k in range(1, nx):
            total = total + decays[k]
        dbox[mez] = total.astype(BF16)
        others(mez, nz, lambda k: send_decay_band(k).start())

    def decay3():
        passed(3, 1, dbox, nz - 1, "recv")
        total = dbox[0].astype(F32)
        for k in range(1, nz):
            total = total + dbox[k].astype(F32)
        dg_out[...] = total * (1.0 / math.sqrt(total_cells))

    def sum4(q):
        owning(
            q,
            lambda: passed(2, q, g5[q], owners[q] - 1, "recv"),
            lambda: passed(2, q, g5[q], owners[q], "recv"),
        )

    def sums_sent():
        for q in range(2):
            owning(
                q,
                lambda q=q: passed(0, q, snd1[q], owners[q] - 1, "send"),
                lambda q=q: passed(0, q, snd1[q], owners[q], "send"),
            )
            owning(q, lambda q=q: passed(2, q, rcv1[q], group - 1, "send"), lambda: None)
            owning(q, lambda q=q: passed(1, q, box[q], nz - 1, "send"), lambda: None)
        passed(3, 1, dbox, nz - 1, "send")
        passed(3, 0, decays, nx - 1, "send")

    def carry_copy(way, k):
        return to_tm(csend.at[way], crecv.at[way, me], car_s.at[way, k], car_r.at[way, me], k)

    do_edges(6, "recv")
    csend[0] = with_neighbours(0, last).astype(BF16)
    each(me + 1, nt, lambda k: carry_copy(0, k).start())

    do_edges(0, "recv")

    def add_drive(way, row):
        r, tap = (R - 1, 2) if way == 0 else (0, 0)
        more = forward_rows(xpad, w_in, all_frames, r, 1, (tap,))
        ag[:, r : r + 1] += more.reshape(T, 1, W, C)

    received(add_drive)

    def forward_step(t, carried):
        rate = lam[pl.ds(t, 1)]
        top, bottom = rate * carried[0] + ag[t, 0], rate * carried[1] + ag[t, R - 1]
        st[t + 1, 0] = top
        st[t + 1, R - 1] = bottom
        return top, bottom

    lax.fori_loop(0, T, forward_step, nothing[1:])

    others(me, nt, lambda k: to_tm(dsend, dall.at[k], dec_s.at[k], dec_r.at[k], 0).wait_recv())

    def join_earlier(k, state):
        got(crecv, 0, k, car_r, to_tm)
        return dall[k, 0:1].reshape(1, 1, C) * state + crecv[0, k].astype(F32)

    carry = lax.fori_loop(0, me, join_earlier, jnp.zeros((R, W, C), F32))
    ces[0, 0] = carry[0].astype(BF16)
    ces[0, 1] = carry[R - 1].astype(BF16)
    do_edges(4, "start")
    st[0] = carry
    cin[...] = carry

    def finish_state(t):
        state = st[t + 1] + ecum[pl.ds(t, 1)].reshape(1, 1, C) * cin[...]
        st[t + 1] = state
        spad[t, 1 : R + 1] = state.astype(BF16)

    each(0, T, finish_state)

    for load in loads[3:]:
        load.wait()

    def output(frames, r0, nr):
        n = frames.size * nr
        x = xpad[frames, r0 + 1 : r0 + 1 + nr].reshape(n, W, C).astype(F32)
        pre = forward_rows(spad, w_out, frames, r0, nr) + gain[...].reshape(1, 1, C) * x
        square = pre * pre
        bend = jnp.tanh(GELU_A * (pre + GELU_B * (square * pre)))
        rise = 0.5 * (1.0 + bend)
        lo[frames, r0 : r0 + nr] = (pre * rise).astype(BF16).reshape(frames.size, nr, W, C)
        slope = rise + 0.5 * pre * (1.0 - bend * bend) * (GELU_A * (1.0 + 3.0 * GELU_B * square))
        grad = ct[frames, r0 : r0 + nr].reshape(n, W, C).astype(F32) * slope
        gp[frames, r0 : r0 + nr] = grad.reshape(frames.size, nr, W, C)
        gsum[...] += jnp.sum((grad * x).reshape(n * W // 8, 8, C), axis=0)
        widen(g3, frames, r0 + 1, nr, grad)

    inner(output)
    do_edges(1, "recv")
    do_edges(4, "recv")

    def state_edge(way, row):
        def step(t):
            value = hs[way, t].astype(F32) + nbd[1 - way, t]
            value = value + ecum[pl.ds(t, 1)] * cer[0, way].astype(F32)
            spad[t, row] = value.astype(BF16)

        each(0, T, step)

    received(state_edge)
    outer(output)
    eg[0] = gp[:, 0].astype(BF16)
    eg[1] = gp[:, R - 1].astype(BF16)
    def kernel_grad(q, pad, wide):
        acc[q] = jnp.zeros((LANES, LANES), F32)
        part = T // 4

        def step(f):
            frames = pl.ds(f * part, part)
            n = part * R * W
            lhs = jnp.concatenate(
                [pad[frames, i : i + R].reshape(n, C) for i in range(TAPS)], axis=-1
            )
            rhs = wide[frames, 1 : R + 1].reshape(n, LANES)
            acc[q] += lax.dot_general(
                lhs, rhs, (((0,), (0,)), ((), ())), preferred_element_type=F32
            )

        each(0, 4, step)

    next_rows(adjoint_rows, g3, w_out, 0, 2)

    def next_backward_step(o, carried):
        t = T - 1 - o
        rate = lam[pl.ds(t, 1)]
        above, below = nbd[0, t] + carried[0], nbd[1, t] + carried[1]
        nbd[0, t] = above
        nbd[1, t] = below
        return rate * above, rate * below

    above, below = lax.fori_loop(0, T, next_backward_step, nothing[1:])
    nbs[1, 0] = above.astype(BF16)
    nbs[1, 1] = below.astype(BF16)
    do_edges(7, "start")
    do_edges(2, "start")

    own_rows(adjoint_rows, g3, w_out, (0, 1), (1, 2))

    def own_backward_step(o, carried):
        t = T - 1 - o
        adjoint = ag[t] + carried
        ag[t, 1 : R - 1] = adjoint[1 : R - 1]
        ea[0, t] = adjoint[0].astype(BF16)
        ea[1, t] = adjoint[R - 1].astype(BF16)
        return lam[pl.ds(t, 1)].reshape(1, 1, C) * adjoint

    first = lax.fori_loop(0, T, own_backward_step, nothing[0])
    do_edges(7, "recv")
    csend[1] = with_neighbours(1, first).astype(BF16)
    each(0, me, lambda k: carry_copy(1, k).start())
    do_edges(3, "start")
    kernel_grad(0, spad, g3)

    do_edges(2, "recv")

    def add_state_grad(way, row):
        widen(g3, all_frames, row, 1, hg[way].astype(F32))
        r, tap = (R - 1, 0) if way == 0 else (0, 2)
        more = adjoint_rows(g3, w_out, all_frames, r, 1, (tap,))
        ag[:, r : r + 1] += more.reshape(T, 1, W, C)

    received(add_state_grad)

    def backward_step(o, carried):
        t = T - 1 - o
        rate = lam[pl.ds(t, 1)]
        top, bottom = ag[t, 0] + carried[0], ag[t, R - 1] + carried[1]
        ag[t, 0] = top
        ag[t, R - 1] = bottom
        return rate * top, rate * bottom

    lax.fori_loop(0, T, backward_step, nothing[1:])
    sum1(0, jnp.concatenate([gsum[...], jnp.zeros((8, C), F32)], axis=0))

    def join_later(o, adjoint):
        k = nt - 1 - o
        got(crecv, 1, k, car_r, to_tm)
        return dall[k, 0:1].reshape(1, 1, C) * adjoint + crecv[1, k].astype(F32)

    back = lax.fori_loop(0, nt - 1 - me, join_later, jnp.zeros((R, W, C), F32))
    ces[1, 0] = back[0].astype(BF16)
    ces[1, 1] = back[R - 1].astype(BF16)
    do_edges(5, "start")
    bin_[...] = back

    def finish_adjoint(t):
        adjoint = ag[t] + erev[pl.ds(t, 1)].reshape(1, 1, C) * bin_[...]
        product = jnp.sum((adjoint * st[t]).reshape(R * W, C), axis=0, keepdims=True)
        dpart[pl.ds(t, 1)] = product * lam[pl.ds(t, 1)]
        for j, part in enumerate((at_next(adjoint), adjoint, at_previous(adjoint))):
            a3[t, 1 : R + 1, :, j * C : (j + 1) * C] = part.astype(BF16)

    each(0, T, finish_adjoint)
    decay1()
    kernel_grad(1, xpad, a3)
    sum1(1)
    sum2(0)

    def video_grad(frames, r0, nr):
        skip = gain[...].reshape(1, 1, C) * gp[frames, r0 : r0 + nr].reshape(-1, W, C)
        value = adjoint_rows(a3, w_in, frames, r0, nr) + skip
        vg[frames, r0 : r0 + nr] = value.astype(BF16).reshape(frames.size, nr, W, C)

    inner(video_grad)
    decay2()
    do_edges(3, "recv")
    do_edges(5, "recv")

    def adjoint_edge(way, row):
        def step(t):
            value = ha[way, t].astype(F32) + nbd[1 - way, t]
            value = value + erev[pl.ds(t, 1)] * cer[1, way].astype(F32)
            widen(a3, pl.ds(t, 1), row, 1, value.reshape(1, W, C))

        each(0, T, step)

    received(adjoint_edge)
    outer(video_grad)
    sum2(1)
    sum3(0)
    decay3()
    sum3(1)
    sum4(0)
    k, r = divmod(LANES, share)
    total_gain = jnp.sum(g5[0][k, r : r + UNIT, 0:C].astype(F32), axis=0, keepdims=True)
    gg_out[...] = total_gain * (1.0 / math.sqrt(total_positions))
    sum4(1)

    for n in range(8):
        do_edges(n, "send")
    others(me, nt, lambda k: decay_copy(k).wait_send())
    each(me + 1, nt, lambda k: carry_copy(0, k).wait_send())
    each(0, me, lambda k: carry_copy(1, k).wait_send())
    sums_sent()


def finish(
    scale, lo, vg, g5_0, g5_1, gg, dg, lo_hbm, vg_hbm, ig_hbm, og_hbm, gg_hbm, dg_hbm, grads, sems
):
    def store(n, src, dst):
        copy = pltpu.make_async_copy(src, dst, sems.at[n])
        copy.start()
        return copy

    copies = [store(0, vg, vg_hbm), store(1, lo, lo_hbm)]
    copies += [store(2, gg, gg_hbm), store(3, dg, dg_hbm)]
    share = g5_0.shape[1]
    for q, g5, out in ((0, g5_0, og_hbm), (1, g5_1, ig_hbm)):
        for row in range(0, LANES, UNIT):
            k, r = divmod(row, share)
            i, c = divmod(row, C)
            for j in range(TAPS):
                piece = g5[k, r : r + UNIT, j * C : (j + 1) * C]
                grads[q, i, j, c : c + UNIT] = piece.astype(F32) * scale
        copies.append(store(4 + q, grads.at[q], out))
    for copy in copies:
        copy.wait()


def on_device(nt, nz, nx, video, cotangent, in_kernel, out_kernel, skip_gain, log_decay):
    seqs, T, R, W, _ = video.shape
    field = (T, R, W, C)
    share = share_of(nt, nx)
    owners = [owners_of(q, share) for q in range(2)]
    dma = pltpu.SemaphoreType.DMA
    vmem = pltpu.VMEM
    scratch = [
        vmem((T, R + 2, W, C), BF16),
        vmem((T, R + 2, W, C), BF16),
        vmem((T, R + 2, W, LANES), BF16),
        vmem((T, R + 2, W, LANES), BF16),
        vmem((T + 1, R, W, C), F32),
        vmem(field, F32),
        vmem(field, F32),
        vmem(field, BF16),
        vmem((TAPS, TAPS, C, C), BF16),
        vmem((TAPS, TAPS, C, C), BF16),
        vmem((1, C), F32),
        vmem((T, C), F32),
        *[vmem((2, T, W, C), BF16)] * 6,
        *[vmem((2, 2, W, C), BF16)] * 4,
        vmem((2, T, W, C), F32),
        *[vmem((T, C), F32)] * 3,
        vmem((8, C), F32),
        vmem((nt, 8, C), F32),
        vmem((2, R, W, C), BF16),
        vmem((2, nt, R, W, C), BF16),
        vmem((R, W, C), F32),
        vmem((R, W, C), F32),
        vmem((8, C), F32),
        vmem((T, C), F32),
        vmem((2, LANES, LANES), F32),
        dma((6,)),
        dma((4, 2)),
        dma((4, 2)),
        dma((4, 2)),
        dma((4, 2)),
        dma((nt,)),
        dma((nt,)),
        *[dma((2, nt))] * 2,
    ]
    scratch += [vmem((nt * nx, share, LANES), BF16)] * 2
    scratch += [vmem((n, share, LANES), BF16) for n in owners]
    scratch += [vmem((nz, TAPS * share, C), BF16)] * 2
    scratch += [vmem((nx, T, C), F32), vmem((nz, T, C), BF16), dma((4, 2)), dma((4, 2))]
    hbm, whole = pl.BlockSpec(memory_space=pltpu.HBM), pl.BlockSpec(memory_space=pltpu.VMEM)
    cells = seqs * nx * R * nz * W
    pieces = pl.pallas_call(
        functools.partial(body, nt, nz, nx, cells, cells * T * nt),
        out_shape=(
            vmem(field, BF16),
            vmem(field, BF16),
            *[vmem((n, share, LANES), BF16) for n in owners],
            vmem((1, C), F32),
            vmem((T, C), F32),
        ),
        in_specs=[hbm] * 6,
        out_specs=(whole,) * 6,
        scratch_shapes=scratch,
        compiler_params=pltpu.CompilerParams(
            collective_id=0, has_side_effects=True, vmem_limit_bytes=48 * 2**20
        ),
    )(
        *[
            pltpu.with_memory_space_constraint(operand, pltpu.HBM)
            for operand in (
                video.reshape(field),
                cotangent.reshape(field),
                in_kernel,
                out_kernel,
                skip_gain.reshape(1, C),
                log_decay,
            )
        ]
    )
    outs = pl.pallas_call(
        functools.partial(finish, 1.0 / math.sqrt(cells * T * nt)),
        out_shape=(
            jax.ShapeDtypeStruct(field, BF16),
            jax.ShapeDtypeStruct(field, BF16),
            jax.ShapeDtypeStruct((TAPS, TAPS, C, C), F32),
            jax.ShapeDtypeStruct((TAPS, TAPS, C, C), F32),
            jax.ShapeDtypeStruct((1, C), F32),
            jax.ShapeDtypeStruct((T, C), F32),
        ),
        in_specs=[whole] * 6,
        out_specs=(hbm,) * 6,
        scratch_shapes=[vmem((2, TAPS, TAPS, C, C), F32), dma((6,))],
        compiler_params=pltpu.CompilerParams(vmem_limit_bytes=16 * 2**20),
    )(*pieces)
    layer_out, video_grad, in_grad, out_grad, gain_grad, decay_grad = outs
    return (
        layer_out.reshape(video.shape),
        video_grad.reshape(video.shape),
        in_grad,
        out_grad,
        gain_grad.reshape(C),
        decay_grad,
    )


def solution(mesh):
    field = P("dp", "tm", "rows", None, None)
    nt, nz, nx = mesh.shape["tm"], mesh.shape["rows"], mesh.shape["dp"]
    return jax.shard_map(
        functools.partial(on_device, nt, nz, nx),
        mesh=mesh,
        in_specs=(field, field, P(), P(), P(), P("tm", None)),
        out_specs=(field, field, P(), P(), P(), P("tm", None)),
        check_vma=False,
    )
```
